128 devices in a mesh: dp: 128 (over x, z, y, core).
Axes of the slice: x: 4, y: 4, z: 4, core: 2. Of those that a mesh axis runs over, the one named last changes fastest.
Arguments:
- hidden_in: bfloat16 [32768, 640], P('dp'), may hold values from -24 to 24
- query_weight: bfloat16 [640, 1024], P('dp'), may hold values from -0.25 to 0.25
- key_weight: bfloat16 [640, 256], P('dp'), may hold values from -0.25 to 0.25
- value_weight: bfloat16 [640, 256], P('dp'), may hold values from -0.25 to 0.25
- output_weight: bfloat16 [1024, 640], P('dp'), may hold values from -0.1875 to 0.1875
- gate_weight: bfloat16 [640, 2048], P('dp'), may hold values from -0.25 to 0.25
- up_weight: bfloat16 [640, 2048], P('dp'), may hold values from -0.25 to 0.25
- down_weight: bfloat16 [2048, 640], P('dp'), may hold values from -0.125 to 0.125
- input_gain: bfloat16 [640], P('dp'), may hold values from -0.5 to 0.5
- query_gain: bfloat16 [256], P('dp'), may hold values from -0.5 to 0.5
- key_gain: bfloat16 [256], P('dp'), may hold values from -0.5 to 0.5
- mixer_gain: bfloat16 [640], P('dp'), may hold values from -0.5 to 0.5
- middle_gain: bfloat16 [640], P('dp'), may hold values from -0.5 to 0.5
- output_gain: bfloat16 [640], P('dp'), may hold values from -0.5 to 0.5
- seq_lengths: int32 [64], replicated, may hold values from 1 to 1024, 32768 in all
- out_grad: bfloat16 [32768, 640], P('dp'), may hold values from -6 to 6
Outputs:
- mixed_out: bfloat16 [32768, 640], P('dp')
- input_grad: float32 [32768, 640], P('dp')
- query_weight_grad: float32 [640, 1024], P('dp')
- key_weight_grad: float32 [640, 256], P('dp')
- value_weight_grad: float32 [640, 256], P('dp')
- output_weight_grad: float32 [1024, 640], P('dp')
- gate_weight_grad: float32 [640, 2048], P('dp')
- up_weight_grad: float32 [640, 2048], P('dp')
- down_weight_grad: float32 [2048, 640], P('dp')
- input_gain_grad: float32 [640], P('dp')
- query_gain_grad: float32 [256], P('dp')
- key_gain_grad: float32 [256], P('dp')
- mixer_gain_grad: float32 [640], P('dp')
- middle_gain_grad: float32 [640], P('dp')
- output_gain_grad: float32 [640], P('dp')
The draws below stay inside these ranges and needn't reach their ends.
Inputs may be any that keep to these rules, and one draw needn't show every extreme that they name: `seq_lengths`: lengths of the packed sequences in order; they sum to 32768, and the longest is exactly 1024.
All inputs are finite; a program needn't handle non-finite values.
Results may differ from the reference program's by a relative error of at most 0.025.
Values may be sent and summed in bfloat16 or wider, within the bound.
A program may use at most 128 MiB of HBM per device.

```python
import math
import jax
import jax.numpy as jnp
import numpy as np
from jax import lax

D = 640
FF = 2048
HEADS = 4
HD = 256
WINDOW = 512
LMAX = 1024
TOKENS = 32768
NSEQ = 64


def spiked(drawn, key, source, target, shards_of, factor):
    def block_of(dim):
        return (jnp.arange(drawn.shape[dim]) // (drawn.shape[dim] // shards_of)).reshape((-1,) + (1,) * (drawn.ndim - 1 - dim))

    near = jax.random.permutation(key, shards_of)[block_of(target)]
    far = (block_of(target) + shards_of // 2) % shards_of
    return jnp.where((block_of(source) == near) | (block_of(source) == far), factor * drawn, drawn)


def steps_of(key, shape, pieces, low, high):
    loudness = 1.0
    for dim, shards_of in pieces:
        steps = jax.random.uniform(jax.random.fold_in(jax.random.fold_in(key, 6), dim), (shards_of,), jnp.float32, low / len(pieces), high / len(pieces))
        loudness = loudness * jnp.repeat(jnp.exp(steps), shape[dim] // shards_of).reshape((-1,) + (1,) * (len(shape) - 1 - dim))
    return loudness


def length_profile(number_of, total, bound, skew):
    loads = [(1 << 20) // math.isqrt(grade ** skew) + 1 for grade in range(2, number_of + 1)]
    rest, holding = total - bound - (number_of - 1), [1] * (number_of - 1)
    while rest > 0:
        candidates = [i for i in range(number_of - 1) if holding[i] < bound]
        mass, remaining = sum([loads[i] for i in candidates]), rest
        for i in candidates:
            addition = min(bound - holding[i], max(1, remaining * loads[i] // mass), rest)
            holding[i] = holding[i] + addition
            rest = rest - addition
    return np.array([bound] + holding)


def ragged(key, amount, total, most, slope):
    if amount == 2:
        one = jax.random.randint(key, (), max(1, total - most), min(most, total - 1) + 1)
        return jnp.stack([one, total - one])
    sizes = jnp.asarray(length_profile(amount, total, most, slope), jnp.int32)
    couples = (amount - 1) // 2
    giver, taker = sizes[1:1 + 2 * couples:2], sizes[2:2 + 2 * couples:2]
    slack = jnp.minimum(giver - 1, most - taker)
    moved = jax.random.randint(jax.random.fold_in(key, 1), (couples,), 0, 1 << 20) % (slack + 1)
    sizes = sizes.at[1:1 + 2 * couples:2].set(giver - moved).at[2:2 + 2 * couples:2].set(taker + moved)
    return sizes[jax.random.permutation(jax.random.fold_in(key, 2), amount)]


def centred(rng, extent, width, limit, split=(), kind=jnp.bfloat16):
    array = width * jax.random.normal(rng, extent, jnp.float32)
    if split:
        array = array * steps_of(rng, extent, split, -0.22, 0.18)
    return jnp.clip(array, -limit, limit).astype(kind)


def noise_with(own_key, shape, spread, reach, split, heavy, held_as=jnp.bfloat16):
    values = spread * jax.random.normal(own_key, shape, jnp.float32)
    if split:
        values = values * steps_of(own_key, shape, split, -0.22, 0.18)
    return jnp.clip(spiked(values, jax.random.fold_in(own_key, 3), *heavy), -reach, reach).astype(held_as)


def setup_inputs(seed: int = 0) -> dict:
    arg_keys = jax.random.split(jax.random.key(seed), 17)
    return {
        "hidden_in": noise_with(arg_keys[0], (TOKENS, D), 1.0, 24.0, ((0, 128),), (0, 1, 128, 5.5)),
        "query_weight": centred(arg_keys[1], (D, HEADS * HD), D ** -0.5, 0.25, ((0, 128),)),
        "key_weight": centred(arg_keys[2], (D, HD), D ** -0.5, 0.25, ((0, 128),)),
        "value_weight": centred(arg_keys[3], (D, HD), D ** -0.5, 0.25, ((0, 128),)),
        "output_weight": centred(arg_keys[4], (HEADS * HD, D), (HEADS * HD) ** -0.5, 0.1875, ((0, 128),)),
        "gate_weight": centred(arg_keys[5], (D, FF), D ** -0.5, 0.25, ((0, 128),)),
        "up_weight": centred(arg_keys[6], (D, FF), D ** -0.5, 0.25, ((0, 128),)),
        "down_weight": centred(arg_keys[7], (FF, D), FF ** -0.5, 0.125, ((0, 128),)),
        "input_gain": jnp.clip(jax.random.uniform(arg_keys[8], (D,), jnp.float32, -0.5, 0.5) * steps_of(arg_keys[8], (D,), ((0, 128),), -0.4, 0.0), -0.5, 0.5).astype(jnp.bfloat16),
        "query_gain": jnp.clip(jax.random.uniform(arg_keys[9], (HD,), jnp.float32, -0.5, 0.5) * steps_of(arg_keys[9], (HD,), ((0, 128),), -0.4, 0.0), -0.5, 0.5).astype(jnp.bfloat16),
        "key_gain": jnp.clip(jax.random.uniform(arg_keys[10], (HD,), jnp.float32, -0.5, 0.5) * steps_of(arg_keys[10], (HD,), ((0, 128),), -0.4, 0.0), -0.5, 0.5).astype(jnp.bfloat16),
        "mixer_gain": jnp.clip(jax.random.uniform(arg_keys[11], (D,), jnp.float32, -0.5, 0.5) * steps_of(arg_keys[11], (D,), ((0, 128),), -0.4, 0.0), -0.5, 0.5).astype(jnp.bfloat16),
        "middle_gain": jnp.clip(jax.random.uniform(arg_keys[12], (D,), jnp.float32, -0.5, 0.5) * steps_of(arg_keys[12], (D,), ((0, 128),), -0.4, 0.0), -0.5, 0.5).astype(jnp.bfloat16),
        "output_gain": jnp.clip(jax.random.uniform(arg_keys[13], (D,), jnp.float32, -0.5, 0.5) * steps_of(arg_keys[13], (D,), ((0, 128),), -0.4, 0.0), -0.5, 0.5).astype(jnp.bfloat16),
        "seq_lengths": ragged(arg_keys[14], NSEQ, TOKENS, LMAX, 2).astype(jnp.int32),
        "out_grad": centred(arg_keys[15], (TOKENS, D), 1.0, 6.0, ((0, 128),)),
    }


@jax.custom_vjp
def low(v):
    return lax.optimization_barrier(v.astype(jnp.bfloat16)).astype(jnp.float32)

@jax.custom_vjp
def low_back(v):
    return v

def low_keep(v):
    return (low(v), None)

def low_pass(kept, grad):
    return (grad,)

def back_keep(v):
    return (v, None)

def back_low(kept, grad):
    return (low(grad),)
low.defvjp(low_keep, low_pass)
low_back.defvjp(back_keep, back_low)
EPSILON = 1e-06
ROPE_BASE = 10000.0
NEG_FILL = -1e+30

def product(left_side, right_side):
    return jnp.dot(left_side, right_side, precision=lax.Precision.HIGHEST, preferred_element_type=jnp.float32)

def rms_norm(values, gain_vec):
    inv_rms = lax.rsqrt(lax.optimization_barrier(jnp.mean(values * values, axis=-1, keepdims=True)) + EPSILON)
    return values * inv_rms * (1.0 + gain_vec)

def rotary(position):
    frequency = ROPE_BASE ** (-2.0 * jnp.arange(HD // 2, dtype=jnp.float32) / HD)
    angles = position[:, None] * frequency[None, :]
    return (jnp.cos(angles), jnp.sin(angles))

def apply_rotary(values, cosine, sine_table):
    half_dim = values.shape[-1] // 2
    front_half = values[..., :half_dim]
    back_half = values[..., half_dim:]
    cos_wide = cosine[:, None, :]
    sin_wide = sine_table[:, None, :]
    return jnp.concatenate([front_half * cos_wide - back_half * sin_wide, back_half * cos_wide + front_half * sin_wide], axis=-1)

def seq_layout(indices, lengths):
    seq_ends = jnp.cumsum(lengths).astype(jnp.int32)
    passed = seq_ends[None, :] <= indices[:, None]
    segment = lax.optimization_barrier(jnp.sum(passed.astype(jnp.int32), axis=1)).astype(jnp.int32)
    seq_start = lax.optimization_barrier(jnp.max(jnp.where(passed, seq_ends[None, :], 0), axis=1)).astype(jnp.int32)
    return (segment, (indices - seq_start).astype(jnp.int32))

def attend(queries, key_rows, value_rows, segment):
    tokens = queries.shape[0]
    block_rows = math.gcd(tokens, 512)
    padding = jnp.zeros((WINDOW, HD), jnp.float32)
    key_padded = jnp.concatenate([padding, key_rows], axis=0)
    value_padded = jnp.concatenate([padding, value_rows], axis=0)
    segment_padded = jnp.concatenate([jnp.full((WINDOW,), -1, jnp.int32), segment])
    score_scale = 1.0 / math.sqrt(HD)

    def one_block(start_at):
        query_block = lax.dynamic_slice_in_dim(queries, start_at, block_rows, 0)
        key_block = lax.dynamic_slice_in_dim(key_padded, start_at, block_rows + WINDOW, 0)
        value_block = lax.dynamic_slice_in_dim(value_padded, start_at, block_rows + WINDOW, 0)
        query_seg = lax.dynamic_slice_in_dim(segment, start_at, block_rows, 0)
        key_seg = lax.dynamic_slice_in_dim(segment_padded, start_at, block_rows + WINDOW, 0)
        query_index = start_at + jnp.arange(block_rows, dtype=jnp.int32)
        key_index = start_at - WINDOW + jnp.arange(block_rows + WINDOW, dtype=jnp.int32)
        distance = query_index[:, None] - key_index[None, :]
        allowed = (query_seg[:, None] == key_seg[None, :]) & (distance >= 0) & (distance < WINDOW)
        scores = jnp.einsum('thd,kd->htk', query_block, key_block, precision=lax.Precision.HIGHEST) * score_scale
        scores = low_back(scores)
        scores = jnp.where(allowed[None], scores, NEG_FILL)
        row_max = lax.optimization_barrier(jnp.max(scores, axis=-1, keepdims=True))
        exp_scores = jnp.exp(scores - row_max)
        softmax_probs = exp_scores / lax.optimization_barrier(jnp.sum(exp_scores, axis=-1, keepdims=True))
        mixed_values = jnp.einsum('htk,kd->thd', low(softmax_probs), value_block, precision=lax.Precision.HIGHEST)
        return mixed_values.reshape(block_rows, HEADS * HD)
    block_starts = jnp.arange(tokens // block_rows, dtype=jnp.int32) * block_rows
    return lax.map(jax.checkpoint(one_block), block_starts).reshape(tokens, HEADS * HD)

def reference(hidden_in, query_weight, key_weight, value_weight, output_weight, gate_weight, up_weight, down_weight, input_gain, query_gain, key_gain, mixer_gain, middle_gain, output_gain, seq_lengths, out_grad):
    indices = jnp.arange(TOKENS, dtype=jnp.int32)
    segment, position = seq_layout(indices, seq_lengths)
    cosine, sine_table = rotary(position.astype(jnp.float32))

    def layer(hidden_in, query_weight, key_weight, value_weight, output_weight, gate_weight, up_weight, down_weight, input_gain, query_gain, key_gain, mixer_gain, middle_gain, output_gain):
        tokens = hidden_in.shape[0]
        normed = low(rms_norm(hidden_in, input_gain))
        query_raw = low_back(product(normed, query_weight)).reshape(tokens, HEADS, HD)
        key_raw = low_back(product(normed, key_weight))
        value_rows = low_back(low(product(normed, value_weight)))
        queries = low(apply_rotary(rms_norm(query_raw, query_gain), cosine, sine_table))
        key_rows = low(apply_rotary(rms_norm(key_raw, key_gain)[:, None, :], cosine, sine_table)[:, 0, :])
        attended = low_back(low(attend(queries, key_rows, value_rows, segment)))
        mixer_out = low_back(product(attended, output_weight))
        middle = hidden_in + rms_norm(mixer_out, mixer_gain)
        middle_normed = low(rms_norm(middle, middle_gain))
        gate_pre = low_back(product(middle_normed, gate_weight))
        up_proj = low_back(product(middle_normed, up_weight))
        hidden_units = low(jax.nn.gelu(gate_pre, approximate=True) * up_proj)
        ffn_out = low_back(product(hidden_units, down_weight))
        return middle + rms_norm(ffn_out, output_gain)
    result, pullback = jax.vjp(layer, hidden_in.astype(jnp.float32), query_weight.astype(jnp.float32), key_weight.astype(jnp.float32), value_weight.astype(jnp.float32), output_weight.astype(jnp.float32), gate_weight.astype(jnp.float32), up_weight.astype(jnp.float32), down_weight.astype(jnp.float32), input_gain.astype(jnp.float32), query_gain.astype(jnp.float32), key_gain.astype(jnp.float32), mixer_gain.astype(jnp.float32), middle_gain.astype(jnp.float32), output_gain.astype(jnp.float32))
    gradients = pullback(out_grad.astype(jnp.float32))
    return (result.astype(jnp.bfloat16), gradients[0], gradients[1], gradients[2], gradients[3], gradients[4], gradients[5], gradients[6], gradients[7], gradients[8], gradients[9], gradients[10], gradients[11], gradients[12], gradients[13])
```

```python
import math

import jax
import jax.numpy as jnp
from jax import lax
from jax.experimental import pallas as pl
from jax.experimental.pallas import tpu as pltpu
from jax.sharding import PartitionSpec as P

WINDOW = 512


EPSILON = 1e-06
ROPE_BASE = 10000.0
NEG_FILL = -1e30


def shifted(value, axis, steps):
    count = lax.axis_size(axis)
    first, last = (max(0, -steps), min(count, count - steps))
    return lax.ppermute(value, axis, [(source, source + steps) for source in range(first, last)])


def norm_parts(values):
    inv_rms = lax.rsqrt(jnp.mean(values * values, axis=-1, keepdims=True) + EPSILON)
    return (values * inv_rms, inv_rms)


def norm_back(upstream, unit_rows, inv_rms):
    return inv_rms * (upstream - unit_rows * jnp.mean(unit_rows * upstream, axis=-1, keepdims=True))


def rotary(position, head_dim):
    frequency = ROPE_BASE ** (-2.0 * jnp.arange(head_dim // 2, dtype=jnp.float32) / head_dim)
    angles = position[:, None] * frequency[None, :]
    return (jnp.cos(angles), jnp.sin(angles))


def apply_rotary(values, cosine, sine_table):
    half_dim = values.shape[-1] // 2
    front_half = values[..., :half_dim]
    back_half = values[..., half_dim:]
    cos_wide = cosine[:, None, :]
    sin_wide = sine_table[:, None, :]
    return jnp.concatenate(
        [
            front_half * cos_wide - back_half * sin_wide,
            back_half * cos_wide + front_half * sin_wide,
        ],
        axis=-1,
    )


def rotary_back(upstream, cosine, sine_table):
    half_dim = upstream.shape[-1] // 2
    front_half = upstream[..., :half_dim]
    back_half = upstream[..., half_dim:]
    cos_wide = cosine[:, None, :]
    sin_wide = sine_table[:, None, :]
    return jnp.concatenate(
        [
            front_half * cos_wide + back_half * sin_wide,
            back_half * cos_wide - front_half * sin_wide,
        ],
        axis=-1,
    )


def seq_layout(indices, lengths):
    seq_ends = jnp.cumsum(lengths)
    passed = seq_ends[None, :] <= indices[:, None]
    segment = jnp.sum(passed.astype(jnp.int32), axis=1)
    seq_start = jnp.max(jnp.where(passed, seq_ends[None, :], 0), axis=1)
    return (segment, indices - seq_start)


def gelu_tanh(values):
    return jax.nn.gelu(values, approximate=True)


def mat_mul(left_side, right_side):
    return jnp.dot(left_side, right_side, preferred_element_type=jnp.float32)


def mat_mul_t(left_side, right_side):
    return lax.dot_general(
        left_side, right_side, (((1,), (1,)), ((), ())), preferred_element_type=jnp.float32
    )


def mat_t_mul(left_side, right_side):
    return lax.dot_general(
        left_side, right_side, (((0,), (0,)), ((), ())), preferred_element_type=jnp.float32
    )


MESH = pl.DeviceIdType.MESH
BF = jnp.bfloat16
F32 = jnp.float32
WX, WZ, WD, WO = 1408, 1536, 640, 384
HID_A = 512
VMEM_CAP = 60 << 20


def place(x, z, y, c):
    return ((x % 4) * 4 + (z % 4)) * 8 + (y % 4) * 2 + c


class Links:
    def __init__(self, send_sems, recv_sems):
        me = lax.axis_index("dp")
        self.at = {"x": me // 32, "z": (me // 8) % 4, "y": (me // 2) % 4}
        self.core = me % 2
        self.send_sems, self.recv_sems, self.used, self.open = send_sems, recv_sems, 0, []

    def peer(self, axis, steps):
        moved = dict(self.at)
        moved[axis] = moved[axis] + steps
        return place(moved["x"], moved["z"], moved["y"], self.core)

    def sibling(self):
        return place(self.at["x"], self.at["z"], self.at["y"], 1 - self.core)

    def slot(self, axis, steps):
        return (self.at[axis] + steps) % 4

    def barrier(self):
        sem = pltpu.get_barrier_semaphore()
        partners = [self.sibling()]
        for axis in ("x", "z", "y"):
            partners += [self.peer(axis, o) for o in (1, 2, 3)]
        for p in partners:
            pl.semaphore_signal(sem, inc=1, device_id=(p,), device_id_type=MESH)
        pl.semaphore_wait(sem, len(partners))

    def send(self, src, dst, target):
        i = self.used
        self.used += 1
        copy = pltpu.make_async_remote_copy(
            src_ref=src,
            dst_ref=dst,
            send_sem=self.send_sems.at[i],
            recv_sem=self.recv_sems.at[i],
            device_id=(target,),
            device_id_type=MESH,
        )
        copy.start()
        self.open.append(copy.wait_send)
        return copy

    def local(self, src, dst):
        i = self.used
        self.used += 1
        copy = pltpu.make_async_copy(src, dst, self.send_sems.at[i])
        copy.start()
        return copy

    def finish(self):
        for wait in self.open:
            wait()


def gather_kernel(
    q_ref, k_ref, v_ref, o_ref, g_ref, u_ref, d_ref, n_ref,
    wx, wz, wd, wo,
    own_x, own_z, own_o, e_src_x, e_dst_x, e_src_z, e_dst_z, e_src_o, e_dst_o,
    s1x, s1z, s1o, s2x, s2z, tmp, b3x, b3z,
    send_sems, recv_sems,
):
    net = Links(send_sems, recv_sems)
    core = net.core
    other = 1 - core
    sib = net.sibling()
    own_x[...] = jnp.zeros_like(own_x)
    own_z[...] = jnp.zeros_like(own_z)
    own_o[...] = jnp.zeros_like(own_o)
    own_x[0, 0:5, 0:1024] = q_ref[...].astype(F32)
    own_x[0, 0:5, 1024:1280] = k_ref[...].astype(F32)
    own_x[0, 0:5, 1280:1408] = n_ref[...].astype(F32)
    own_x[1, 0:5, 0:256] = v_ref[...].astype(F32)
    own_x[1, 0:5, 256:768] = g_ref[:, 0:HID_A].astype(F32)
    own_x[1, 0:5, 768:1280] = u_ref[:, 0:HID_A].astype(F32)
    own_z[0, 0:5, :] = g_ref[:, HID_A:].astype(F32)
    own_z[1, 0:5, :] = u_ref[:, HID_A:].astype(F32)
    own_o[0, 0:8, :] = o_ref[:, 0:384].astype(F32)
    own_o[1, 0:8, 0:256] = o_ref[:, 384:640].astype(F32)
    e_src_x[...] = own_x[other].astype(BF)
    e_src_z[...] = own_z[other].astype(BF)
    e_src_o[...] = own_o[other].astype(BF)
    net.barrier()

    swaps = [
        net.send(e_src_x, e_dst_x, sib),
        net.send(e_src_z, e_dst_z, sib),
        net.send(e_src_o, e_dst_o, sib),
    ]
    xz = net.at["x"] * 4 + net.at["z"]
    d_rows = wd.at[xz, net.at["y"], core]
    d1 = [net.send(d_ref, d_rows, net.peer("z", o)) for o in (1, 2, 3)]
    locals_ = [net.local(d_ref, d_rows)]

    streams = []
    for own, e_dst, s1, s2, b3, w, width, axes, swap in (
        (own_x, e_dst_x, s1x, s2x, b3x, wx, WX, ("y", "z", "x"), swaps[0]),
        (own_z, e_dst_z, s1z, s2z, b3z, wz, WZ, ("x", "y", "z"), swaps[1]),
    ):
        swap.wait_recv()
        mine = own[core][0:5]
        theirs = e_dst[...].astype(F32)[0:5]
        first = core == 0
        tmp[0:5, 0:width] = jnp.where(first, mine, theirs)
        tmp[5:10, 0:width] = jnp.where(first, theirs, mine)
        slot = s1.at[net.at[axes[0]]]
        slot[...] = tmp[0:16, 0:width].astype(BF)
        p1 = [net.send(slot, slot, net.peer(axes[0], o)) for o in (1, 2, 3)]
        streams.append((s1, s2, b3, w, width, axes, p1))
    swaps[2].wait_recv()
    mine, theirs = own_o[core][0:8], e_dst_o[...].astype(F32)[0:8]
    tmp[0:8, 0:WO] = jnp.where(core == 0, mine, theirs)
    tmp[8:16, 0:WO] = jnp.where(core == 0, theirs, mine)
    s1o[...] = tmp[0:16, 0:WO].astype(BF)
    o_cols = pl.ds(pl.multiple_of(core * WO, 128), WO)
    o_rows = wo.at[xz, net.at["y"], :, o_cols]
    o1 = [net.send(s1o, o_rows, net.peer("z", o)) for o in (1, 2, 3)]
    locals_.append(net.local(s1o, o_rows))

    thirds = []
    for s1, s2, b3, w, width, axes, p1 in streams:
        for copy in p1:
            copy.wait_recv()
        for j in range(4):
            tmp[10 * j : 10 * j + 10, 0:width] = s1[j].astype(F32)[0:10]
        slot = s2.at[net.at[axes[1]]]
        slot[...] = tmp[0:48, 0:width].astype(BF)
        p2 = [net.send(slot, slot, net.peer(axes[1], o)) for o in (1, 2, 3)]
        thirds.append((s2, b3, w, width, axes, p2))
    for copy in d1 + o1:
        copy.wait_recv()
    for copy in locals_:
        copy.wait()
    x_rows = pl.ds(net.at["x"] * 4, 4)
    d_part = wd.at[x_rows, net.at["y"], core]
    o_part = wo.at[x_rows, net.at["y"], :, o_cols]
    d2 = [net.send(d_part, d_part, net.peer("x", o)) for o in (1, 2, 3)]
    o2 = [net.send(o_part, o_part, net.peer("x", o)) for o in (1, 2, 3)]

    def view_of(w, width):
        cols = pl.ds(pl.multiple_of(core * width, 128), width)
        return lambda slot, at, n: w.at[slot, pl.ds(at, n), :, cols]

    rings, ends = [], []
    for s2, b3, w, width, axes, p2 in thirds:
        for copy in p2:
            copy.wait_recv()
        for j in range(4):
            tmp[40 * j : 40 * j + 40, 0:width] = s2[j].astype(F32)[0:40]
        for j in range(10):
            b3[j] = tmp[16 * j : 16 * j + 16, 0:width].astype(BF)
        view = view_of(w, width)
        dst = view(net.at[axes[2]], 0, 10)
        ends.append(net.local(b3, dst).wait)
        up = net.send(b3, dst, net.peer(axes[2], 1))
        down = net.send(b3, dst, net.peer(axes[2], 3))
        ends.append(net.send(b3, dst, sib).wait_recv)
        rings.append((view, 10, axes[2], up, down))
    for copy in d2 + o2:
        copy.wait_recv()
    for view in (
        lambda slot, at, n: wd.at[pl.ds(at, n), slot, core],
        lambda slot, at, n: wo.at[pl.ds(at, n), slot, :, o_cols],
    ):
        part = view(net.at["y"], 0, 16)
        up = net.send(part, part, net.peer("y", 1))
        down = net.send(part, part, net.peer("y", 3))
        ends.append(net.send(part, part, sib).wait_recv)
        rings.append((view, 16, "y", up, down))
    fars = []
    for view, n, axis, up, down in rings:
        up.wait_recv()
        part = view(net.slot(axis, 3), 0, n // 2)
        fars.append((net.send(part, part, net.peer(axis, 1)), view, axis, 0, n // 2))
        whole = view(net.slot(axis, 3), 0, n)
        ends.append(net.send(whole, whole, sib).wait_recv)
        down.wait_recv()
        part = view(net.slot(axis, 1), n // 2, n // 2)
        fars.append((net.send(part, part, net.peer(axis, 3)), view, axis, n // 2, n // 2))
        whole = view(net.slot(axis, 1), 0, n)
        ends.append(net.send(whole, whole, sib).wait_recv)
    for copy, view, axis, at, n in fars:
        copy.wait_recv()
        part = view(net.slot(axis, 2), at, n)
        ends.append(net.send(part, part, sib).wait_recv)
    for wait in ends:
        wait()
    net.finish()


def gather_all(q, k, v, o, g, u, d, n):
    sems = 80
    anywhere = pl.BlockSpec(memory_space=pl.ANY)
    inside = pl.BlockSpec(memory_space=pltpu.VMEM)
    return pl.pallas_call(
        gather_kernel,
        out_shape=(
            jax.ShapeDtypeStruct((4, 10, 16, 2 * WX), BF),
            jax.ShapeDtypeStruct((4, 10, 16, 2 * WZ), BF),
            jax.ShapeDtypeStruct((16, 4, 2, 16, WD), BF),
            jax.ShapeDtypeStruct((16, 4, 16, 2 * WO), BF),
        ),
        in_specs=[inside] * 8,
        out_specs=(anywhere,) * 4,
        scratch_shapes=[
            pltpu.VMEM((2, 16, WX), F32),
            pltpu.VMEM((2, 16, WZ), F32),
            pltpu.VMEM((2, 16, WO), F32),
            pltpu.VMEM((16, WX), BF),
            pltpu.VMEM((16, WX), BF),
            pltpu.VMEM((16, WZ), BF),
            pltpu.VMEM((16, WZ), BF),
            pltpu.VMEM((16, WO), BF),
            pltpu.VMEM((16, WO), BF),
            pltpu.VMEM((4, 16, WX), BF),
            pltpu.VMEM((4, 16, WZ), BF),
            pltpu.VMEM((16, WO), BF),
            pltpu.VMEM((4, 48, WX), BF),
            pltpu.VMEM((4, 48, WZ), BF),
            pltpu.VMEM((160, WZ), F32),
            pltpu.VMEM((10, 16, WX), BF),
            pltpu.VMEM((10, 16, WZ), BF),
            pltpu.SemaphoreType.DMA((sems,)),
            pltpu.SemaphoreType.DMA((sems,)),
        ],
        compiler_params=pltpu.CompilerParams(
            collective_id=0, has_side_effects=True, vmem_limit_bytes=VMEM_CAP
        ),
        name="gather_weights",
    )(q, k, v, o, g, u, d, n)


def scatter_kernel(
    gx, gz, gd, go,
    rx, rz, rd, ro,
    ax, az, ad, ao, bx, bz, bd, bo,
    fx, fz, fd, fo, nx, nz, nd, no,
    t2x, t2z, t2d, t2o, r2x, r2z, r2d, r2o,
    t1x, t1z, t1d, t1o, r1x, r1z, r1d, r1o,
    sum_x, sum_z, sum_d, sum_o, swap_x, swap_z, swap_o, got_x, got_z, got_o,
    send_sems, recv_sems,
):
    net = Links(send_sems, recv_sems)
    core = net.core
    other = 1 - core
    sib = net.sibling()
    xz = net.at["x"] * 4 + net.at["z"]

    def cols(which, width):
        return pl.ds(pl.multiple_of(which * width, 128), width)

    views = {
        "x": lambda t, which: gx.at[t, :, :, cols(which, WX)],
        "z": lambda t, which: gz.at[t, :, :, cols(which, WZ)],
        "d": lambda t, which: gd.at[:, t, which],
        "o": lambda t, which: go.at[:, t, :, cols(which, WO)],
    }
    plan = (
        ("x", ax, bx, fx, nx, 10, "x"),
        ("z", az, bz, fz, nz, 10, "z"),
        ("d", ad, bd, fd, nd, 16, "y"),
        ("o", ao, bo, fo, no, 16, "y"),
    )
    order = (2, 1, 3, 0)
    mine = {}
    for steps in order:
        for name, a, b, f, n, blocks, axis in plan:
            t = net.slot(axis, steps)
            mine[name, steps] = net.local(views[name](t, core), a.at[steps])
    net.barrier()
    swaps = {}
    for steps in order:
        for name, a, b, f, n, blocks, axis in plan:
            t = net.slot(axis, steps)
            swaps[name, steps] = net.send(views[name](t, other), b.at[steps], sib)

    def add_rows(out, left, right, count):
        def body(i, carry):
            out[i] = (left[i].astype(F32) + right[i].astype(F32)).astype(BF)
            return carry

        lax.fori_loop(0, count, body, 0)

    onward, near = {}, {}
    for steps in order:
        for name, a, b, f, n, blocks, axis in plan:
            half = blocks // 2
            mine[name, steps].wait()
            swaps[name, steps].wait_recv()
            add_rows(a.at[steps], a.at[steps], b.at[steps], blocks)
            lo, hi = pl.ds(0, half), pl.ds(half, half)
            if steps == 2:
                onward[name, 1] = net.send(a.at[2, lo], f.at[0], net.peer(axis, 1))
                onward[name, 3] = net.send(a.at[2, hi], f.at[1], net.peer(axis, 3))
            elif steps == 1:
                near[name, "a"] = net.send(a.at[1, hi], n.at[0, hi], net.peer(axis, 1))
            elif steps == 3:
                near[name, "b"] = net.send(a.at[3, lo], n.at[1, lo], net.peer(axis, 3))
    for name, a, b, f, n, blocks, axis in plan:
        half = blocks // 2
        lo, hi = pl.ds(0, half), pl.ds(half, half)
        onward[name, 1].wait_recv()
        add_rows(a.at[1, lo], a.at[1, lo], f.at[0], half)
        near[name, "c"] = net.send(a.at[1, lo], n.at[0, lo], net.peer(axis, 1))
        onward[name, 3].wait_recv()
        add_rows(a.at[3, hi], a.at[3, hi], f.at[1], half)
        near[name, "d"] = net.send(a.at[3, hi], n.at[1, hi], net.peer(axis, 3))

    def arrived(name):
        for part in "abcd":
            near[name, part].wait_recv()

    def total3(a, n, i):
        return a[0, i].astype(F32) + n[0, i].astype(F32) + n[1, i].astype(F32)

    seconds = []
    for name, a, n, total, t2, r2, t1, r1, width, axes in (
        ("x", ax, nx, sum_x, t2x, r2x, t1x, r1x, WX, ("y", "z")),
        ("z", az, nz, sum_z, t2z, r2z, t1z, r1z, WZ, ("x", "y")),
    ):
        arrived(name)
        for i in range(10):
            total[16 * i : 16 * i + 16] = total3(a, n, i)
        for j in range(4):
            t2[j, 0:32] = total[40 * j : 40 * j + 32].astype(BF)
            t2[j, 32:48] = jnp.concatenate(
                [total[40 * j + 32 : 40 * j + 40], jnp.zeros((8, width), F32)], axis=0
            ).astype(BF)
        p2 = [
            net.send(t2.at[net.slot(axes[1], o)], r2.at[o - 1], net.peer(axes[1], o))
            for o in (1, 2, 3)
        ]
        seconds.append((total, t2, r2, t1, r1, width, axes, p2))
    flat2 = []
    for name, a, n, t2, r2 in (("d", ad, nd, t2d, r2d), ("o", ao, no, t2o, r2o)):
        arrived(name)

        def body(i, carry, a=a, n=n, t2=t2):
            t2[i] = total3(a, n, i).astype(BF)
            return carry

        lax.fori_loop(0, 16, body, 0)
        p2 = [
            net.send(
                t2.at[pl.ds(net.slot("x", o) * 4, 4)], r2.at[o - 1], net.peer("x", o)
            )
            for o in (1, 2, 3)
        ]
        flat2.append(p2)

    firsts = []
    for total, t2, r2, t1, r1, width, axes, p2 in seconds:
        for copy in p2:
            copy.wait_recv()
        own = t2[net.at[axes[1]]].astype(F32)
        for o in range(3):
            own = own + r2[o].astype(F32)
        total[0:48] = own
        for j in range(4):
            part = total[10 * j : 10 * j + 10]
            t1[j] = jnp.concatenate([part, jnp.zeros((6, width), F32)], axis=0).astype(BF)
        p1 = [
            net.send(t1.at[net.slot(axes[0], o)], r1.at[o - 1], net.peer(axes[0], o))
            for o in (1, 2, 3)
        ]
        firsts.append((total, t1, r1, width, axes, p1))
    flat1 = []
    for (t2, r2, t1, r1), p2 in zip(((t2d, r2d, t1d, r1d), (t2o, r2o, t1o, r1o)), flat2):
        for copy in p2:
            copy.wait_recv()
        for j in range(4):
            value = t2[net.at["x"] * 4 + j].astype(F32)
            for o in range(3):
                value = value + r2[o, j].astype(F32)
            t1[j] = value.astype(BF)
        flat1.append(
            [
                net.send(t1.at[net.slot("z", o)], r1.at[o - 1], net.peer("z", o))
                for o in (1, 2, 3)
            ]
        )

    last = []
    for (total, t1, r1, width, axes, p1), swap, got, out in zip(
        firsts, (swap_x, swap_z), (got_x, got_z), (rx, rz)
    ):
        for copy in p1:
            copy.wait_recv()
        own = t1[net.at[axes[0]]].astype(F32)
        for o in range(3):
            own = own + r1[o].astype(F32)
        total[0:16] = own
        low_rows = total[0:8]
        high_rows = total[5:13]
        first = core == 0
        swap[...] = jnp.where(first, high_rows, low_rows)
        out[core] = jnp.where(first, low_rows, high_rows)
        last.append((net.send(swap, got, sib), got, out))
    for copy in flat1[0]:
        copy.wait_recv()
    own = t1d[net.at["z"]].astype(F32)
    for o in range(3):
        own = own + r1d[o].astype(F32)
    rd[...] = own
    for copy in flat1[1]:
        copy.wait_recv()
    own = t1o[net.at["z"]].astype(F32)
    for o in range(3):
        own = own + r1o[o].astype(F32)
    first = core == 0
    swap_o[...] = jnp.where(first, own[8:16], own[0:8])
    ro[core] = jnp.where(first, own[0:8], own[8:16])
    last.append((net.send(swap_o, got_o, sib), got_o, ro))
    for copy, got, out in last:
        copy.wait_recv()
        out[other] = got[...]
    net.finish()


def scatter_all(gx, gz, gd, go):
    sems = 120
    anywhere = pl.BlockSpec(memory_space=pl.ANY)
    inside = pl.BlockSpec(memory_space=pltpu.VMEM)
    chunk = ((10, 16, WX), (10, 16, WZ), (16, 16, WD), (16, 16, WO))
    halves = ((5, 16, WX), (5, 16, WZ), (8, 16, WD), (8, 16, WO))

    def many(count, shapes, kind=BF):
        return [pltpu.VMEM((count, *s) if count else s, kind) for s in shapes]

    return pl.pallas_call(
        scatter_kernel,
        out_shape=(
            jax.ShapeDtypeStruct((2, 8, WX), F32),
            jax.ShapeDtypeStruct((2, 8, WZ), F32),
            jax.ShapeDtypeStruct((16, WD), F32),
            jax.ShapeDtypeStruct((2, 8, WO), F32),
        ),
        in_specs=[anywhere] * 4,
        out_specs=(inside,) * 4,
        scratch_shapes=[
            *many(4, chunk),
            *many(4, chunk),
            *many(2, halves),
            *many(2, chunk),
            *many(0, ((4, 48, WX), (4, 48, WZ), (16, 16, WD), (16, 16, WO))),
            *many(0, ((3, 48, WX), (3, 48, WZ), (3, 4, 16, WD), (3, 4, 16, WO))),
            *many(0, ((4, 16, WX), (4, 16, WZ), (4, 16, WD), (4, 16, WO))),
            *many(0, ((3, 16, WX), (3, 16, WZ), (3, 16, WD), (3, 16, WO))),
            *many(0, ((160, WX), (160, WZ), (16, WD), (16, WO)), F32),
            *many(0, ((8, WX), (8, WZ), (8, WO)) * 2, F32),
            pltpu.SemaphoreType.DMA((sems,)),
            pltpu.SemaphoreType.DMA((sems,)),
        ],
        compiler_params=pltpu.CompilerParams(
            collective_id=1, has_side_effects=True, vmem_limit_bytes=VMEM_CAP
        ),
        name="scatter_grads",
    )(gx, gz, gd, go)


def turned_order():
    spot = jnp.arange(640, dtype=jnp.int32)
    z, y, x, rest = spot // 160, (spot // 40) % 4, (spot // 10) % 4, spot % 10
    source = x * 160 + z * 40 + y * 10 + rest
    return (jnp.arange(640, dtype=jnp.int32)[:, None] == source[None, :]).astype(jnp.bfloat16)


def per_device(
    hidden_in,
    query_weight,
    key_weight,
    value_weight,
    output_weight,
    gate_weight,
    up_weight,
    down_weight,
    input_gain,
    query_gain,
    key_gain,
    mixer_gain,
    middle_gain,
    output_gain,
    seq_lengths,
    out_grad,
):
    tok_rows = hidden_in.shape[0]
    hop_count = (WINDOW + tok_rows - 2) // tok_rows
    head_dim = key_weight.shape[1]
    head_count = query_weight.shape[1] // head_dim
    score_scale = 1.0 / math.sqrt(head_dim)
    offset = lax.axis_index("dp") * tok_rows
    query_index = offset + jnp.arange(tok_rows, dtype=jnp.int32)
    key_index = (
        offset - hop_count * tok_rows + jnp.arange((hop_count + 1) * tok_rows, dtype=jnp.int32)
    )
    query_seg, position = seq_layout(query_index, seq_lengths)
    key_seg = seq_layout(key_index, seq_lengths)[0]
    distance = query_index[:, None] - key_index[None, :]
    allowed = (
        (query_seg[:, None] == key_seg[None, :])
        & (distance >= 0)
        & (distance < WINDOW)
        & (key_index[None, :] >= 0)
    )
    cosine, sine_table = rotary(position.astype(jnp.float32), head_dim)
    gains = jnp.stack(
        [input_gain, mixer_gain, middle_gain, output_gain]
        + [jnp.pad(a, (0, 3)) for a in (query_gain, key_gain)],
        axis=1,
    )
    gains = jnp.pad(gains, ((0, 0), (0, 122)))
    got_x, got_z, got_d, got_o = gather_all(
        query_weight, key_weight, value_weight, output_weight, gate_weight, up_weight, down_weight,
        gains,
    )
    got_x = got_x.reshape(640, 2 * WX)
    got_z = got_z.reshape(640, 2 * WZ)
    down_full = got_d.reshape(2048, 640)
    output_full = got_o.reshape(1024, 2 * WO)[:, :640]
    query_full = got_x[:, 0:1024]
    key_full = got_x[:, 1024:1280]
    value_full = got_x[:, WX : WX + 256]
    gain_columns = got_x[:, 1280:1408]
    input_full, mixer_full, middle_full, outgain_full = [gain_columns[:, i] for i in range(4)]
    head_gains = gain_columns.reshape(128, 5, 128)
    qgain_full = head_gains[:, :2, 4].reshape(256)
    kgain_full = head_gains[:, :2, 5].reshape(256)
    gate_a, up_a = got_x[:, WX + 256 : WX + 768], got_x[:, WX + 768 : WX + 1280]
    gate_b, up_b = got_z[:, :WZ], got_z[:, WZ:]
    turn = turned_order()
    input_mult = 1.0 + input_full.astype(jnp.float32)
    query_mult = 1.0 + qgain_full.astype(jnp.float32)
    key_mult = 1.0 + kgain_full.astype(jnp.float32)
    mixer_mult = 1.0 + mixer_full.astype(jnp.float32)
    hidden = hidden_in.astype(jnp.float32)
    input_unit, input_inv = norm_parts(hidden)
    normed = (input_unit * input_mult).astype(jnp.bfloat16)
    query_raw = mat_mul(normed, query_full).reshape(tok_rows, head_count, head_dim)
    key_raw = mat_mul(normed, key_full)
    value_rows = mat_mul(normed, value_full).astype(jnp.bfloat16)
    query_unit, query_inv = norm_parts(query_raw)
    queries = apply_rotary(query_unit * query_mult, cosine, sine_table).astype(jnp.bfloat16)
    key_unit, key_inv = norm_parts(key_raw)
    key_rows = apply_rotary((key_unit * key_mult)[:, None, :], cosine, sine_table)[:, 0, :].astype(
        jnp.bfloat16
    )
    key_parts = []
    value_parts = []
    for step_back in range(hop_count, 0, -1):
        far_keys, far_values = shifted((key_rows, value_rows), "dp", step_back)
        key_parts.append(far_keys)
        value_parts.append(far_values)
    key_all = jnp.concatenate(key_parts + [key_rows], axis=0)
    value_all = jnp.concatenate(value_parts + [value_rows], axis=0)

    def masked_scores(query_block):
        raw_scores = (
            jnp.einsum("thd,kd->htk", query_block, key_all, preferred_element_type=jnp.float32)
            * score_scale
        )
        return jnp.where(allowed[None], raw_scores, NEG_FILL)

    scores = masked_scores(queries)
    row_max = jnp.max(scores, axis=-1, keepdims=True)
    exp_scores = jnp.exp(scores - row_max)
    row_total = jnp.sum(exp_scores, axis=-1, keepdims=True)
    probs_low = (exp_scores / row_total).astype(jnp.bfloat16)
    log_total = row_max + jnp.log(row_total)
    attended = (
        jnp.einsum("htk,kd->thd", probs_low, value_all, preferred_element_type=jnp.float32)
        .reshape(tok_rows, head_count * head_dim)
        .astype(jnp.bfloat16)
    )
    mixer_out = mat_mul(attended, output_full)
    mixer_unit, mixer_inv = norm_parts(mixer_out)
    middle = hidden + mixer_unit * mixer_mult
    middle_mult = 1.0 + middle_full.astype(jnp.float32)
    output_mult = 1.0 + outgain_full.astype(jnp.float32)
    middle_unit, middle_inv = norm_parts(middle)
    middle_normed = (middle_unit * middle_mult).astype(jnp.bfloat16)
    middle_turned = mat_mul(middle_normed, turn).astype(jnp.bfloat16)
    gate_pre = jnp.concatenate([mat_mul(middle_normed, gate_a), mat_mul(middle_turned, gate_b)], axis=1)
    up_proj = jnp.concatenate([mat_mul(middle_normed, up_a), mat_mul(middle_turned, up_b)], axis=1)
    activation, gelu_pullback = jax.vjp(gelu_tanh, gate_pre)
    hidden_units = (activation * up_proj).astype(jnp.bfloat16)
    ffn_out = mat_mul(hidden_units, down_full)
    ffn_unit, ffn_inv = norm_parts(ffn_out)
    mixed_out = (middle + ffn_unit * output_mult).astype(jnp.bfloat16)
    grad_out = out_grad.astype(jnp.float32)
    output_gain_part = jnp.sum(grad_out * ffn_unit, axis=0)
    grad_ffn = norm_back(grad_out * output_mult, ffn_unit, ffn_inv).astype(jnp.bfloat16)
    grad_hidden = mat_mul_t(grad_ffn, down_full)
    down_term = mat_t_mul(hidden_units, grad_ffn).astype(jnp.bfloat16)
    grad_gate = gelu_pullback(grad_hidden * up_proj)[0].astype(jnp.bfloat16)
    grad_up = (grad_hidden * activation).astype(jnp.bfloat16)
    grad_turned = mat_mul_t(grad_gate[:, HID_A:], gate_b) + mat_mul_t(grad_up[:, HID_A:], up_b)
    turned_high = grad_turned.astype(jnp.bfloat16)
    turned_low = (grad_turned - turned_high.astype(jnp.float32)).astype(jnp.bfloat16)
    grad_middle_in = (
        mat_mul_t(grad_gate[:, :HID_A], gate_a)
        + mat_mul_t(grad_up[:, :HID_A], up_a)
        + mat_mul_t(turned_high, turn)
        + mat_mul_t(turned_low, turn)
    )
    middle_gain_part = jnp.sum(grad_middle_in * middle_unit, axis=0)
    gate_up_a = mat_t_mul(
        middle_normed, jnp.concatenate([grad_gate[:, :HID_A], grad_up[:, :HID_A]], axis=1)
    ).astype(jnp.bfloat16)
    gate_up_b = mat_t_mul(
        middle_turned, jnp.concatenate([grad_gate[:, HID_A:], grad_up[:, HID_A:]], axis=1)
    ).astype(jnp.bfloat16)
    grad_middle = grad_out + norm_back(grad_middle_in * middle_mult, middle_unit, middle_inv)
    query_back, key_back, value_back, output_back = (query_full, key_full, value_full, output_full)
    mixer_gain_part = jnp.sum(grad_middle * mixer_unit, axis=0)
    grad_mixer = norm_back(grad_middle * mixer_mult, mixer_unit, mixer_inv).astype(jnp.bfloat16)
    output_grad_full = mat_t_mul(attended, grad_mixer)
    grad_attended = (
        mat_mul_t(grad_mixer, output_back)
        .astype(jnp.bfloat16)
        .reshape(tok_rows, head_count, head_dim)
    )
    probs = jnp.exp(masked_scores(queries) - log_total)
    grad_probs = jnp.einsum(
        "thd,kd->htk", grad_attended, value_all, preferred_element_type=jnp.float32
    )
    delta_rows = jnp.sum(probs * grad_probs, axis=-1, keepdims=True)
    grad_scores = (probs * (grad_probs - delta_rows)).astype(jnp.bfloat16)
    grad_queries = (
        jnp.einsum("htk,kd->thd", grad_scores, key_all, preferred_element_type=jnp.float32)
        * score_scale
    )
    grad_keys_all = (
        jnp.einsum("htk,thd->kd", grad_scores, queries, preferred_element_type=jnp.float32)
        * score_scale
    )
    grad_values_all = jnp.einsum(
        "htk,thd->kd", probs_low, grad_attended, preferred_element_type=jnp.float32
    )
    own_start = hop_count * tok_rows
    key_grad = grad_keys_all[own_start:]
    value_grad = grad_values_all[own_start:]
    for step_back in range(1, hop_count + 1):
        block_at = (hop_count - step_back) * tok_rows
        back_keys, back_values = (
            shifted(
                grad_keys_all[block_at : block_at + tok_rows].astype(jnp.bfloat16), "dp", -step_back
            ).astype(jnp.float32),
            shifted(
                grad_values_all[block_at : block_at + tok_rows].astype(jnp.bfloat16),
                "dp",
                -step_back,
            ).astype(jnp.float32),
        )
        key_grad = key_grad + back_keys
        value_grad = value_grad + back_values
    key_grad_rot = rotary_back(key_grad[:, None, :], cosine, sine_table)[:, 0, :]
    key_gain_part = jnp.sum(key_grad_rot * key_unit, axis=0)
    grad_key_raw = norm_back(key_grad_rot * key_mult, key_unit, key_inv).astype(jnp.bfloat16)
    grad_value = value_grad.astype(jnp.bfloat16)
    query_grad_rot = rotary_back(grad_queries, cosine, sine_table)
    query_gain_part = jnp.sum(query_grad_rot * query_unit, axis=(0, 1))
    grad_query_raw = (
        norm_back(query_grad_rot * query_mult, query_unit, query_inv)
        .astype(jnp.bfloat16)
        .reshape(tok_rows, head_count * head_dim)
    )
    grad_normed = (
        mat_mul_t(grad_query_raw, query_back)
        + mat_mul_t(grad_key_raw, key_back)
        + mat_mul_t(grad_value, value_back)
    )
    input_gain_part = jnp.sum(grad_normed * input_unit, axis=0)
    input_grad = grad_middle + norm_back(grad_normed * input_mult, input_unit, input_inv)
    qk_term = mat_t_mul(normed, jnp.concatenate([grad_query_raw, grad_key_raw], axis=1))
    value_term = mat_t_mul(normed, grad_value)
    gain_terms = jnp.stack(
        [input_gain_part, mixer_gain_part, middle_gain_part, output_gain_part]
        + [
            jnp.pad(a.reshape(128, 2), ((0, 0), (0, 3))).reshape(640)
            for a in (query_gain_part, key_gain_part)
        ],
        axis=1,
    )
    term_x = jnp.concatenate(
        [
            qk_term.astype(jnp.bfloat16),
            jnp.pad(gain_terms, ((0, 0), (0, 122))).astype(jnp.bfloat16),
            value_term.astype(jnp.bfloat16),
            gate_up_a,
            jnp.zeros((640, 128), jnp.bfloat16),
        ],
        axis=1,
    )
    term_o = jnp.pad(output_grad_full.astype(jnp.bfloat16), ((0, 0), (0, 128)))
    sum_x, sum_z, down_grad, sum_o = scatter_all(
        term_x.reshape(4, 10, 16, 2 * WX),
        gate_up_b.reshape(4, 10, 16, 2 * WZ),
        down_term.reshape(16, 4, 2, 16, WD),
        term_o.reshape(16, 4, 16, 2 * WO),
    )
    query_wgrad = sum_x[0, :5, :1024]
    key_wgrad = sum_x[0, :5, 1024:1280]
    value_wgrad = sum_x[1, :5, :256]
    gate_grad = jnp.concatenate([sum_x[1, :5, 256:768], sum_z[0, :5]], axis=1)
    up_grad = jnp.concatenate([sum_x[1, :5, 768:1280], sum_z[1, :5]], axis=1)
    output_wgrad = jnp.concatenate([sum_o[0], sum_o[1, :, :256]], axis=1)
    sums = sum_x[0, :5, 1280:1408]
    input_gain_grad, mixer_gain_grad, middle_gain_grad, output_gain_grad = [
        sums[:, i] for i in range(4)
    ]
    query_gain_grad, key_gain_grad = sums[:2, 4], sums[:2, 5]
    return (
        mixed_out,
        input_grad,
        query_wgrad,
        key_wgrad,
        value_wgrad,
        output_wgrad,
        gate_grad,
        up_grad,
        down_grad,
        input_gain_grad,
        query_gain_grad,
        key_gain_grad,
        mixer_gain_grad,
        middle_gain_grad,
        output_gain_grad,
    )


def solution(mesh):
    return jax.shard_map(
        per_device,
        mesh=mesh,
        in_specs=(
            P("dp", None),
            P("dp", None),
            P("dp", None),
            P("dp", None),
            P("dp", None),
            P("dp", None),
            P("dp", None),
            P("dp", None),
            P("dp"),
            P("dp"),
            P("dp"),
            P("dp"),
            P("dp"),
            P("dp"),
            P(),
            P("dp", None),
        ),
        out_specs=(
            P("dp", None),
            P("dp", None),
            P("dp", None),
            P("dp", None),
            P("dp", None),
            P("dp", None),
            P("dp", None),
            P("dp", None),
            P("dp", None),
            P("dp"),
            P("dp"),
            P("dp"),
            P("dp"),
            P("dp"),
            P("dp"),
        ),
        check_vma=False,
    )
```

```python
import math

import jax
import jax.numpy as jnp
from jax import lax
from jax.experimental import pallas as pl
from jax.experimental.pallas import tpu as pltpu
from jax.sharding import PartitionSpec as P

MESH = pl.DeviceIdType.MESH
BF = jnp.bfloat16
F32 = jnp.float32
T = 256
D = 640
HD = 256
HEADS = 4
SPAN = 3 * T
WINDOW = 512
EPSILON = 1e-06
ROPE_BASE = 10000.0
NEG_FILL = -1e30
SCALE = 1.0 / math.sqrt(HD)
GELU_A = math.sqrt(2.0 / math.pi)
GELU_B = 0.044715
WX1, WZ1, WX2, WZ2, WD, WO = 512, 384, 1024, 1024, 640, 384
SEMS = 232
VMEM_CAP = 62 << 20


def place(x, z, y, c):
    return ((x % 4) * 4 + (z % 4)) * 8 + (y % 4) * 2 + c


class Links:
    def __init__(self, send_sems, recv_sems):
        self.me = lax.axis_index("dp")
        self.at = {"x": self.me // 32, "z": (self.me // 8) % 4, "y": (self.me // 2) % 4}
        self.core = self.me % 2
        self.other = 1 - self.core
        self.sib = place(self.at["x"], self.at["z"], self.at["y"], self.other)
        self.xz = self.at["x"] * 4 + self.at["z"]
        self.send_sems, self.recv_sems, self.used, self.open = send_sems, recv_sems, 0, []

    def peer(self, axis, steps):
        moved = dict(self.at)
        moved[axis] = moved[axis] + steps
        return place(moved["x"], moved["z"], moved["y"], self.core)

    def along(self, steps):
        return (self.me + 128 + steps) % 128

    def slot(self, axis, steps):
        return (self.at[axis] + steps) % 4

    def greet(self):
        sem = pltpu.get_barrier_semaphore()
        partners = [self.sib] + [self.along(s) for s in (1, 2, -1, -2)]
        for axis in ("x", "z", "y"):
            partners += [self.peer(axis, o) for o in (1, 2, 3)]
        for p in partners:
            pl.semaphore_signal(sem, inc=1, device_id=(p,), device_id_type=MESH)
        self.greeted = len(partners)

    def meet(self):
        pl.semaphore_wait(pltpu.get_barrier_semaphore(), self.greeted)

    def send(self, src, dst, target):
        i = self.used
        self.used += 1
        copy = pltpu.make_async_remote_copy(
            src_ref=src,
            dst_ref=dst,
            send_sem=self.send_sems.at[i],
            recv_sem=self.recv_sems.at[i],
            device_id=(target,),
            device_id_type=MESH,
        )
        copy.start()
        self.open.append(copy.wait_send)
        return copy

    def local(self, src, dst):
        i = self.used
        self.used += 1
        copy = pltpu.make_async_copy(src, dst, self.send_sems.at[i])
        copy.start()
        return copy

    def finish(self):
        for wait in self.open:
            wait()
        self.open = []


class Rows:
    def __init__(self, net, axes, width, refs):
        self.net, self.axes, self.width = net, axes, width
        self.own, self.e_src, self.e_dst, self.s1, self.s2, self.b3, self.w, self.tmp = refs
        self.ends = []

    def view(self, slot, at, n):
        rows = pl.ds(pl.multiple_of(slot * 160 + at * 16, 16), n * 16)
        return self.w.at[self.net.core, rows]

    def step0(self):
        self.e_src[...] = self.own[self.net.other].astype(BF)

    def step0b(self):
        self.swap = self.net.send(self.e_src, self.e_dst, self.net.sib)

    def step1(self):
        net, wide = self.net, slice(0, self.width)
        self.swap.wait_recv()
        mine = self.own[net.core][0:5]
        theirs = self.e_dst[...].astype(F32)[0:5]
        first = net.core == 0
        self.tmp[0:5, wide] = jnp.where(first, mine, theirs)
        self.tmp[5:10, wide] = jnp.where(first, theirs, mine)
        slot = self.s1.at[net.at[self.axes[0]]]
        slot[...] = self.tmp[0:16, wide].astype(BF)
        self.p = [net.send(slot, slot, net.peer(self.axes[0], o)) for o in (1, 2, 3)]

    def step2(self):
        net, wide = self.net, slice(0, self.width)
        for copy in self.p:
            copy.wait_recv()
        for j in range(4):
            self.tmp[10 * j : 10 * j + 10, wide] = self.s1[j].astype(F32)[0:10]
        slot = self.s2.at[net.at[self.axes[1]]]
        slot[...] = self.tmp[0:48, wide].astype(BF)
        self.p = [net.send(slot, slot, net.peer(self.axes[1], o)) for o in (1, 2, 3)]

    def step3(self):
        net, wide = self.net, slice(0, self.width)
        for copy in self.p:
            copy.wait_recv()
        for j in range(4):
            self.tmp[40 * j : 40 * j + 40, wide] = self.s2[j].astype(F32)[0:40]
        self.b3[...] = self.tmp[0:160, wide].astype(BF)
        axis = self.axes[2]
        dst = self.view(net.at[axis], 0, 10)
        self.up = net.send(self.b3, dst, net.peer(axis, 1))
        self.down = net.send(self.b3, dst, net.peer(axis, 3))
        self.ends.append(net.send(self.b3, dst, net.sib).wait_recv)
        self.ends.append(net.local(self.b3, dst).wait)

    blocks = 10

    def step4(self):
        net, axis, n = self.net, self.axes[2], self.blocks
        half = n // 2
        self.up.wait_recv()
        part = self.view(net.slot(axis, 3), 0, half)
        self.far_up = net.send(part, part, net.peer(axis, 1))
        self.down.wait_recv()
        part = self.view(net.slot(axis, 1), half, half)
        self.far_down = net.send(part, part, net.peer(axis, 3))
        for steps in (3, 1):
            whole = self.view(net.slot(axis, steps), 0, n)
            self.ends.append(net.send(whole, whole, net.sib).wait_recv)

    def step5(self):
        net, axis, half = self.net, self.axes[2], self.blocks // 2
        for copy, at in ((self.far_up, 0), (self.far_down, half)):
            copy.wait_recv()
            part = self.view(net.slot(axis, 2), at, half)
            self.ends.append(net.send(part, part, net.sib).wait_recv)

    def step6(self):
        for wait in self.ends:
            wait()


class Tiles(Rows):
    blocks = 16

    def __init__(self, net, w, by_core):
        self.net, self.w, self.by_core, self.axes = net, w, by_core, ("z", "x", "y")
        self.ends = []

    def view(self, slot, at, n):
        if self.by_core:
            return self.w.at[pl.ds(at, n), slot, self.net.core]
        return self.w.at[self.net.core, pl.ds(at, n), slot]

    def first(self, src):
        net = self.net
        dst = self.w.at[net.xz, net.at["y"], net.core] if self.by_core else self.w.at[net.core, net.xz, net.at["y"]]
        self.p = [net.send(src, dst, net.peer("z", o)) for o in (1, 2, 3)]
        self.kept = net.local(src, dst)

    def step2(self):
        net = self.net
        for copy in self.p:
            copy.wait_recv()
        self.kept.wait()
        part = self.view(net.at["y"], net.at["x"] * 4, 4)
        self.p = [net.send(part, part, net.peer("x", o)) for o in (1, 2, 3)]

    def step3(self):
        net = self.net
        for copy in self.p:
            copy.wait_recv()
        part = self.view(net.at["y"], 0, 16)
        self.up = net.send(part, part, net.peer("y", 1))
        self.down = net.send(part, part, net.peer("y", 3))
        self.ends.append(net.send(part, part, net.sib).wait_recv)


class RowSums:
    blocks = 10

    def __init__(self, net, axes, width, refs):
        self.net, self.axes, self.width = net, axes, width
        (self.g, self.b, self.f, self.n, self.t2, self.r2, self.t1, self.r1, self.total) = refs[:9]
        self.rest = refs[9:]
        self.swaps, self.onward, self.near = {}, {}, {}

    def view(self, steps, at, n, which):
        slot = self.net.slot(self.axes[2], steps)
        rows = pl.ds(pl.multiple_of(slot * 160 + at * 16, 16), n * 16)
        return self.g.at[which, rows]

    def rows(self, at, n):
        return pl.ds(at * 16, n * 16)

    def tile(self, steps, i):
        slot = self.net.slot(self.axes[2], steps)
        return (self.net.core, pl.ds(pl.multiple_of(slot * 160 + i * 16, 16), 16))

    def block(self, i):
        return pl.ds(pl.multiple_of(i * 16, 16), 16)

    def step0(self):
        net = self.net
        for steps in (2, 1, 3, 0):
            src = self.view(steps, 0, self.blocks, net.other)
            self.swaps[steps] = net.send(src, self.b.at[steps], net.sib)

    def add(self, steps, held, at, count):
        def body(i, carry):
            where = self.tile(steps, i + at)
            total = self.g[where].astype(F32) + held[self.block(i)].astype(F32)
            self.g[where] = total.astype(BF)
            return carry

        lax.fori_loop(0, count, body, 0)

    def step1(self):
        net, axis, n, core = self.net, self.axes[2], self.blocks, self.net.core
        half = n // 2
        for steps in (2, 1, 3, 0):
            self.swaps[steps].wait_recv()
            self.add(steps, self.b.at[steps], 0, n)
            if steps == 2:
                self.onward[1] = net.send(self.view(2, 0, half, core), self.f.at[0], net.peer(axis, 1))
                self.onward[3] = net.send(self.view(2, half, half, core), self.f.at[1], net.peer(axis, 3))
            elif steps == 1:
                self.near["a"] = net.send(
                    self.view(1, half, half, core), self.n.at[0, self.rows(half, half)], net.peer(axis, 1)
                )
            elif steps == 3:
                self.near["b"] = net.send(
                    self.view(3, 0, half, core), self.n.at[1, self.rows(0, half)], net.peer(axis, 3)
                )

    def step2(self):
        net, axis, core = self.net, self.axes[2], self.net.core
        half = self.blocks // 2
        self.onward[1].wait_recv()
        self.add(1, self.f.at[0], 0, half)
        self.near["c"] = net.send(self.view(1, 0, half, core), self.n.at[0, self.rows(0, half)], net.peer(axis, 1))
        self.onward[3].wait_recv()
        self.add(3, self.f.at[1], half, half)
        self.near["d"] = net.send(
            self.view(3, half, half, core), self.n.at[1, self.rows(half, half)], net.peer(axis, 3)
        )

    def total3(self, i):
        at = self.block(i)
        return self.g[self.tile(0, i)].astype(F32) + self.n[0, at].astype(F32) + self.n[1, at].astype(F32)

    def step3(self):
        net, width, axis = self.net, self.width, self.axes[1]
        for part in "abcd":
            self.near[part].wait_recv()

        def body(i, carry):
            self.total[self.block(i), 0 : self.width] = self.total3(i)
            return carry

        lax.fori_loop(0, 10, body, 0)
        for j in range(4):
            part = self.total[40 * j : 40 * j + 40, 0:width]
            self.t2[j] = jnp.concatenate([part, jnp.zeros((8, width), F32)], axis=0).astype(BF)
        self.p = [net.send(self.t2.at[net.slot(axis, o)], self.r2.at[o - 1], net.peer(axis, o)) for o in (1, 2, 3)]

    def step4(self):
        net, width, axis = self.net, self.width, self.axes[0]
        for copy in self.p:
            copy.wait_recv()
        own = self.t2[net.at[self.axes[1]]].astype(F32)
        for o in range(3):
            own = own + self.r2[o].astype(F32)
        self.total[0:48, 0:width] = own
        for j in range(4):
            part = self.total[10 * j : 10 * j + 10, 0:width]
            self.t1[j] = jnp.concatenate([part, jnp.zeros((6, width), F32)], axis=0).astype(BF)
        self.p = [net.send(self.t1.at[net.slot(axis, o)], self.r1.at[o - 1], net.peer(axis, o)) for o in (1, 2, 3)]

    def step5(self):
        net = self.net
        swap, got, out = self.rest
        for copy in self.p:
            copy.wait_recv()
        own = self.t1[net.at[self.axes[0]]].astype(F32)
        for o in range(3):
            own = own + self.r1[o].astype(F32)
        self.total[0:16, 0 : self.width] = own
        low_rows = self.total[0:8, 0 : self.width]
        high_rows = self.total[5:13, 0 : self.width]
        first = net.core == 0
        swap[...] = jnp.where(first, high_rows, low_rows)
        out[net.core] = jnp.where(first, low_rows, high_rows)
        self.last = net.send(swap, got, net.sib)

    def step6(self):
        swap, got, out = self.rest
        self.last.wait_recv()
        out[self.net.other] = got[...]


class TileSums(RowSums):
    blocks = 16

    def __init__(self, net, width, by_core, refs):
        self.by_core = by_core
        super().__init__(net, ("z", "x", "y"), width, refs)

    def view(self, steps, at, n, which):
        slot = self.net.slot("y", steps)
        if self.by_core:
            return self.g.at[pl.ds(at, n), slot, which]
        return self.g.at[which, pl.ds(at, n), slot]

    def rows(self, at, n):
        return pl.ds(at, n)

    def tile(self, steps, i):
        slot = self.net.slot("y", steps)
        return (i, slot, self.net.core) if self.by_core else (self.net.core, i, slot)

    def block(self, i):
        return i

    def step3(self):
        net = self.net
        for part in "abcd":
            self.near[part].wait_recv()

        def body(i, carry):
            self.t2[i] = self.total3(i).astype(BF)
            return carry

        lax.fori_loop(0, 16, body, 0)
        self.p = [
            net.send(self.t2.at[pl.ds(net.slot("x", o) * 4, 4)], self.r2.at[o - 1], net.peer("x", o))
            for o in (1, 2, 3)
        ]

    def step4(self):
        net = self.net
        for copy in self.p:
            copy.wait_recv()
        for j in range(4):
            value = self.t2[net.at["x"] * 4 + j].astype(F32)
            for o in range(3):
                value = value + self.r2[o, j].astype(F32)
            self.t1[j] = value.astype(BF)
        self.p = [net.send(self.t1.at[net.slot("z", o)], self.r1.at[o - 1], net.peer("z", o)) for o in (1, 2, 3)]

    def step5(self):
        net = self.net
        for copy in self.p:
            copy.wait_recv()
        own = self.t1[net.at["z"]].astype(F32)
        for o in range(3):
            own = own + self.r1[o].astype(F32)
        if self.by_core:
            self.rest[0][...] = own
            return
        swap, got, out = self.rest
        first = net.core == 0
        swap[...] = jnp.where(first, own[8:16], own[0:8])
        out[net.core] = jnp.where(first, own[0:8], own[8:16])
        self.last = net.send(swap, got, net.sib)

    def step6(self):
        if not self.by_core:
            super().step6()


def mm(left, right):
    return jnp.dot(left, right, preferred_element_type=F32)


def mm_t(left, right):
    return lax.dot_general(left, right, (((1,), (1,)), ((), ())), preferred_element_type=F32)


def t_mm(left, right):
    return lax.dot_general(left, right, (((0,), (0,)), ((), ())), preferred_element_type=F32)


def inv_of(values):
    return lax.rsqrt(jnp.mean(values * values, axis=-1, keepdims=True) + EPSILON)


def norm_back(upstream, unit_rows, inv_rms):
    return inv_rms * (upstream - unit_rows * jnp.mean(unit_rows * upstream, axis=-1, keepdims=True))


def spin(values, cosine, sine):
    a, b = values[:, :128], values[:, 128:]
    return jnp.concatenate([a * cosine - b * sine, b * cosine + a * sine], axis=1)


def spin_back(values, cosine, sine):
    a, b = values[:, :128], values[:, 128:]
    return jnp.concatenate([a * cosine + b * sine, b * cosine - a * sine], axis=1)


def count(shape, dim):
    return lax.broadcasted_iota(jnp.int32, shape, dim)


def hot(condition):
    return jnp.where(condition, 1.0, 0.0).astype(BF)


def split_dot(value, fixed):
    high = value.astype(BF)
    low = (value - high.astype(F32)).astype(BF)
    return mm_t(high, fixed) + mm_t(low, fixed)


class Refs:
    pass


def gather_setup(net, r):
    for ref in (r.own_x1, r.own_z1, r.own_x2, r.own_z2, r.own_o):
        ref[...] = jnp.zeros_like(ref)
    q = r.q[...].astype(F32)
    r.own_x1[0, 0:5] = q[:, 0:512]
    r.own_x1[1, 0:5, 0:256] = r.k[...].astype(F32)
    lane, row = count((8, 128), 1), count((8, 128), 0)
    fifth = (lane * 205) >> 10
    model = (lane < 20) & (lane - 5 * fifth == row)
    head = (lane >= 20) & (lane < 24) & (((lane - 20) & 1) == row)
    spread = jnp.where(model | head, jnp.broadcast_to(r.gains[...], (8, 128)), 0.0).astype(BF)
    source, target = count((128, 128), 0), count((128, 128), 1)
    place_of = jnp.where(source < 20, (source * 205) >> 10, 4 + ((source - 20) >> 1))
    tile = mm(spread, hot((place_of == target) & (source < 24)))
    r.own_x1[1, 0:5, 256:384] = tile[0:5]
    r.own_z1[0, 0:5] = q[:, 512:896]
    r.own_z1[1, 0:5, 0:128] = q[:, 896:1024]
    r.own_z1[1, 0:5, 128:384] = r.v[...].astype(F32)
    g, u = r.g[...].astype(F32), r.u[...].astype(F32)
    r.own_x2[0, 0:5] = g[:, 0:1024]
    r.own_x2[1, 0:5] = u[:, 0:1024]
    r.own_z2[0, 0:5] = g[:, 1024:2048]
    r.own_z2[1, 0:5] = u[:, 1024:2048]
    o = r.o[...].astype(F32)
    r.own_o[0, 0:8] = o[:, 0:384]
    r.own_o[1, 0:8, 0:256] = o[:, 384:640]

    def rows(name, axes, width):
        names = ("own_", "es_", "ed_", "s1_", "s2_", "b3_", "w_")
        return Rows(net, axes, width, [getattr(r, n + name) for n in names] + [r.tmp])

    x1 = rows("x1", ("y", "z", "x"), WX1)
    z1 = rows("z1", ("x", "y", "z"), WZ1)
    x2 = rows("x2", ("y", "z", "x"), WX2)
    z2 = rows("z2", ("x", "y", "z"), WZ2)
    for s in (x1, z1, x2, z2):
        s.step0()
    r.es_o[...] = r.own_o[net.other].astype(BF)
    return x1, z1, x2, z2, Tiles(net, r.w_o, False), Tiles(net, r.w_d, True)


def layer_kernel(names, *refs):
    r = Refs()
    for name, ref in zip(names, refs):
        setattr(r, name, ref)
    r.g_x2, r.g_z2, r.g_d, r.g_o = r.w_x2, r.w_z2, r.w_d, r.w_o
    for name in ("x1", "z1", "x2", "z2"):
        setattr(r, "t2_" + name, getattr(r, "s2_" + name))
        setattr(r, "t1_" + name, getattr(r, "s1_" + name))
    r.total_x2 = r.total_x1 = r.total_o = r.total_d = r.tmp
    r.g_middle = r.igrad
    net = Links(r.send_sems, r.recv_sems)
    net.greet()
    x1, z1, x2, z2, ow, dw = gather_setup(net, r)
    net.meet()
    x1.step0b()
    z1.step0b()
    swap_o = net.send(r.es_o, r.ed_o, net.sib)
    x2.step0b()
    z2.step0b()
    x1.step1()
    z1.step1()
    swap_o.wait_recv()
    mine, theirs = r.own_o[net.core][0:8], r.ed_o[...].astype(F32)[0:8]
    r.tmp[0:8, 0:WO] = jnp.where(net.core == 0, mine, theirs)
    r.tmp[8:16, 0:WO] = jnp.where(net.core == 0, theirs, mine)
    r.s1_o[...] = r.tmp[0:16, 0:WO].astype(BF)
    ow.first(r.s1_o)
    x2.step1()
    z2.step1()
    dw.first(r.d)

    k_dim, j_dim = count((D, D), 0), count((D, D), 1)
    tens = (j_dim * 52429) >> 19
    source = (tens & 3) * 160 + (tens >> 4) * 40 + ((tens >> 2) & 3) * 10 + (j_dim - 10 * tens)
    r.turn[...] = hot(k_dim == source)
    r.eye[...] = hot(k_dim == j_dim)
    spot = count((64, 64), 0)
    lens = jnp.broadcast_to(r.lens[...].astype(F32), (64, 64))
    column = jnp.sum(jnp.where(spot == count((64, 64), 1), lens, 0.0), axis=1, keepdims=True)
    ends = jnp.sum(jnp.where(spot <= count((64, 64), 1), column, 0.0), axis=0, keepdims=True)
    offset = net.me * T
    token = (count((T, 64), 0) + offset).astype(F32)
    start = jnp.max(jnp.where(ends <= token, ends, 0.0), axis=1, keepdims=True)
    position = token[:, 0:1] - start
    pair = count((1, 128), 1).astype(F32)
    angle = position * jnp.exp(pair * (-2.0 * math.log(ROPE_BASE) / HD))
    r.cosine[...] = jnp.cos(angle)
    r.sine[...] = jnp.sin(angle)
    ahead = count((T, SPAN), 1) - 2 * T
    distance = count((T, SPAN), 0) - ahead
    inside = (distance >= 0) & (distance < WINDOW) & ((ahead + offset).astype(F32) >= start)
    r.bias[...] = jnp.where(inside, 0.0, NEG_FILL)
    hidden = r.h[...].astype(F32)
    input_inv = inv_of(hidden)
    r.in_unit[...] = hidden * input_inv

    for s in (x1, z1, ow, x2, z2, dw):
        s.step2()
    for s in (x1, z1, ow, x2, z2, dw):
        s.step3()
    for s in (x1, z1, ow):
        s.step4()
    for s in (x1, z1, ow):
        s.step5()
    x1.step6()
    z1.step6()

    gain_tile = r.w_x1[1, :, 256:384]
    gain_rows = t_mm(gain_tile, r.eye[...])
    far, near = count((D, HD), 0), count((D, HD), 1)
    r.pick[...] = hot(far == 5 * (near >> 1) + (near & 1))
    head_rows = t_mm(gain_tile, r.pick[...])
    r.mults[0:4] = 1.0 + gain_rows[0:4]
    r.mults[4:6, 0:HD] = 1.0 + head_rows[4:6]
    normed = (r.in_unit[...] * r.mults[0:1]).astype(BF)
    r.normed[...] = normed
    turned = mm(normed, r.turn[...]).astype(BF)
    r.normed_t[...] = turned
    cosine, sine = r.cosine[...], r.sine[...]
    key_raw = mm(normed, r.w_x1[1, :, 0:256])
    key_inv = inv_of(key_raw)
    r.k_unit[...] = key_raw * key_inv
    r.keys[2 * T :] = spin(r.k_unit[...] * r.mults[5:6, 0:HD], cosine, sine).astype(BF)
    r.values[2 * T :] = mm(turned, r.w_z1[1, :, 128:384]).astype(BF)
    halo = []
    for steps, at in ((1, T), (2, 0)):
        for whole in (r.keys, r.values):
            halo.append(net.send(whole.at[pl.ds(2 * T, T)], whole.at[pl.ds(at, T)], net.along(steps)))
    for h in range(HEADS):
        if h < 2:
            raw = mm(normed, r.w_x1[0, :, 256 * h : 256 * h + 256])
        elif h == 2:
            raw = mm(turned, r.w_z1[0, :, 0:256])
        else:
            raw = jnp.concatenate(
                [mm(turned, r.w_z1[0, :, 256:384]), mm(turned, r.w_z1[1, :, 0:128])], axis=1
            )
        inv = inv_of(raw)
        r.q_inv[h] = inv
        r.q_unit[h] = raw * inv
        r.queries[h] = spin(raw * inv * r.mults[4:5, 0:HD], cosine, sine).astype(BF)
    for s in (x2, z2, dw):
        s.step4()
    for copy in halo:
        copy.wait_recv()

    def attend(h, carry):
        scores = mm_t(r.queries[h], r.keys[...]) * SCALE + r.bias[...]
        row_max = jnp.max(scores, axis=1, keepdims=True)
        weights = jnp.exp(scores - row_max)
        probs = weights / jnp.sum(weights, axis=1, keepdims=True)
        r.probs[h] = probs
        r.attended[h] = mm(probs.astype(BF), r.values[...]).astype(BF)
        return carry

    lax.fori_loop(0, 2, attend, 0)
    for s in (x2, z2, dw):
        s.step5()
    lax.fori_loop(2, 4, attend, 0)

    ow.step6()
    left = jnp.zeros((T, 384), F32)
    right = jnp.zeros((T, 256), F32)
    for h in range(HEADS):
        some = slice(4 * h, 4 * h + 4)
        left = left + mm(r.attended[h], r.w_o[0, some].reshape(256, WO))
        right = right + mm(r.attended[h], r.w_o[1, some].reshape(256, WO)[:, 0:256])
    mixer_out = jnp.concatenate([left, right], axis=1)
    mixer_inv = inv_of(mixer_out)
    r.mix_unit[...] = mixer_out * mixer_inv
    middle = r.h[...].astype(F32) + r.mix_unit[...] * r.mults[1:2]
    middle_inv = inv_of(middle)
    r.mid_unit[...] = middle * middle_inv
    r.middle[...] = middle
    r.mid[...] = (r.mid_unit[...] * r.mults[2:3]).astype(BF)
    r.mid_t[...] = mm(r.mid[...], r.turn[...]).astype(BF)
    for s in (x2, z2, dw):
        s.step6()

    r.acc[...] = jnp.zeros_like(r.acc)
    for w, rows_in, first in ((r.w_x2, r.mid, 0), (r.w_z2, r.mid_t, 2)):

        def forward(j, carry, w=w, rows_in=rows_in, first=first):
            cols = pl.ds(pl.multiple_of(j * 512, 512), 512)
            gate = mm(rows_in[...], w[0, :, cols])
            up = mm(rows_in[...], w[1, :, cols])
            square = gate * gate
            tanh = jnp.tanh(GELU_A * gate * (1.0 + GELU_B * square))
            active = 0.5 * gate * (1.0 + tanh)
            slope = 0.5 * (1.0 + tanh) + 0.5 * gate * (1.0 - tanh * tanh) * (
                GELU_A * (1.0 + 3.0 * GELU_B * square)
            )
            units = (active * up).astype(BF)
            part = first + j
            r.units[part] = units
            r.active[part] = active
            r.slope_up[part] = slope * up
            r.acc[...] += mm(units, r.w_d[pl.ds(part * 4, 4)].reshape(512, D))
            return carry

        lax.fori_loop(0, 2, forward, 0)
    ffn_out = r.acc[...]
    ffn_inv = inv_of(ffn_out)
    ffn_unit = ffn_out * ffn_inv
    r.mixed[...] = (r.middle[...] + ffn_unit * r.mults[3:4]).astype(BF)
    grad_out = r.og[...].astype(F32)
    r.gain_sums[...] = jnp.zeros_like(r.gain_sums)
    r.gain_sums[3:4] = jnp.sum(grad_out * ffn_unit, axis=0, keepdims=True)
    r.g_ffn[...] = norm_back(grad_out * r.mults[3:4], ffn_unit, ffn_inv).astype(BF)
    net.finish()
    for w, g, rows_in, first, total in (
        (r.w_x2, r.g_x2, r.mid, 0, r.acc),
        (r.w_z2, r.g_z2, r.mid_t, 2, r.acc_t),
    ):
        total[...] = jnp.zeros_like(total)

        def backward(j, carry, w=w, g=g, rows_in=rows_in, first=first, total=total):
            cols = pl.ds(pl.multiple_of(j * 512, 512), 512)
            part = first + j
            some = pl.ds(part * 4, 4)
            g_ffn = r.g_ffn[...]
            grad_hidden = mm_t(g_ffn, r.w_d[some].reshape(512, D))
            r.g_d[some] = t_mm(r.units[part], g_ffn).astype(BF).reshape(4, 4, 2, 16, D)
            grad_gate = (grad_hidden * r.slope_up[part]).astype(BF)
            grad_up = (grad_hidden * r.active[part]).astype(BF)
            total[...] += mm_t(grad_gate, w[0, :, cols]) + mm_t(grad_up, w[1, :, cols])
            g[0, :, cols] = t_mm(rows_in[...], grad_gate).astype(BF)
            g[1, :, cols] = t_mm(rows_in[...], grad_up).astype(BF)
            return carry

        lax.fori_loop(0, 2, backward, 0)

    def sums(kind, name, *args):
        tags = ("g_", "b_", "f_", "n_", "t2_", "r2_", "t1_", "r1_", "total_", "swap_", "got_", "out_")
        if name == "d":
            tags = tags[:9] + tags[11:]
        return kind(net, *args, [getattr(r, tag + name) for tag in tags])

    sx1 = sums(RowSums, "x1", ("y", "z", "x"), WX1)
    sz1 = sums(RowSums, "z1", ("x", "y", "z"), WZ1)
    sx2 = sums(RowSums, "x2", ("y", "z", "x"), WX2)
    sz2 = sums(RowSums, "z2", ("x", "y", "z"), WZ2)
    so = sums(TileSums, "o", WO, False)
    sd = sums(TileSums, "d", WD, True)
    for s in (sx2, sz2, sd):
        s.step0()

    grad_in = r.acc[...] + split_dot(r.acc_t[...], r.turn[...])
    mid_unit = r.mid_unit[...]
    r.gain_sums[2:3] = jnp.sum(grad_in * mid_unit, axis=0, keepdims=True)
    grad_middle = r.og[...].astype(F32) + norm_back(grad_in * r.mults[2:3], mid_unit, inv_of(r.middle[...]))
    r.g_middle[...] = grad_middle
    mix_unit = r.mix_unit[...]
    r.gain_sums[1:2] = jnp.sum(grad_middle * mix_unit, axis=0, keepdims=True)
    grad_mixer = norm_back(grad_middle * r.mults[1:2], mix_unit, mixer_inv).astype(BF)
    for h in range(HEADS):
        some = slice(4 * h, 4 * h + 4)
        r.g_att[h] = (
            mm_t(grad_mixer[:, 0:384], r.w_o[0, some].reshape(256, WO))
            + mm_t(grad_mixer[:, 384:640], r.w_o[1, some].reshape(256, WO)[:, 0:256])
        ).astype(BF)
        grad = t_mm(r.attended[h], grad_mixer).astype(BF)
        r.g_o[0, some] = grad[:, 0:384].reshape(4, 4, 16, 384)
        r.g_o[1, some, :, :, 0:256] = grad[:, 384:640].reshape(4, 4, 16, 256)
    so.step0()
    for s in (sx2, sz2, sd, so):
        s.step1()

    r.d_keys[...] = jnp.zeros_like(r.d_keys)
    r.d_values[...] = jnp.zeros_like(r.d_values)
    r.q_gain[...] = jnp.zeros_like(r.q_gain)

    def attend_back(h, carry):
        probs = r.probs[h]
        g_att = r.g_att[h]
        grad_probs = mm_t(g_att, r.values[...])
        delta = jnp.sum(probs * grad_probs, axis=1, keepdims=True)
        grad_scores = (probs * (grad_probs - delta)).astype(BF)
        grad_q = mm(grad_scores, r.keys[...]) * SCALE
        r.d_keys[...] += t_mm(grad_scores, r.queries[h])
        r.d_values[...] += t_mm(probs.astype(BF), g_att)
        back = spin_back(grad_q, r.cosine[...], r.sine[...])
        unit = r.q_unit[h]
        r.q_gain[...] += jnp.sum(back * unit, axis=0, keepdims=True)
        r.g_q[h] = norm_back(back * r.mults[4:5, 0:HD], unit, r.q_inv[h]).astype(BF)
        return carry

    lax.fori_loop(0, 2, attend_back, 0)
    for s in (sx2, sz2, sd, so):
        s.step2()
    lax.fori_loop(2, 4, attend_back, 0)
    back_halo = []
    for i, (whole, low) in enumerate(((r.d_keys, r.dk_low), (r.d_values, r.dv_low))):
        scale = SCALE if i == 0 else 1.0
        low[...] = (whole[0 : 2 * T] * scale).astype(BF)
        for steps, at in ((-1, T), (-2, 0)):
            back_halo.append(
                net.send(low.at[pl.ds(at, T)], r.halo_back.at[i, 0 if at else 1], net.along(steps))
            )

    normed, turned = r.normed[...], r.normed_t[...]
    for h in range(HEADS):
        if h < 2:
            r.g_x1[0, :, 256 * h : 256 * h + 256] = t_mm(normed, r.g_q[h]).astype(BF)
        elif h == 2:
            r.g_z1[0, :, 0:256] = t_mm(turned, r.g_q[h]).astype(BF)
        else:
            last = t_mm(turned, r.g_q[h]).astype(BF)
            r.g_z1[0, :, 256:384] = last[:, 0:128]
            r.g_z1[1, :, 0:128] = last[:, 128:256]
    for s in (sx2, sz2, sd, so):
        s.step3()
    for copy in back_halo:
        copy.wait_recv()
    own_k = r.d_keys[2 * T :] * SCALE
    own_v = r.d_values[2 * T :]
    for i in range(2):
        own_k = own_k + r.halo_back[0, i].astype(F32)
        own_v = own_v + r.halo_back[1, i].astype(F32)
    key_back = spin_back(own_k, r.cosine[...], r.sine[...])
    k_unit = r.k_unit[...]
    key_gain = jnp.sum(key_back * k_unit, axis=0, keepdims=True)
    grad_k = norm_back(key_back * r.mults[5:6, 0:HD], k_unit, key_inv).astype(BF)
    grad_v = own_v.astype(BF)
    r.g_z1[1, :, 128:384] = t_mm(turned, grad_v).astype(BF)
    sz1.step0()
    r.g_x1[1, :, 0:256] = t_mm(normed, grad_k).astype(BF)
    r.g_x1[1, :, 384:512] = jnp.zeros((D, 128), BF)
    grad_natural = (
        mm_t(r.g_q[0], r.w_x1[0, :, 0:256])
        + mm_t(r.g_q[1], r.w_x1[0, :, 256:512])
        + mm_t(grad_k, r.w_x1[1, :, 0:256])
    )
    g_last = r.g_q[3]
    grad_turned = (
        mm_t(r.g_q[2], r.w_z1[0, :, 0:256])
        + mm_t(g_last[:, 0:128], r.w_z1[0, :, 256:384])
        + mm_t(g_last[:, 128:256], r.w_z1[1, :, 0:128])
        + mm_t(grad_v, r.w_z1[1, :, 128:384])
    )
    grad_normed = grad_natural + split_dot(grad_turned, r.turn[...])
    in_unit = r.in_unit[...]
    r.gain_sums[0:1] = jnp.sum(grad_normed * in_unit, axis=0, keepdims=True)
    both = jnp.concatenate([r.q_gain[...], key_gain, jnp.zeros((6, HD), F32)], axis=0).astype(BF)
    r.gain_sums[4:6] = mm_t(both, r.pick[...])[0:2]
    r.g_x1[1, :, 256:384] = mm_t(r.eye[...], r.gain_sums[...].astype(BF)).astype(BF)
    sx1.step0()
    r.igrad[...] = r.g_middle[...] + norm_back(grad_normed * r.mults[0:1], in_unit, input_inv)
    for s in (sx2, sz2, sd, so):
        s.step4()
    sz1.step1()
    sx1.step1()
    for s in (sx2, sz2, sd, so):
        s.step5()
    for step in ("step2", "step3", "step4", "step5", "step6"):
        for s in (sz1, sx1):
            getattr(s, step)()
    for s in (sx2, sz2, sd, so):
        s.step6()
    net.finish()


def layer(h, q, k, v, o, g, u, d, gains, lens, og):
    vmem = pltpu.VMEM
    ins = ("h", "q", "k", "v", "o", "g", "u", "d", "gains", "lens", "og")
    outs = {
        "mixed": ((T, D), BF),
        "igrad": ((T, D), F32),
        "out_x1": ((2, 8, WX1), F32),
        "out_z1": ((2, 8, WZ1), F32),
        "out_o": ((2, 8, WO), F32),
        "out_x2": ((2, 8, WX2), F32),
        "out_z2": ((2, 8, WZ2), F32),
        "out_d": ((16, WD), F32),
    }
    scratch = {}
    for name, w in (("x1", WX1), ("z1", WZ1), ("x2", WX2), ("z2", WZ2)):
        scratch |= {
            "own_" + name: ((2, 16, w), F32),
            "es_" + name: ((16, w), BF),
            "ed_" + name: ((16, w), BF),
            "s1_" + name: ((4, 16, w), BF),
            "s2_" + name: ((4, 48, w), BF),
            "b3_" + name: ((160, w), BF),
            "w_" + name: ((2, D, w), BF),
            "b_" + name: ((4, 160, w), BF),
            "f_" + name: ((2, 80, w), BF),
            "n_" + name: ((2, 160, w), BF),
            "r2_" + name: ((3, 48, w), BF),
            "r1_" + name: ((3, 16, w), BF),
            "swap_" + name: ((8, w), F32),
            "got_" + name: ((8, w), F32),
        }
    for name, w in (("o", WO), ("d", WD)):
        scratch |= {
            "b_" + name: ((4, 16, 16, w), BF),
            "f_" + name: ((2, 8, 16, w), BF),
            "n_" + name: ((2, 16, 16, w), BF),
            "t2_" + name: ((16, 16, w), BF),
            "r2_" + name: ((3, 4, 16, w), BF),
            "t1_" + name: ((4, 16, w), BF),
            "r1_" + name: ((3, 16, w), BF),
        }
    scratch |= {
        "g_x1": ((2, D, WX1), BF),
        "g_z1": ((2, D, WZ1), BF),
        "total_z2": ((160, WZ2), F32),
        "total_z1": ((160, WZ1), F32),
        "own_o": ((2, 16, WO), F32),
        "es_o": ((16, WO), BF),
        "ed_o": ((16, WO), BF),
        "s1_o": ((16, WO), BF),
        "swap_o": ((8, WO), F32),
        "got_o": ((8, WO), F32),
        "w_o": ((2, 16, 4, 16, WO), BF),
        "w_d": ((16, 4, 2, 16, WD), BF),
        "tmp": ((160, 1024), F32),
        "turn": ((D, D), BF),
        "eye": ((D, D), BF),
        "pick": ((D, HD), BF),
        "cosine": ((T, 128), F32),
        "sine": ((T, 128), F32),
        "bias": ((T, SPAN), F32),
        "mults": ((8, D), F32),
        "gain_sums": ((128, D), F32),
        "in_unit": ((T, D), F32),
        "normed": ((T, D), BF),
        "normed_t": ((T, D), BF),
        "k_unit": ((T, HD), F32),
        "keys": ((SPAN, HD), BF),
        "values": ((SPAN, HD), BF),
        "queries": ((HEADS, T, HD), BF),
        "q_unit": ((HEADS, T, HD), F32),
        "q_inv": ((HEADS, T, 1), F32),
        "probs": ((HEADS, T, SPAN), F32),
        "attended": ((HEADS, T, HD), BF),
        "mix_unit": ((T, D), F32),
        "mid_unit": ((T, D), F32),
        "middle": ((T, D), F32),
        "mid": ((T, D), BF),
        "mid_t": ((T, D), BF),
        "units": ((4, T, 512), BF),
        "active": ((4, T, 512), F32),
        "slope_up": ((4, T, 512), F32),
        "acc": ((T, D), F32),
        "acc_t": ((T, D), F32),
        "g_ffn": ((T, D), BF),
        "g_att": ((HEADS, T, HD), BF),
        "g_q": ((HEADS, T, HD), BF),
        "d_keys": ((SPAN, HD), F32),
        "d_values": ((SPAN, HD), F32),
        "dk_low": ((2 * T, HD), BF),
        "dv_low": ((2 * T, HD), BF),
        "halo_back": ((2, 2, T, HD), BF),
        "q_gain": ((1, HD), F32),
    }
    inside = pl.BlockSpec(memory_space=vmem)
    names = (*ins, *outs, *scratch, "send_sems", "recv_sems")
    return pl.pallas_call(
        lambda *refs: layer_kernel(names, *refs),
        out_shape=[jax.ShapeDtypeStruct(*s) for s in outs.values()],
        in_specs=[inside] * len(ins),
        out_specs=[inside] * len(outs),
        scratch_shapes=[vmem(*s) for s in scratch.values()] + [pltpu.SemaphoreType.DMA((SEMS,))] * 2,
        compiler_params=pltpu.CompilerParams(
            collective_id=0, has_side_effects=True, vmem_limit_bytes=VMEM_CAP
        ),
        name="decoder_layer",
    )(h, q, k, v, o, g, u, d, gains, lens, og)


def per_device(
    hidden_in,
    query_weight,
    key_weight,
    value_weight,
    output_weight,
    gate_weight,
    up_weight,
    down_weight,
    input_gain,
    query_gain,
    key_gain,
    mixer_gain,
    middle_gain,
    output_gain,
    seq_lengths,
    out_grad,
):
    gains = jnp.concatenate([input_gain, mixer_gain, middle_gain, output_gain, query_gain, key_gain])
    gains = jnp.pad(gains.astype(F32), (0, 104)).reshape(1, 128)
    mixed, igrad, x1, z1, o, x2, z2, down_grad = layer(
        hidden_in,
        query_weight,
        key_weight,
        value_weight,
        output_weight,
        gate_weight,
        up_weight,
        down_weight,
        gains,
        seq_lengths.reshape(1, 64),
        out_grad,
    )
    sums = x1[1, :5, 256:384]
    return (
        mixed,
        igrad,
        jnp.concatenate([x1[0, :5], z1[0, :5], z1[1, :5, 0:128]], axis=1),
        x1[1, :5, 0:256],
        z1[1, :5, 128:384],
        jnp.concatenate([o[0], o[1, :, 0:256]], axis=1),
        jnp.concatenate([x2[0, :5], z2[0, :5]], axis=1),
        jnp.concatenate([x2[1, :5], z2[1, :5]], axis=1),
        down_grad,
        sums[:, 0],
        sums[:2, 4],
        sums[:2, 5],
        sums[:, 1],
        sums[:, 2],
        sums[:, 3],
    )


def solution(mesh):
    return jax.shard_map(
        per_device,
        mesh=mesh,
        in_specs=(
            P("dp", None),
            P("dp", None),
            P("dp", None),
            P("dp", None),
            P("dp", None),
            P("dp", None),
            P("dp", None),
            P("dp", None),
            P("dp"),
            P("dp"),
            P("dp"),
            P("dp"),
            P("dp"),
            P("dp"),
            P(),
            P("dp", None),
        ),
        out_specs=(
            P("dp", None),
            P("dp", None),
            P("dp", None),
            P("dp", None),
            P("dp", None),
            P("dp", None),
            P("dp", None),
            P("dp", None),
            P("dp", None),
            P("dp"),
            P("dp"),
            P("dp"),
            P("dp"),
            P("dp"),
            P("dp"),
        ),
        check_vma=False,
    )
```

```python
import math

import jax
import jax.numpy as jnp
from jax import lax
from jax.experimental import pallas as pl
from jax.experimental.pallas import tpu as pltpu
from jax.sharding import PartitionSpec as P

MESH = pl.DeviceIdType.MESH
BF = jnp.bfloat16
F32 = jnp.float32
T = 256
D = 640
HD = 256
HEADS = 4
SPAN = 3 * T
WINDOW = 512
EPSILON = 1e-06
ROPE_BASE = 10000.0
NEG_FILL = -1e30
SCALE = 1.0 / math.sqrt(HD)
GELU_A = math.sqrt(2.0 / math.pi)
GELU_B = 0.044715
WX1, WZ1, WX2, WZ2, WD, WO = 512, 384, 1024, 1024, 640, 384
SEMS = 232
GAINS = ("n_in", "n_mix", "n_mid", "n_out", "n_q", "n_k")
VMEM_CAP = 62 << 20


def place(x, z, y, c):
    return ((x % 4) * 4 + (z % 4)) * 8 + (y % 4) * 2 + c


class Links:
    def __init__(self, send_sems, recv_sems):
        self.me = lax.axis_index("dp")
        self.at = {"x": self.me // 32, "z": (self.me // 8) % 4, "y": (self.me // 2) % 4}
        self.core = self.me % 2
        self.other = 1 - self.core
        self.sib = place(self.at["x"], self.at["z"], self.at["y"], self.other)
        self.xz = self.at["x"] * 4 + self.at["z"]
        self.send_sems, self.recv_sems, self.used, self.open = send_sems, recv_sems, 0, []

    def peer(self, axis, steps):
        moved = dict(self.at)
        moved[axis] = moved[axis] + steps
        return place(moved["x"], moved["z"], moved["y"], self.core)

    def along(self, steps):
        return (self.me + 128 + steps) % 128

    def slot(self, axis, steps):
        return (self.at[axis] + steps) % 4

    def greet(self):
        sem = pltpu.get_barrier_semaphore()
        partners = [self.sib] + [self.along(s) for s in (1, 2, -1, -2)]
        for axis in ("x", "z", "y"):
            partners += [self.peer(axis, o) for o in (1, 2, 3)]
        for p in partners:
            pl.semaphore_signal(sem, inc=1, device_id=(p,), device_id_type=MESH)
        self.greeted = len(partners)

    def meet(self):
        pl.semaphore_wait(pltpu.get_barrier_semaphore(), self.greeted)

    def send(self, src, dst, target):
        i = self.used
        self.used += 1
        copy = pltpu.make_async_remote_copy(
            src_ref=src,
            dst_ref=dst,
            send_sem=self.send_sems.at[i],
            recv_sem=self.recv_sems.at[i],
            device_id=(target,),
            device_id_type=MESH,
        )
        copy.start()
        self.open.append(copy.wait_send)
        return copy

    def local(self, src, dst):
        i = self.used
        self.used += 1
        copy = pltpu.make_async_copy(src, dst, self.send_sems.at[i])
        copy.start()
        return copy

    def finish(self):
        for wait in self.open:
            wait()
        self.open = []


class Rows:
    def __init__(self, net, axes, width, refs):
        self.net, self.axes, self.width = net, axes, width
        self.own, self.e_src, self.e_dst, self.s1, self.s2, self.b3, self.w, self.tmp = refs
        self.ends = []

    def view(self, slot, at, n):
        rows = pl.ds(pl.multiple_of(slot * 160 + at * 16, 16), n * 16)
        return self.w.at[self.net.core, rows]

    def step0(self):
        self.e_src[...] = self.own[self.net.other].astype(BF)

    def step0b(self):
        self.swap = self.net.send(self.e_src, self.e_dst, self.net.sib)

    def step1(self):
        net, wide = self.net, slice(0, self.width)
        self.swap.wait_recv()
        mine = self.own[net.core][0:5]
        theirs = self.e_dst[...].astype(F32)[0:5]
        first = net.core == 0
        self.tmp[0:5, wide] = jnp.where(first, mine, theirs)
        self.tmp[5:10, wide] = jnp.where(first, theirs, mine)
        slot = self.s1.at[net.at[self.axes[0]]]
        slot[...] = self.tmp[0:16, wide].astype(BF)
        self.p = [net.send(slot, slot, net.peer(self.axes[0], o)) for o in (1, 2, 3)]

    def step2(self):
        net, wide = self.net, slice(0, self.width)
        for copy in self.p:
            copy.wait_recv()
        for j in range(4):
            self.tmp[10 * j : 10 * j + 10, wide] = self.s1[j].astype(F32)[0:10]
        slot = self.s2.at[net.at[self.axes[1]]]
        slot[...] = self.tmp[0:48, wide].astype(BF)
        self.p = [net.send(slot, slot, net.peer(self.axes[1], o)) for o in (1, 2, 3)]

    def step3(self):
        net, wide = self.net, slice(0, self.width)
        for copy in self.p:
            copy.wait_recv()
        for j in range(4):
            self.tmp[40 * j : 40 * j + 40, wide] = self.s2[j].astype(F32)[0:40]
        self.b3[...] = self.tmp[0:160, wide].astype(BF)
        axis = self.axes[2]
        dst = self.view(net.at[axis], 0, 10)
        self.up = net.send(self.b3, dst, net.peer(axis, 1))
        self.down = net.send(self.b3, dst, net.peer(axis, 3))
        self.ends.append(net.send(self.b3, dst, net.sib).wait_recv)
        self.ends.append(net.local(self.b3, dst).wait)

    blocks = 10

    def step4(self):
        net, axis, n = self.net, self.axes[2], self.blocks
        half = n // 2
        self.up.wait_recv()
        part = self.view(net.slot(axis, 3), 0, half)
        self.far_up = net.send(part, part, net.peer(axis, 1))
        self.down.wait_recv()
        part = self.view(net.slot(axis, 1), half, half)
        self.far_down = net.send(part, part, net.peer(axis, 3))
        for steps in (3, 1):
            whole = self.view(net.slot(axis, steps), 0, n)
            self.ends.append(net.send(whole, whole, net.sib).wait_recv)

    def step5(self):
        net, axis, half = self.net, self.axes[2], self.blocks // 2
        for copy, at in ((self.far_up, 0), (self.far_down, half)):
            copy.wait_recv()
            part = self.view(net.slot(axis, 2), at, half)
            self.ends.append(net.send(part, part, net.sib).wait_recv)

    def step6(self):
        for wait in self.ends:
            wait()


class Tiles(Rows):
    blocks = 16

    def __init__(self, net, w, by_core):
        self.net, self.w, self.by_core, self.axes = net, w, by_core, ("z", "x", "y")
        self.ends = []

    def view(self, slot, at, n):
        if self.by_core:
            return self.w.at[pl.ds(at, n), slot, self.net.core]
        return self.w.at[self.net.core, pl.ds(at, n), slot]

    def first(self, src):
        net = self.net
        dst = self.w.at[net.xz, net.at["y"], net.core] if self.by_core else self.w.at[net.core, net.xz, net.at["y"]]
        self.p = [net.send(src, dst, net.peer("z", o)) for o in (1, 2, 3)]
        self.kept = net.local(src, dst)

    def step2(self):
        net = self.net
        for copy in self.p:
            copy.wait_recv()
        self.kept.wait()
        part = self.view(net.at["y"], net.at["x"] * 4, 4)
        self.p = [net.send(part, part, net.peer("x", o)) for o in (1, 2, 3)]

    def step3(self):
        net = self.net
        for copy in self.p:
            copy.wait_recv()
        part = self.view(net.at["y"], 0, 16)
        self.up = net.send(part, part, net.peer("y", 1))
        self.down = net.send(part, part, net.peer("y", 3))
        self.ends.append(net.send(part, part, net.sib).wait_recv)


class RowSums:
    blocks = 10

    def __init__(self, net, axes, width, refs):
        self.net, self.axes, self.width = net, axes, width
        (self.g, self.b, self.f, self.n, self.t2, self.r2, self.t1, self.r1, self.total) = refs[:9]
        self.rest = refs[9:]
        self.swaps, self.onward, self.near = {}, {}, {}

    def view(self, steps, at, n, which):
        slot = self.net.slot(self.axes[2], steps)
        rows = pl.ds(pl.multiple_of(slot * 160 + at * 16, 16), n * 16)
        return self.g.at[which, rows]

    def rows(self, at, n):
        return pl.ds(at * 16, n * 16)

    def tile(self, steps, i):
        slot = self.net.slot(self.axes[2], steps)
        return (self.net.core, pl.ds(pl.multiple_of(slot * 160 + i * 16, 16), 16))

    def block(self, i):
        return pl.ds(pl.multiple_of(i * 16, 16), 16)

    def give(self, steps):
        src = self.view(steps, 0, self.blocks, self.net.other)
        self.swaps[steps] = self.net.send(src, self.b.at[steps], self.net.sib)

    def add(self, steps, held, at, count):
        def body(i, carry):
            where = self.tile(steps, i + at)
            self.g[where] = self.g[where] + held[self.block(i)]
            return carry

        lax.fori_loop(0, count, body, 0)

    def take(self, steps):
        net, axis, n, core = self.net, self.axes[2], self.blocks, self.net.core
        half = n // 2
        self.swaps[steps].wait_recv()
        if steps == 0:
            return
        self.add(steps, self.b.at[steps], 0, n)
        if steps == 2:
            self.onward[1] = net.send(self.view(2, 0, half, core), self.f.at[0], net.peer(axis, 1))
            self.onward[3] = net.send(self.view(2, half, half, core), self.f.at[1], net.peer(axis, 3))
        elif steps == 1:
            self.near["a"] = net.send(
                self.view(1, half, half, core), self.n.at[0, self.rows(half, half)], net.peer(axis, 1)
            )
        else:
            self.near["b"] = net.send(
                self.view(3, 0, half, core), self.n.at[1, self.rows(0, half)], net.peer(axis, 3)
            )

    def step2(self):
        net, axis, core = self.net, self.axes[2], self.net.core
        half = self.blocks // 2
        self.onward[1].wait_recv()
        self.add(1, self.f.at[0], 0, half)
        self.near["c"] = net.send(self.view(1, 0, half, core), self.n.at[0, self.rows(0, half)], net.peer(axis, 1))
        self.onward[3].wait_recv()
        self.add(3, self.f.at[1], half, half)
        self.near["d"] = net.send(
            self.view(3, half, half, core), self.n.at[1, self.rows(half, half)], net.peer(axis, 3)
        )

    def total3(self, i):
        at = self.block(i)
        own = self.g[self.tile(0, i)].astype(F32) + self.b[0, at].astype(F32)
        return own + self.n[0, at].astype(F32) + self.n[1, at].astype(F32)

    def step3(self):
        net, width, axis = self.net, self.width, self.axes[1]
        for part in "abcd":
            self.near[part].wait_recv()

        def body(i, carry):
            self.total[self.block(i), 0 : self.width] = self.total3(i)
            return carry

        lax.fori_loop(0, 10, body, 0)
        for j in range(4):
            part = self.total[40 * j : 40 * j + 40, 0:width]
            self.t2[j] = jnp.concatenate([part, jnp.zeros((8, width), F32)], axis=0).astype(BF)
        self.p = [net.send(self.t2.at[net.slot(axis, o)], self.r2.at[o - 1], net.peer(axis, o)) for o in (1, 2, 3)]

    def step4(self):
        net, width, axis = self.net, self.width, self.axes[0]
        for copy in self.p:
            copy.wait_recv()
        own = self.t2[net.at[self.axes[1]]].astype(F32)
        for o in range(3):
            own = own + self.r2[o].astype(F32)
        self.total[0:48, 0:width] = own
        for j in range(4):
            part = self.total[10 * j : 10 * j + 10, 0:width]
            self.t1[j] = jnp.concatenate([part, jnp.zeros((6, width), F32)], axis=0).astype(BF)
        self.p = [net.send(self.t1.at[net.slot(axis, o)], self.r1.at[o - 1], net.peer(axis, o)) for o in (1, 2, 3)]

    def step5(self):
        net = self.net
        swap, got, out = self.rest
        for copy in self.p:
            copy.wait_recv()
        own = self.t1[net.at[self.axes[0]]].astype(F32)
        for o in range(3):
            own = own + self.r1[o].astype(F32)
        self.total[0:16, 0 : self.width] = own
        low_rows = self.total[0:8, 0 : self.width]
        high_rows = self.total[5:13, 0 : self.width]
        first = net.core == 0
        swap[...] = jnp.where(first, high_rows, low_rows)
        out[net.core] = jnp.where(first, low_rows, high_rows)
        self.last = net.send(swap, got, net.sib)

    def step6(self):
        swap, got, out = self.rest
        self.last.wait_recv()
        out[self.net.other] = got[...]


class TileSums(RowSums):
    blocks = 16

    def __init__(self, net, width, by_core, refs):
        self.by_core = by_core
        super().__init__(net, ("z", "x", "y"), width, refs)

    def view(self, steps, at, n, which):
        slot = self.net.slot("y", steps)
        if self.by_core:
            return self.g.at[pl.ds(at, n), slot, which]
        return self.g.at[which, pl.ds(at, n), slot]

    def rows(self, at, n):
        return pl.ds(at, n)

    def tile(self, steps, i):
        slot = self.net.slot("y", steps)
        return (i, slot, self.net.core) if self.by_core else (self.net.core, i, slot)

    def block(self, i):
        return i

    def step3(self):
        net = self.net
        for part in "abcd":
            self.near[part].wait_recv()

        def body(i, carry):
            self.t2[i] = self.total3(i).astype(BF)
            return carry

        lax.fori_loop(0, 16, body, 0)
        self.p = [
            net.send(self.t2.at[pl.ds(net.slot("x", o) * 4, 4)], self.r2.at[o - 1], net.peer("x", o))
            for o in (1, 2, 3)
        ]

    def step4(self):
        net = self.net
        for copy in self.p:
            copy.wait_recv()
        for j in range(4):
            value = self.t2[net.at["x"] * 4 + j].astype(F32)
            for o in range(3):
                value = value + self.r2[o, j].astype(F32)
            self.t1[j] = value.astype(BF)
        self.p = [net.send(self.t1.at[net.slot("z", o)], self.r1.at[o - 1], net.peer("z", o)) for o in (1, 2, 3)]

    def step5(self):
        net = self.net
        for copy in self.p:
            copy.wait_recv()
        own = self.t1[net.at["z"]].astype(F32)
        for o in range(3):
            own = own + self.r1[o].astype(F32)
        if self.by_core:
            self.rest[0][...] = own
            return
        swap, got, out = self.rest
        first = net.core == 0
        swap[...] = jnp.where(first, own[8:16], own[0:8])
        out[net.core] = jnp.where(first, own[0:8], own[8:16])
        self.last = net.send(swap, got, net.sib)

    def step6(self):
        if not self.by_core:
            super().step6()


def mm(left, right):
    return jnp.dot(left, right, preferred_element_type=F32)


def mm_t(left, right):
    return lax.dot_general(left, right, (((1,), (1,)), ((), ())), preferred_element_type=F32)


def t_mm(left, right):
    return lax.dot_general(left, right, (((0,), (0,)), ((), ())), preferred_element_type=F32)


def inv_of(values):
    return lax.rsqrt(jnp.mean(values * values, axis=-1, keepdims=True) + EPSILON)


def norm_back(upstream, unit_rows, inv_rms):
    return inv_rms * (upstream - unit_rows * jnp.mean(unit_rows * upstream, axis=-1, keepdims=True))


def spin(values, cosine, sine):
    a, b = values[:, :128], values[:, 128:]
    return jnp.concatenate([a * cosine - b * sine, b * cosine + a * sine], axis=1)


def spin_back(values, cosine, sine):
    a, b = values[:, :128], values[:, 128:]
    return jnp.concatenate([a * cosine + b * sine, b * cosine - a * sine], axis=1)


def count(shape, dim):
    return lax.broadcasted_iota(jnp.int32, shape, dim)


def hot(condition):
    return jnp.where(condition, 1.0, 0.0).astype(BF)


def split_dot(value, fixed):
    high = value.astype(BF)
    low = (value - high.astype(F32)).astype(BF)
    return mm_t(high, fixed) + mm_t(low, fixed)


class Refs:
    pass


def gather_setup(net, r):
    for ref in (r.own_x1, r.own_z1, r.own_x2, r.own_z2, r.own_o):
        ref[...] = jnp.zeros_like(ref)
    q = r.q[...].astype(F32)
    r.own_x1[0, 0:5] = q[:, 0:512]
    r.own_x1[1, 0:5, 0:256] = r.k[...].astype(F32)
    r.gain_rows[...] = jnp.zeros_like(r.gain_rows)
    for i, gain in enumerate((r.n_in, r.n_mix, r.n_mid, r.n_out, r.n_q, r.n_k)):
        r.gain_rows[i : i + 1, 0 : gain.shape[1]] = gain[...].astype(F32)
    tile = t_mm(r.gain_rows[...].astype(BF), hot(count((16, 128), 0) == count((16, 128), 1)))
    r.own_x1[1, 0:5, 256:384] = tile[0:5]
    r.own_z1[0, 0:5] = q[:, 512:896]
    r.own_z1[1, 0:5, 0:128] = q[:, 896:1024]
    r.own_z1[1, 0:5, 128:384] = r.v[...].astype(F32)
    g, u = r.g[...].astype(F32), r.u[...].astype(F32)
    r.own_x2[0, 0:5] = g[:, 0:1024]
    r.own_x2[1, 0:5] = u[:, 0:1024]
    r.own_z2[0, 0:5] = g[:, 1024:2048]
    r.own_z2[1, 0:5] = u[:, 1024:2048]
    o = r.o[...].astype(F32)
    r.own_o[0, 0:8] = o[:, 0:384]
    r.own_o[1, 0:8, 0:256] = o[:, 384:640]

    def rows(name, axes, width):
        names = ("own_", "es_", "ed_", "s1_", "s2_", "b3_", "w_")
        return Rows(net, axes, width, [getattr(r, n + name) for n in names] + [r.tmp])

    x1 = rows("x1", ("y", "z", "x"), WX1)
    z1 = rows("z1", ("x", "y", "z"), WZ1)
    x2 = rows("x2", ("y", "z", "x"), WX2)
    z2 = rows("z2", ("x", "y", "z"), WZ2)
    for s in (x1, z1, x2, z2):
        s.step0()
    r.es_o[...] = r.own_o[net.other].astype(BF)
    return x1, z1, x2, z2, Tiles(net, r.w_o, False), Tiles(net, r.w_d, True)


def layer_kernel(names, *refs):
    r = Refs()
    for name, ref in zip(names, refs):
        setattr(r, name, ref)
    r.g_x2, r.g_z2, r.g_d, r.g_o = r.w_x2, r.w_z2, r.w_d, r.w_o
    for name in ("x1", "z1", "x2", "z2"):
        setattr(r, "t2_" + name, getattr(r, "s2_" + name))
        setattr(r, "t1_" + name, getattr(r, "s1_" + name))
    r.total_x2 = r.total_x1 = r.total_o = r.total_d = r.tmp
    r.g_middle = r.igrad
    net = Links(r.send_sems, r.recv_sems)
    net.greet()
    x1, z1, x2, z2, ow, dw = gather_setup(net, r)
    net.meet()
    x1.step0b()
    z1.step0b()
    swap_o = net.send(r.es_o, r.ed_o, net.sib)
    x2.step0b()
    z2.step0b()
    x1.step1()
    z1.step1()
    swap_o.wait_recv()
    mine, theirs = r.own_o[net.core][0:8], r.ed_o[...].astype(F32)[0:8]
    r.tmp[0:8, 0:WO] = jnp.where(net.core == 0, mine, theirs)
    r.tmp[8:16, 0:WO] = jnp.where(net.core == 0, theirs, mine)
    r.s1_o[...] = r.tmp[0:16, 0:WO].astype(BF)
    ow.first(r.s1_o)
    x2.step1()
    z2.step1()
    dw.first(r.d)

    k_dim, j_dim = count((D, D), 0), count((D, D), 1)
    tens = (j_dim * 52429) >> 19
    source = (tens & 3) * 160 + (tens >> 4) * 40 + ((tens >> 2) & 3) * 10 + (j_dim - 10 * tens)
    r.turn[...] = hot(k_dim == source)
    r.eye[...] = hot(k_dim == j_dim)
    spot = count((64, 64), 0)
    lens = jnp.broadcast_to(r.lens[...].astype(F32), (64, 64))
    column = jnp.sum(jnp.where(spot == count((64, 64), 1), lens, 0.0), axis=1, keepdims=True)
    ends = jnp.sum(jnp.where(spot <= count((64, 64), 1), column, 0.0), axis=0, keepdims=True)
    offset = net.me * T
    token = (count((T, 64), 0) + offset).astype(F32)
    start = jnp.max(jnp.where(ends <= token, ends, 0.0), axis=1, keepdims=True)
    position = token[:, 0:1] - start
    pair = count((1, 128), 1).astype(F32)
    angle = position * jnp.exp(pair * (-2.0 * math.log(ROPE_BASE) / HD))
    r.cosine[...] = jnp.cos(angle)
    r.sine[...] = jnp.sin(angle)
    ahead = count((T, SPAN), 1) - 2 * T
    distance = count((T, SPAN), 0) - ahead
    inside = (distance >= 0) & (distance < WINDOW) & ((ahead + offset).astype(F32) >= start)
    r.bias[...] = jnp.where(inside, 0.0, NEG_FILL)
    hidden = r.h[...].astype(F32)
    input_inv = inv_of(hidden)
    r.in_unit[...] = hidden * input_inv

    early, late = (x1, z1, ow), (x2, z2, dw)
    for s in early:
        s.step2()
    for s in late:
        s.step2()
    for s in early:
        s.step3()
    for s in early:
        s.step4()
    for s in late:
        s.step3()
    for s in early:
        s.step5()
    x1.step6()
    z1.step6()

    gain_tile = r.w_x1[1, :, 256:384]
    gain_rows = t_mm(gain_tile, r.eye[...])
    far, near = count((D, HD), 0), count((D, HD), 1)
    r.pick[...] = hot(far == 5 * (near >> 1) + (near & 1))
    head_rows = t_mm(gain_tile, r.pick[...])
    r.mults[0:4] = 1.0 + gain_rows[0:4]
    r.mults[4:6, 0:HD] = 1.0 + head_rows[4:6]
    normed = (r.in_unit[...] * r.mults[0:1]).astype(BF)
    r.normed[...] = normed
    turned = mm(normed, r.turn[...]).astype(BF)
    r.normed_t[...] = turned
    cosine, sine = r.cosine[...], r.sine[...]
    key_raw = mm(normed, r.w_x1[1, :, 0:256])
    key_inv = inv_of(key_raw)
    r.k_unit[...] = key_raw * key_inv
    r.keys[2 * T :] = spin(r.k_unit[...] * r.mults[5:6, 0:HD], cosine, sine).astype(BF)
    r.values[2 * T :] = mm(turned, r.w_z1[1, :, 128:384]).astype(BF)
    halo = []
    for steps, at in ((1, T), (2, 0)):
        for whole in (r.keys, r.values):
            halo.append(net.send(whole.at[pl.ds(2 * T, T)], whole.at[pl.ds(at, T)], net.along(steps)))
    for h in range(HEADS):
        if h < 2:
            raw = mm(normed, r.w_x1[0, :, 256 * h : 256 * h + 256])
        elif h == 2:
            raw = mm(turned, r.w_z1[0, :, 0:256])
        else:
            raw = jnp.concatenate(
                [mm(turned, r.w_z1[0, :, 256:384]), mm(turned, r.w_z1[1, :, 0:128])], axis=1
            )
        inv = inv_of(raw)
        r.q_inv[h] = inv
        r.q_unit[h] = raw * inv
        r.queries[h] = spin(raw * inv * r.mults[4:5, 0:HD], cosine, sine).astype(BF)
    for s in late:
        s.step4()
    for copy in halo:
        copy.wait_recv()

    def attend(h):
        scores = mm_t(r.queries[h], r.keys[...]) * SCALE + r.bias[...]
        row_max = jnp.max(scores, axis=1, keepdims=True)
        weights = jnp.exp(scores - row_max)
        probs = weights / jnp.sum(weights, axis=1, keepdims=True)
        r.probs[h] = probs
        r.attended[h] = mm(probs.astype(BF), r.values[...]).astype(BF)

    attend(0)
    attend(1)
    for s in late:
        s.step5()
    attend(2)
    attend(3)

    ow.step6()
    left = jnp.zeros((T, 384), F32)
    right = jnp.zeros((T, 256), F32)
    for h in range(HEADS):
        some = slice(4 * h, 4 * h + 4)
        left = left + mm(r.attended[h], r.w_o[0, some].reshape(256, WO))
        right = right + mm(r.attended[h], r.w_o[1, some].reshape(256, WO)[:, 0:256])
    mixer_out = jnp.concatenate([left, right], axis=1)
    mixer_inv = inv_of(mixer_out)
    r.mix_unit[...] = mixer_out * mixer_inv
    middle = r.h[...].astype(F32) + r.mix_unit[...] * r.mults[1:2]
    middle_inv = inv_of(middle)
    r.mid_unit[...] = middle * middle_inv
    r.middle[...] = middle
    r.mid[...] = (r.mid_unit[...] * r.mults[2:3]).astype(BF)
    r.mid_t[...] = mm(r.mid[...], r.turn[...]).astype(BF)
    for s in late:
        s.step6()

    r.acc[...] = jnp.zeros_like(r.acc)
    for w, rows_in, first in ((r.w_x2, r.mid, 0), (r.w_z2, r.mid_t, 2)):

        def forward(j, carry, w=w, rows_in=rows_in, first=first):
            cols = pl.ds(pl.multiple_of(j * 512, 512), 512)
            gate = mm(rows_in[...], w[0, :, cols])
            up = mm(rows_in[...], w[1, :, cols])
            square = gate * gate
            tanh = jnp.tanh(GELU_A * gate * (1.0 + GELU_B * square))
            active = 0.5 * gate * (1.0 + tanh)
            slope = 0.5 * (1.0 + tanh) + 0.5 * gate * (1.0 - tanh * tanh) * (
                GELU_A * (1.0 + 3.0 * GELU_B * square)
            )
            units = (active * up).astype(BF)
            part = first + j
            r.units[part] = units
            r.active[part] = active
            r.slope_up[part] = slope * up
            r.acc[...] += mm(units, r.w_d[pl.ds(part * 4, 4)].reshape(512, D))
            return carry

        lax.fori_loop(0, 2, forward, 0)
    ffn_out = r.acc[...]
    ffn_inv = inv_of(ffn_out)
    ffn_unit = ffn_out * ffn_inv
    r.mixed[...] = (r.middle[...] + ffn_unit * r.mults[3:4]).astype(BF)
    grad_out = r.og[...].astype(F32)
    r.gain_sums[...] = jnp.zeros_like(r.gain_sums)
    r.gain_sums[3:4] = jnp.sum(grad_out * ffn_unit, axis=0, keepdims=True)
    r.g_ffn[...] = norm_back(grad_out * r.mults[3:4], ffn_unit, ffn_inv).astype(BF)
    net.finish()

    def sums(kind, name, *args):
        tags = ("g_", "b_", "f_", "n_", "t2_", "r2_", "t1_", "r1_", "total_", "swap_", "got_", "out_")
        if name == "d":
            tags = tags[:9] + tags[11:]
        return kind(net, *args, [getattr(r, tag + name) for tag in tags])

    sx1 = sums(RowSums, "x1", ("y", "z", "x"), WX1)
    sz1 = sums(RowSums, "z1", ("x", "y", "z"), WZ1)
    sx2 = sums(RowSums, "x2", ("y", "z", "x"), WX2)
    sz2 = sums(RowSums, "z2", ("x", "y", "z"), WZ2)
    so = sums(TileSums, "o", WO, False)
    sd = sums(TileSums, "d", WD, True)
    wide = (sx2, sz2, sd)
    for w, g, rows_in, first, total in (
        (r.w_x2, r.g_x2, r.mid, 0, r.acc),
        (r.w_z2, r.g_z2, r.mid_t, 2, r.acc_t),
    ):
        total[...] = jnp.zeros_like(total)

        def backward(j, carry, w=w, g=g, rows_in=rows_in, first=first, total=total):
            cols = pl.ds(pl.multiple_of(j * 512, 512), 512)
            part = first + j
            some = pl.ds(part * 4, 4)
            g_ffn = r.g_ffn[...]
            grad_hidden = mm_t(g_ffn, r.w_d[some].reshape(512, D))
            r.g_d[some] = t_mm(r.units[part], g_ffn).astype(BF).reshape(4, 4, 2, 16, D)
            grad_gate = (grad_hidden * r.slope_up[part]).astype(BF)
            grad_up = (grad_hidden * r.active[part]).astype(BF)
            total[...] += mm_t(grad_gate, w[0, :, cols]) + mm_t(grad_up, w[1, :, cols])
            g[0, :, cols] = t_mm(rows_in[...], grad_gate).astype(BF)
            g[1, :, cols] = t_mm(rows_in[...], grad_up).astype(BF)
            return carry

        lax.fori_loop(0, 2, backward, 0)
        if first == 0:
            for steps in (2, 1, 3, 0):
                sx2.give(steps)
    for steps in (2, 1, 3, 0):
        sz2.give(steps)
        sd.give(steps)

    grad_in = r.acc[...] + split_dot(r.acc_t[...], r.turn[...])
    mid_unit = r.mid_unit[...]
    r.gain_sums[2:3] = jnp.sum(grad_in * mid_unit, axis=0, keepdims=True)
    grad_middle = r.og[...].astype(F32) + norm_back(grad_in * r.mults[2:3], mid_unit, inv_of(r.middle[...]))
    r.g_middle[...] = grad_middle
    mix_unit = r.mix_unit[...]
    r.gain_sums[1:2] = jnp.sum(grad_middle * mix_unit, axis=0, keepdims=True)
    grad_mixer = norm_back(grad_middle * r.mults[1:2], mix_unit, mixer_inv).astype(BF)
    for s in wide:
        s.take(2)
    for h in range(HEADS):
        some = slice(4 * h, 4 * h + 4)
        r.g_att[h] = (
            mm_t(grad_mixer[:, 0:384], r.w_o[0, some].reshape(256, WO))
            + mm_t(grad_mixer[:, 384:640], r.w_o[1, some].reshape(256, WO)[:, 0:256])
        ).astype(BF)
        grad = t_mm(r.attended[h], grad_mixer).astype(BF)
        r.g_o[0, some] = grad[:, 0:384].reshape(4, 4, 16, 384)
        r.g_o[1, some, :, :, 0:256] = grad[:, 384:640].reshape(4, 4, 16, 256)
    for steps in (2, 1, 3, 0):
        so.give(steps)
    for s in wide:
        s.take(1)

    r.d_keys[...] = jnp.zeros_like(r.d_keys)
    r.d_values[...] = jnp.zeros_like(r.d_values)
    r.q_gain[...] = jnp.zeros_like(r.q_gain)

    def attend_back(h):
        probs = r.probs[h]
        g_att = r.g_att[h]
        grad_probs = mm_t(g_att, r.values[...])
        delta = jnp.sum(probs * grad_probs, axis=1, keepdims=True)
        grad_scores = (probs * (grad_probs - delta)).astype(BF)
        grad_q = mm(grad_scores, r.keys[...]) * SCALE
        r.d_keys[...] += t_mm(grad_scores, r.queries[h])
        r.d_values[...] += t_mm(probs.astype(BF), g_att)
        back = spin_back(grad_q, r.cosine[...], r.sine[...])
        unit = r.q_unit[h]
        r.q_gain[...] += jnp.sum(back * unit, axis=0, keepdims=True)
        r.g_q[h] = norm_back(back * r.mults[4:5, 0:HD], unit, r.q_inv[h]).astype(BF)

    attend_back(0)
    for s in wide:
        s.take(3)
    so.take(2)
    attend_back(1)
    so.take(1)
    so.take(3)
    attend_back(2)
    sx2.step2()
    attend_back(3)
    back_halo = []
    for i, (whole, low) in enumerate(((r.d_keys, r.dk_low), (r.d_values, r.dv_low))):
        scale = SCALE if i == 0 else 1.0
        low[...] = (whole[0 : 2 * T] * scale).astype(BF)
        for steps, at in ((-1, T), (-2, 0)):
            back_halo.append(
                net.send(low.at[pl.ds(at, T)], r.halo_back.at[i, 0 if at else 1], net.along(steps))
            )
    sz2.step2()
    sd.step2()
    so.step2()

    normed, turned = r.normed[...], r.normed_t[...]
    for h in range(HEADS):
        if h < 2:
            r.g_x1[0, :, 256 * h : 256 * h + 256] = t_mm(normed, r.g_q[h]).astype(BF)
        elif h == 2:
            r.g_z1[0, :, 0:256] = t_mm(turned, r.g_q[h]).astype(BF)
        else:
            last = t_mm(turned, r.g_q[h]).astype(BF)
            r.g_z1[0, :, 256:384] = last[:, 0:128]
            r.g_z1[1, :, 0:128] = last[:, 128:256]
    for copy in back_halo:
        copy.wait_recv()
    own_k = r.d_keys[2 * T :] * SCALE
    own_v = r.d_values[2 * T :]
    for i in range(2):
        own_k = own_k + r.halo_back[0, i].astype(F32)
        own_v = own_v + r.halo_back[1, i].astype(F32)
    key_back = spin_back(own_k, r.cosine[...], r.sine[...])
    k_unit = r.k_unit[...]
    key_gain = jnp.sum(key_back * k_unit, axis=0, keepdims=True)
    grad_k = norm_back(key_back * r.mults[5:6, 0:HD], k_unit, key_inv).astype(BF)
    grad_v = own_v.astype(BF)
    r.g_z1[1, :, 128:384] = t_mm(turned, grad_v).astype(BF)
    for steps in (2, 1, 3, 0):
        sz1.give(steps)
    r.g_x1[1, :, 0:256] = t_mm(normed, grad_k).astype(BF)
    r.g_x1[1, :, 384:512] = jnp.zeros((D, 128), BF)
    grad_natural = (
        mm_t(r.g_q[0], r.w_x1[0, :, 0:256])
        + mm_t(r.g_q[1], r.w_x1[0, :, 256:512])
        + mm_t(grad_k, r.w_x1[1, :, 0:256])
    )
    g_last = r.g_q[3]
    grad_turned = (
        mm_t(r.g_q[2], r.w_z1[0, :, 0:256])
        + mm_t(g_last[:, 0:128], r.w_z1[0, :, 256:384])
        + mm_t(g_last[:, 128:256], r.w_z1[1, :, 0:128])
        + mm_t(grad_v, r.w_z1[1, :, 128:384])
    )
    grad_normed = grad_natural + split_dot(grad_turned, r.turn[...])
    in_unit = r.in_unit[...]
    r.gain_sums[0:1] = jnp.sum(grad_normed * in_unit, axis=0, keepdims=True)
    both = jnp.concatenate([r.q_gain[...], key_gain, jnp.zeros((6, HD), F32)], axis=0).astype(BF)
    r.gain_sums[4:6] = mm_t(both, r.pick[...])[0:2]
    r.g_x1[1, :, 256:384] = mm_t(r.eye[...], r.gain_sums[...].astype(BF)).astype(BF)
    for steps in (2, 1, 3, 0):
        sx1.give(steps)
    wide = (sx2, sz2, sd, so)
    slim = (sz1, sx1)
    for s in wide:
        s.take(0)
        s.step3()
    for steps in (2, 1, 3):
        for s in slim:
            s.take(steps)
    r.igrad[...] = r.g_middle[...] + norm_back(grad_normed * r.mults[0:1], in_unit, input_inv)
    for s in wide:
        s.step4()
    for s in slim:
        s.step2()
    for s in wide:
        s.step5()
    for s in slim:
        s.take(0)
        s.step3()
    for s in wide:
        s.step6()
    for s in slim:
        s.step4()
    for s in slim:
        s.step5()
    for s in slim:
        s.step6()
    net.finish()


def layer(*args):
    vmem = pltpu.VMEM
    ins = ("h", "q", "k", "v", "o", "g", "u", "d", *GAINS, "lens", "og")
    outs = {
        "mixed": ((T, D), BF),
        "igrad": ((T, D), F32),
        "out_x1": ((2, 8, WX1), F32),
        "out_z1": ((2, 8, WZ1), F32),
        "out_o": ((2, 8, WO), F32),
        "out_x2": ((2, 8, WX2), F32),
        "out_z2": ((2, 8, WZ2), F32),
        "out_d": ((16, WD), F32),
    }
    scratch = {}
    for name, w in (("x1", WX1), ("z1", WZ1), ("x2", WX2), ("z2", WZ2)):
        scratch |= {
            "own_" + name: ((2, 16, w), F32),
            "es_" + name: ((16, w), BF),
            "ed_" + name: ((16, w), BF),
            "s1_" + name: ((4, 16, w), BF),
            "s2_" + name: ((4, 48, w), BF),
            "b3_" + name: ((160, w), BF),
            "w_" + name: ((2, D, w), BF),
            "b_" + name: ((4, 160, w), BF),
            "f_" + name: ((2, 80, w), BF),
            "n_" + name: ((2, 160, w), BF),
            "r2_" + name: ((3, 48, w), BF),
            "r1_" + name: ((3, 16, w), BF),
            "swap_" + name: ((8, w), F32),
            "got_" + name: ((8, w), F32),
        }
    for name, w in (("o", WO), ("d", WD)):
        scratch |= {
            "b_" + name: ((4, 16, 16, w), BF),
            "f_" + name: ((2, 8, 16, w), BF),
            "n_" + name: ((2, 16, 16, w), BF),
            "t2_" + name: ((16, 16, w), BF),
            "r2_" + name: ((3, 4, 16, w), BF),
            "t1_" + name: ((4, 16, w), BF),
            "r1_" + name: ((3, 16, w), BF),
        }
    scratch |= {
        "g_x1": ((2, D, WX1), BF),
        "g_z1": ((2, D, WZ1), BF),
        "total_z2": ((160, WZ2), F32),
        "total_z1": ((160, WZ1), F32),
        "own_o": ((2, 16, WO), F32),
        "es_o": ((16, WO), BF),
        "ed_o": ((16, WO), BF),
        "s1_o": ((16, WO), BF),
        "swap_o": ((8, WO), F32),
        "got_o": ((8, WO), F32),
        "w_o": ((2, 16, 4, 16, WO), BF),
        "w_d": ((16, 4, 2, 16, WD), BF),
        "tmp": ((160, 1024), F32),
        "gain_rows": ((16, 128), F32),
        "turn": ((D, D), BF),
        "eye": ((D, D), BF),
        "pick": ((D, HD), BF),
        "cosine": ((T, 128), F32),
        "sine": ((T, 128), F32),
        "bias": ((T, SPAN), F32),
        "mults": ((8, D), F32),
        "gain_sums": ((128, D), F32),
        "in_unit": ((T, D), F32),
        "normed": ((T, D), BF),
        "normed_t": ((T, D), BF),
        "k_unit": ((T, HD), F32),
        "keys": ((SPAN, HD), BF),
        "values": ((SPAN, HD), BF),
        "queries": ((HEADS, T, HD), BF),
        "q_unit": ((HEADS, T, HD), F32),
        "q_inv": ((HEADS, T, 1), F32),
        "probs": ((HEADS, T, SPAN), F32),
        "attended": ((HEADS, T, HD), BF),
        "mix_unit": ((T, D), F32),
        "mid_unit": ((T, D), F32),
        "middle": ((T, D), F32),
        "mid": ((T, D), BF),
        "mid_t": ((T, D), BF),
        "units": ((4, T, 512), BF),
        "active": ((4, T, 512), F32),
        "slope_up": ((4, T, 512), F32),
        "acc": ((T, D), F32),
        "acc_t": ((T, D), F32),
        "g_ffn": ((T, D), BF),
        "g_att": ((HEADS, T, HD), BF),
        "g_q": ((HEADS, T, HD), BF),
        "d_keys": ((SPAN, HD), F32),
        "d_values": ((SPAN, HD), F32),
        "dk_low": ((2 * T, HD), BF),
        "dv_low": ((2 * T, HD), BF),
        "halo_back": ((2, 2, T, HD), BF),
        "q_gain": ((1, HD), F32),
    }
    inside = pl.BlockSpec(memory_space=vmem)
    names = (*ins, *outs, *scratch, "send_sems", "recv_sems")
    return pl.pallas_call(
        lambda *refs: layer_kernel(names, *refs),
        out_shape=[jax.ShapeDtypeStruct(*s) for s in outs.values()],
        in_specs=[inside] * len(ins),
        out_specs=[inside] * len(outs),
        scratch_shapes=[vmem(*s) for s in scratch.values()] + [pltpu.SemaphoreType.DMA((SEMS,))] * 2,
        compiler_params=pltpu.CompilerParams(
            collective_id=0, has_side_effects=True, vmem_limit_bytes=VMEM_CAP
        ),
        name="decoder_layer",
    )(*args)


def deliver_kernel(mixed, igrad, x1, z1, o, x2, z2, d, *outs):
    outs[0][...] = mixed[...]
    outs[1][...] = igrad[...]
    outs[2][:, 0:512] = x1[0, 0:5]
    outs[2][:, 512:896] = z1[0, 0:5]
    outs[2][:, 896:1024] = z1[1, 0:5, 0:128]
    outs[3][...] = x1[1, 0:5, 0:256]
    outs[4][...] = z1[1, 0:5, 128:384]
    outs[5][:, 0:384] = o[0]
    outs[5][:, 384:640] = o[1, :, 0:256]
    for i in range(2):
        outs[6 + i][:, 0:1024] = x2[i, 0:5]
        outs[6 + i][:, 1024:2048] = z2[i, 0:5]
    outs[8][...] = d[...]
    gains = x1[1, :, 256:384].T
    for at, row, n in ((9, 0, 5), (10, 4, 2), (11, 5, 2), (12, 1, 5), (13, 2, 5), (14, 3, 5)):
        outs[at][...] = gains[row : row + 1, 0:n].reshape(n)


def deliver(*parts):
    inside = pl.BlockSpec(memory_space=pltpu.VMEM)
    shapes = [(T, D), (5, 1024), (5, 256), (5, 256), (8, D), (5, 2048), (5, 2048), (16, D)]
    shapes += [(5,), (2,), (2,), (5,), (5,), (5,)]
    return pl.pallas_call(
        deliver_kernel,
        out_shape=[jax.ShapeDtypeStruct((T, D), BF)] + [jax.ShapeDtypeStruct(s, F32) for s in shapes],
        in_specs=[inside] * len(parts),
        out_specs=[inside] * 15,
        name="deliver",
    )(*parts)


def per_device(
    hidden_in,
    query_weight,
    key_weight,
    value_weight,
    output_weight,
    gate_weight,
    up_weight,
    down_weight,
    input_gain,
    query_gain,
    key_gain,
    mixer_gain,
    middle_gain,
    output_gain,
    seq_lengths,
    out_grad,
):
    gains = (input_gain, mixer_gain, middle_gain, output_gain, query_gain, key_gain)
    parts = layer(
        hidden_in,
        query_weight,
        key_weight,
        value_weight,
        output_weight,
        gate_weight,
        up_weight,
        down_weight,
        *[a.reshape(1, -1) for a in gains],
        seq_lengths.reshape(1, 64),
        out_grad,
    )
    return tuple(deliver(*parts))


def solution(mesh):
    return jax.shard_map(
        per_device,
        mesh=mesh,
        in_specs=(
            P("dp", None),
            P("dp", None),
            P("dp", None),
            P("dp", None),
            P("dp", None),
            P("dp", None),
            P("dp", None),
            P("dp", None),
            P("dp"),
            P("dp"),
            P("dp"),
            P("dp"),
            P("dp"),
            P("dp"),
            P(),
            P("dp", None),
        ),
        out_specs=(
            P("dp", None),
            P("dp", None),
            P("dp", None),
            P("dp", None),
            P("dp", None),
            P("dp", None),
            P("dp", None),
            P("dp", None),
            P("dp", None),
            P("dp"),
            P("dp"),
            P("dp"),
            P("dp"),
            P("dp"),
            P("dp"),
        ),
        check_vma=False,
    )
```

```python
import math

import jax
import jax.numpy as jnp
from jax import lax
from jax.experimental import pallas as pl
from jax.experimental.pallas import tpu as pltpu
from jax.sharding import PartitionSpec as P

MESH = pl.DeviceIdType.MESH
BF = jnp.bfloat16
F32 = jnp.float32
T = 256
D = 640
HD = 256
HEADS = 4
SPAN = 3 * T
WINDOW = 512
EPSILON = 1e-06
ROPE_BASE = 10000.0
NEG_FILL = -1e30
SCALE = 1.0 / math.sqrt(HD)
GELU_A = math.sqrt(2.0 / math.pi)
GELU_B = 0.044715
WX1, WZ1, WX2, WZ2, WD, WO = 512, 384, 1024, 1024, 640, 384
SEMS = 232
GAINS = ("n_in", "n_mix", "n_mid", "n_out", "n_q", "n_k")
VMEM_CAP = 62 << 20


def place(x, z, y, c):
    return ((x % 4) * 4 + (z % 4)) * 8 + (y % 4) * 2 + c


class Links:
    def __init__(self, send_sems, recv_sems):
        self.me = lax.axis_index("dp")
        self.at = {"x": self.me // 32, "z": (self.me // 8) % 4, "y": (self.me // 2) % 4}
        self.core = self.me % 2
        self.other = 1 - self.core
        self.sib = place(self.at["x"], self.at["z"], self.at["y"], self.other)
        self.xz = self.at["x"] * 4 + self.at["z"]
        self.send_sems, self.recv_sems, self.used, self.open = send_sems, recv_sems, 0, []

    def peer(self, axis, steps):
        moved = dict(self.at)
        moved[axis] = moved[axis] + steps
        return place(moved["x"], moved["z"], moved["y"], self.core)

    def along(self, steps):
        return (self.me + 128 + steps) % 128

    def slot(self, axis, steps):
        return (self.at[axis] + steps) % 4

    def greet(self):
        sem = pltpu.get_barrier_semaphore()
        partners = [self.sib] + [self.along(s) for s in (1, 2, -1, -2)]
        for axis in ("x", "z", "y"):
            partners += [self.peer(axis, o) for o in (1, 2, 3)]
        for p in partners:
            pl.semaphore_signal(sem, inc=1, device_id=(p,), device_id_type=MESH)
        self.greeted = len(partners)

    def meet(self):
        pl.semaphore_wait(pltpu.get_barrier_semaphore(), self.greeted)

    def send(self, src, dst, target):
        i = self.used
        self.used += 1
        copy = pltpu.make_async_remote_copy(
            src_ref=src,
            dst_ref=dst,
            send_sem=self.send_sems.at[i],
            recv_sem=self.recv_sems.at[i],
            device_id=(target,),
            device_id_type=MESH,
        )
        copy.start()
        self.open.append(copy.wait_send)
        return copy

    def local(self, src, dst):
        i = self.used
        self.used += 1
        copy = pltpu.make_async_copy(src, dst, self.send_sems.at[i])
        copy.start()
        return copy

    def finish(self):
        for wait in self.open:
            wait()
        self.open = []


class Rows:
    def __init__(self, net, axes, width, refs):
        self.net, self.axes, self.width = net, axes, width
        self.own, self.e_src, self.e_dst, self.s1, self.s2, self.b3, self.w, self.tmp = refs
        self.ends = []

    def view(self, slot, at, n):
        rows = pl.ds(pl.multiple_of(slot * 160 + at * 16, 16), n * 16)
        return self.w.at[self.net.core, rows]

    def step0(self):
        self.e_src[...] = self.own[self.net.other].astype(BF)

    def step0b(self):
        self.swap = self.net.send(self.e_src, self.e_dst, self.net.sib)

    def step1(self):
        net, wide = self.net, slice(0, self.width)
        self.swap.wait_recv()
        mine = self.own[net.core][0:5]
        theirs = self.e_dst[...].astype(F32)[0:5]
        first = net.core == 0
        self.tmp[0:5, wide] = jnp.where(first, mine, theirs)
        self.tmp[5:10, wide] = jnp.where(first, theirs, mine)
        slot = self.s1.at[net.at[self.axes[0]]]
        slot[...] = self.tmp[0:16, wide].astype(BF)
        self.p = [net.send(slot, slot, net.peer(self.axes[0], o)) for o in (1, 2, 3)]

    def step2(self):
        net, wide = self.net, slice(0, self.width)
        for copy in self.p:
            copy.wait_recv()
        for j in range(4):
            self.tmp[10 * j : 10 * j + 10, wide] = self.s1[j].astype(F32)[0:10]
        slot = self.s2.at[net.at[self.axes[1]]]
        slot[...] = self.tmp[0:48, wide].astype(BF)
        self.p = [net.send(slot, slot, net.peer(self.axes[1], o)) for o in (1, 2, 3)]

    def step3(self):
        net, wide = self.net, slice(0, self.width)
        for copy in self.p:
            copy.wait_recv()
        for j in range(4):
            self.tmp[40 * j : 40 * j + 40, wide] = self.s2[j].astype(F32)[0:40]
        self.b3[...] = self.tmp[0:160, wide].astype(BF)
        axis = self.axes[2]
        dst = self.view(net.at[axis], 0, 10)
        self.up = net.send(self.b3, dst, net.peer(axis, 1))
        self.down = net.send(self.b3, dst, net.peer(axis, 3))
        self.ends.append(net.send(self.b3, dst, net.sib).wait_recv)
        self.ends.append(net.local(self.b3, dst).wait)

    blocks = 10

    def step4(self):
        net, axis, n = self.net, self.axes[2], self.blocks
        half = n // 2
        self.up.wait_recv()
        part = self.view(net.slot(axis, 3), 0, half)
        self.far_up = net.send(part, part, net.peer(axis, 1))
        self.down.wait_recv()
        part = self.view(net.slot(axis, 1), half, half)
        self.far_down = net.send(part, part, net.peer(axis, 3))
        for steps in (3, 1):
            whole = self.view(net.slot(axis, steps), 0, n)
            self.ends.append(net.send(whole, whole, net.sib).wait_recv)

    def step5(self):
        net, axis, half = self.net, self.axes[2], self.blocks // 2
        for copy, at in ((self.far_up, 0), (self.far_down, half)):
            copy.wait_recv()
            part = self.view(net.slot(axis, 2), at, half)
            self.ends.append(net.send(part, part, net.sib).wait_recv)

    def step6(self):
        for wait in self.ends:
            wait()


class Tiles(Rows):
    blocks = 16

    def __init__(self, net, w, by_core):
        self.net, self.w, self.by_core, self.axes = net, w, by_core, ("z", "x", "y")
        self.ends = []

    def view(self, slot, at, n):
        if self.by_core:
            return self.w.at[pl.ds(at, n), slot, self.net.core]
        return self.w.at[self.net.core, pl.ds(at, n), slot]

    def first(self, src):
        net = self.net
        dst = self.w.at[net.xz, net.at["y"], net.core] if self.by_core else self.w.at[net.core, net.xz, net.at["y"]]
        self.p = [net.send(src, dst, net.peer("z", o)) for o in (1, 2, 3)]
        self.kept = net.local(src, dst)

    def step2(self):
        net = self.net
        for copy in self.p:
            copy.wait_recv()
        self.kept.wait()
        part = self.view(net.at["y"], net.at["x"] * 4, 4)
        self.p = [net.send(part, part, net.peer("x", o)) for o in (1, 2, 3)]

    def step3(self):
        net = self.net
        for copy in self.p:
            copy.wait_recv()
        part = self.view(net.at["y"], 0, 16)
        self.up = net.send(part, part, net.peer("y", 1))
        self.down = net.send(part, part, net.peer("y", 3))
        self.ends.append(net.send(part, part, net.sib).wait_recv)


class RowSums:
    blocks = 10

    def __init__(self, net, axes, width, refs):
        self.net, self.axes, self.width = net, axes, width
        (self.g, self.b, self.f, self.n, self.t2, self.r2, self.t1, self.r1, self.total) = refs[:9]
        self.rest = refs[9:]
        self.swaps, self.onward, self.near = {}, {}, {}

    def view(self, steps, at, n, which):
        slot = self.net.slot(self.axes[2], steps)
        rows = pl.ds(pl.multiple_of(slot * 160 + at * 16, 16), n * 16)
        return self.g.at[which, rows]

    def rows(self, at, n):
        return pl.ds(at * 16, n * 16)

    def tile(self, steps, i):
        slot = self.net.slot(self.axes[2], steps)
        return (self.net.core, pl.ds(pl.multiple_of(slot * 160 + i * 16, 16), 16))

    def block(self, i):
        return pl.ds(pl.multiple_of(i * 16, 16), 16)

    def give(self, steps):
        src = self.view(steps, 0, self.blocks, self.net.other)
        self.swaps[steps] = self.net.send(src, self.b.at[steps], self.net.sib)

    def add(self, steps, held, at, count):
        def body(i, carry):
            where = self.tile(steps, i + at)
            self.g[where] = self.g[where] + held[self.block(i)]
            return carry

        lax.fori_loop(0, count, body, 0)

    def take(self, steps):
        net, axis, n, core = self.net, self.axes[2], self.blocks, self.net.core
        half = n // 2
        self.swaps[steps].wait_recv()
        if steps == 0:
            return
        self.add(steps, self.b.at[steps], 0, n)
        if steps == 2:
            self.onward[1] = net.send(self.view(2, 0, half, core), self.f.at[0], net.peer(axis, 1))
            self.onward[3] = net.send(self.view(2, half, half, core), self.f.at[1], net.peer(axis, 3))
        elif steps == 1:
            self.near["a"] = net.send(
                self.view(1, half, half, core), self.n.at[0, self.rows(half, half)], net.peer(axis, 1)
            )
        else:
            self.near["b"] = net.send(
                self.view(3, 0, half, core), self.n.at[1, self.rows(0, half)], net.peer(axis, 3)
            )

    def step2(self):
        net, axis, core = self.net, self.axes[2], self.net.core
        half = self.blocks // 2
        self.onward[1].wait_recv()
        self.add(1, self.f.at[0], 0, half)
        self.near["c"] = net.send(self.view(1, 0, half, core), self.n.at[0, self.rows(0, half)], net.peer(axis, 1))
        self.onward[3].wait_recv()
        self.add(3, self.f.at[1], half, half)
        self.near["d"] = net.send(
            self.view(3, half, half, core), self.n.at[1, self.rows(half, half)], net.peer(axis, 3)
        )

    def total3(self, i):
        at = self.block(i)
        own = self.g[self.tile(0, i)].astype(F32) + self.b[0, at].astype(F32)
        return own + self.n[0, at].astype(F32) + self.n[1, at].astype(F32)

    def step3(self):
        net, width, axis = self.net, self.width, self.axes[1]
        for part in "abcd":
            self.near[part].wait_recv()

        def body(i, carry):
            self.total[self.block(i), 0 : self.width] = self.total3(i)
            return carry

        lax.fori_loop(0, 10, body, 0)
        for j in range(4):
            part = self.total[40 * j : 40 * j + 40, 0:width]
            self.t2[j] = jnp.concatenate([part, jnp.zeros((8, width), F32)], axis=0).astype(BF)
        self.p = [net.send(self.t2.at[net.slot(axis, o)], self.r2.at[o - 1], net.peer(axis, o)) for o in (1, 2, 3)]

    def step4(self):
        net, width, axis = self.net, self.width, self.axes[0]
        for copy in self.p:
            copy.wait_recv()
        own = self.t2[net.at[self.axes[1]]].astype(F32)
        for o in range(3):
            own = own + self.r2[o].astype(F32)
        self.total[0:48, 0:width] = own
        for j in range(4):
            part = self.total[10 * j : 10 * j + 10, 0:width]
            self.t1[j] = jnp.concatenate([part, jnp.zeros((6, width), F32)], axis=0).astype(BF)
        self.p = [net.send(self.t1.at[net.slot(axis, o)], self.r1.at[o - 1], net.peer(axis, o)) for o in (1, 2, 3)]

    def step5(self):
        net = self.net
        swap, got, out = self.rest
        for copy in self.p:
            copy.wait_recv()
        own = self.t1[net.at[self.axes[0]]].astype(F32)
        for o in range(3):
            own = own + self.r1[o].astype(F32)
        self.total[0:16, 0 : self.width] = own
        low_rows = self.total[0:8, 0 : self.width]
        high_rows = self.total[5:13, 0 : self.width]
        first = net.core == 0
        swap[...] = jnp.where(first, high_rows, low_rows)
        out[net.core] = jnp.where(first, low_rows, high_rows)
        self.last = net.send(swap, got, net.sib)

    def step6(self):
        swap, got, out = self.rest
        self.last.wait_recv()
        out[self.net.other] = got[...]


class TileSums(RowSums):
    blocks = 16

    def __init__(self, net, width, by_core, refs):
        self.by_core = by_core
        super().__init__(net, ("z", "x", "y"), width, refs)

    def view(self, steps, at, n, which):
        slot = self.net.slot("y", steps)
        if self.by_core:
            return self.g.at[pl.ds(at, n), slot, which]
        return self.g.at[which, pl.ds(at, n), slot]

    def rows(self, at, n):
        return pl.ds(at, n)

    def tile(self, steps, i):
        slot = self.net.slot("y", steps)
        return (i, slot, self.net.core) if self.by_core else (self.net.core, i, slot)

    def block(self, i):
        return i

    def step3(self):
        net = self.net
        for part in "abcd":
            self.near[part].wait_recv()

        def body(i, carry):
            self.t2[i] = self.total3(i).astype(BF)
            return carry

        lax.fori_loop(0, 16, body, 0)
        self.p = [
            net.send(self.t2.at[pl.ds(net.slot("x", o) * 4, 4)], self.r2.at[o - 1], net.peer("x", o))
            for o in (1, 2, 3)
        ]

    def step4(self):
        net = self.net
        for copy in self.p:
            copy.wait_recv()
        for j in range(4):
            value = self.t2[net.at["x"] * 4 + j].astype(F32)
            for o in range(3):
                value = value + self.r2[o, j].astype(F32)
            self.t1[j] = value.astype(BF)
        self.p = [net.send(self.t1.at[net.slot("z", o)], self.r1.at[o - 1], net.peer("z", o)) for o in (1, 2, 3)]

    def step5(self):
        net = self.net
        for copy in self.p:
            copy.wait_recv()
        own = self.t1[net.at["z"]].astype(F32)
        for o in range(3):
            own = own + self.r1[o].astype(F32)
        if self.by_core:
            self.rest[0][...] = own
            return
        swap, got, out = self.rest
        first = net.core == 0
        swap[...] = jnp.where(first, own[8:16], own[0:8])
        out[net.core] = jnp.where(first, own[0:8], own[8:16])
        self.last = net.send(swap, got, net.sib)

    def step6(self):
        if not self.by_core:
            super().step6()


def mm(left, right):
    return jnp.dot(left, right, preferred_element_type=F32)


def mm_t(left, right):
    return lax.dot_general(left, right, (((1,), (1,)), ((), ())), preferred_element_type=F32)


def t_mm(left, right):
    return lax.dot_general(left, right, (((0,), (0,)), ((), ())), preferred_element_type=F32)


def inv_of(values):
    return lax.rsqrt(jnp.mean(values * values, axis=-1, keepdims=True) + EPSILON)


def norm_back(upstream, unit_rows, inv_rms):
    return inv_rms * (upstream - unit_rows * jnp.mean(unit_rows * upstream, axis=-1, keepdims=True))


def spin(values, cosine, sine):
    a, b = values[:, :128], values[:, 128:]
    return jnp.concatenate([a * cosine - b * sine, b * cosine + a * sine], axis=1)


def spin_back(values, cosine, sine):
    a, b = values[:, :128], values[:, 128:]
    return jnp.concatenate([a * cosine + b * sine, b * cosine - a * sine], axis=1)


def count(shape, dim):
    return lax.broadcasted_iota(jnp.int32, shape, dim)


def hot(condition):
    return jnp.where(condition, 1.0, 0.0).astype(BF)


def split_dot(value, fixed):
    high = value.astype(BF)
    low = (value - high.astype(F32)).astype(BF)
    return mm_t(high, fixed) + mm_t(low, fixed)


class Refs:
    pass


def gather_setup(net, r):
    for ref in (r.own_x1, r.own_z1, r.own_x2, r.own_z2, r.own_o):
        ref[...] = jnp.zeros_like(ref)
    q = r.q[...].astype(F32)
    r.own_x1[0, 0:5] = q[:, 0:512]
    r.own_x1[1, 0:5, 0:256] = r.k[...].astype(F32)
    r.gain_rows[...] = jnp.zeros_like(r.gain_rows)
    for i, gain in enumerate((r.n_in, r.n_mix, r.n_mid, r.n_out, r.n_q, r.n_k)):
        r.gain_rows[i : i + 1, 0 : gain.shape[1]] = gain[...].astype(F32)
    tile = t_mm(r.gain_rows[...].astype(BF), hot(count((16, 128), 0) == count((16, 128), 1)))
    r.own_x1[1, 0:5, 256:384] = tile[0:5]
    r.own_z1[0, 0:5] = q[:, 512:896]
    r.own_z1[1, 0:5, 0:128] = q[:, 896:1024]
    r.own_z1[1, 0:5, 128:384] = r.v[...].astype(F32)
    g, u = r.g[...].astype(F32), r.u[...].astype(F32)
    r.own_x2[0, 0:5] = g[:, 0:1024]
    r.own_x2[1, 0:5] = u[:, 0:1024]
    r.own_z2[0, 0:5] = g[:, 1024:2048]
    r.own_z2[1, 0:5] = u[:, 1024:2048]
    o = r.o[...].astype(F32)
    r.own_o[0, 0:8] = o[:, 0:384]
    r.own_o[1, 0:8, 0:256] = o[:, 384:640]

    def rows(name, axes, width):
        names = ("own_", "es_", "ed_", "s1_", "s2_", "b3_", "w_")
        return Rows(net, axes, width, [getattr(r, n + name) for n in names] + [r.tmp])

    x1 = rows("x1", ("y", "z", "x"), WX1)
    z1 = rows("z1", ("x", "y", "z"), WZ1)
    x2 = rows("x2", ("y", "z", "x"), WX2)
    z2 = rows("z2", ("x", "y", "z"), WZ2)
    for s in (x1, z1, x2, z2):
        s.step0()
    r.es_o[...] = r.own_o[net.other].astype(BF)
    return x1, z1, x2, z2, Tiles(net, r.w_o, False), Tiles(net, r.w_d, True)


def layer_kernel(names, *refs):
    r = Refs()
    for name, ref in zip(names, refs):
        setattr(r, name, ref)
    r.g_x2, r.g_z2, r.g_d, r.g_o = r.w_x2, r.w_z2, r.w_d, r.w_o
    for name in ("x1", "z1", "x2", "z2"):
        setattr(r, "t2_" + name, getattr(r, "s2_" + name))
        setattr(r, "t1_" + name, getattr(r, "s1_" + name))
    r.total_x2 = r.total_x1 = r.total_o = r.total_d = r.tmp
    r.g_middle = r.igrad
    net = Links(r.send_sems, r.recv_sems)
    net.greet()
    x1, z1, x2, z2, ow, dw = gather_setup(net, r)
    net.meet()
    x1.step0b()
    z1.step0b()
    swap_o = net.send(r.es_o, r.ed_o, net.sib)
    x2.step0b()
    z2.step0b()
    x1.step1()
    z1.step1()
    swap_o.wait_recv()
    mine, theirs = r.own_o[net.core][0:8], r.ed_o[...].astype(F32)[0:8]
    r.tmp[0:8, 0:WO] = jnp.where(net.core == 0, mine, theirs)
    r.tmp[8:16, 0:WO] = jnp.where(net.core == 0, theirs, mine)
    r.s1_o[...] = r.tmp[0:16, 0:WO].astype(BF)
    ow.first(r.s1_o)
    x2.step1()
    z2.step1()
    dw.first(r.d)

    k_dim, j_dim = count((D, D), 0), count((D, D), 1)
    tens = (j_dim * 52429) >> 19
    source = (tens & 3) * 160 + (tens >> 4) * 40 + ((tens >> 2) & 3) * 10 + (j_dim - 10 * tens)
    r.turn[...] = hot(k_dim == source)
    r.eye[...] = hot(k_dim == j_dim)
    spot = count((64, 64), 0)
    lens = jnp.broadcast_to(r.lens[...].astype(F32), (64, 64))
    column = jnp.sum(jnp.where(spot == count((64, 64), 1), lens, 0.0), axis=1, keepdims=True)
    ends = jnp.sum(jnp.where(spot <= count((64, 64), 1), column, 0.0), axis=0, keepdims=True)
    offset = net.me * T
    token = (count((T, 64), 0) + offset).astype(F32)
    start = jnp.max(jnp.where(ends <= token, ends, 0.0), axis=1, keepdims=True)
    position = token[:, 0:1] - start
    pair = count((1, 128), 1).astype(F32)
    angle = position * jnp.exp(pair * (-2.0 * math.log(ROPE_BASE) / HD))
    r.cosine[...] = jnp.cos(angle)
    r.sine[...] = jnp.sin(angle)
    ahead = count((T, SPAN), 1) - 2 * T
    distance = count((T, SPAN), 0) - ahead
    inside = (distance >= 0) & (distance < WINDOW) & ((ahead + offset).astype(F32) >= start)
    r.bias[...] = jnp.where(inside, 0.0, NEG_FILL)
    hidden = r.h[...].astype(F32)
    input_inv = inv_of(hidden)
    r.in_unit[...] = hidden * input_inv

    early, late = (x1, z1, ow), (x2, z2, dw)
    for s in early:
        s.step2()
    for s in late:
        s.step2()
    for s in (*early, *late):
        s.step3()
    for s in (*early, *late):
        s.step4()
    for s in early:
        s.step5()
    x1.step6()
    z1.step6()

    gain_tile = r.w_x1[1, :, 256:384]
    gain_rows = t_mm(gain_tile, r.eye[...])
    far, near = count((D, HD), 0), count((D, HD), 1)
    r.pick[...] = hot(far == 5 * (near >> 1) + (near & 1))
    head_rows = t_mm(gain_tile, r.pick[...])
    r.mults[0:4] = 1.0 + gain_rows[0:4]
    r.mults[4:6, 0:HD] = 1.0 + head_rows[4:6]
    normed = (r.in_unit[...] * r.mults[0:1]).astype(BF)
    r.normed[...] = normed
    turned = mm(normed, r.turn[...]).astype(BF)
    r.normed_t[...] = turned
    cosine, sine = r.cosine[...], r.sine[...]
    key_raw = mm(normed, r.w_x1[1, :, 0:256])
    key_inv = inv_of(key_raw)
    r.k_unit[...] = key_raw * key_inv
    r.keys[2 * T :] = spin(r.k_unit[...] * r.mults[5:6, 0:HD], cosine, sine).astype(BF)
    r.values[2 * T :] = mm(turned, r.w_z1[1, :, 128:384]).astype(BF)
    halo = []
    for steps, at in ((1, T), (2, 0)):
        for whole in (r.keys, r.values):
            halo.append(net.send(whole.at[pl.ds(2 * T, T)], whole.at[pl.ds(at, T)], net.along(steps)))
    for h in range(HEADS):
        if h < 2:
            raw = mm(normed, r.w_x1[0, :, 256 * h : 256 * h + 256])
        elif h == 2:
            raw = mm(turned, r.w_z1[0, :, 0:256])
        else:
            raw = jnp.concatenate(
                [mm(turned, r.w_z1[0, :, 256:384]), mm(turned, r.w_z1[1, :, 0:128])], axis=1
            )
        inv = inv_of(raw)
        r.q_inv[h] = inv
        r.q_unit[h] = raw * inv
        r.queries[h] = spin(raw * inv * r.mults[4:5, 0:HD], cosine, sine).astype(BF)
    for s in late:
        s.step5()
    for copy in halo:
        copy.wait_recv()

    def attend(h):
        scores = mm_t(r.queries[h], r.keys[...]) * SCALE + r.bias[...]
        row_max = jnp.max(scores, axis=1, keepdims=True)
        weights = jnp.exp(scores - row_max)
        probs = weights / jnp.sum(weights, axis=1, keepdims=True)
        r.probs[h] = probs
        r.attended[h] = mm(probs.astype(BF), r.values[...]).astype(BF)

    for h in range(HEADS):
        attend(h)

    ow.step6()
    left = jnp.zeros((T, 384), F32)
    right = jnp.zeros((T, 256), F32)
    for h in range(HEADS):
        some = slice(4 * h, 4 * h + 4)
        left = left + mm(r.attended[h], r.w_o[0, some].reshape(256, WO))
        right = right + mm(r.attended[h], r.w_o[1, some].reshape(256, WO)[:, 0:256])
    mixer_out = jnp.concatenate([left, right], axis=1)
    mixer_inv = inv_of(mixer_out)
    r.mix_unit[...] = mixer_out * mixer_inv
    middle = r.h[...].astype(F32) + r.mix_unit[...] * r.mults[1:2]
    middle_inv = inv_of(middle)
    r.mid_unit[...] = middle * middle_inv
    r.middle[...] = middle
    r.mid[...] = (r.mid_unit[...] * r.mults[2:3]).astype(BF)
    r.mid_t[...] = mm(r.mid[...], r.turn[...]).astype(BF)
    for s in late:
        s.step6()

    r.acc[...] = jnp.zeros_like(r.acc)
    for w, rows_in, first in ((r.w_x2, r.mid, 0), (r.w_z2, r.mid_t, 2)):

        def forward(j, carry, w=w, rows_in=rows_in, first=first):
            cols = pl.ds(pl.multiple_of(j * 512, 512), 512)
            gate = mm(rows_in[...], w[0, :, cols])
            up = mm(rows_in[...], w[1, :, cols])
            square = gate * gate
            tanh = jnp.tanh(GELU_A * gate * (1.0 + GELU_B * square))
            active = 0.5 * gate * (1.0 + tanh)
            slope = 0.5 * (1.0 + tanh) + 0.5 * gate * (1.0 - tanh * tanh) * (
                GELU_A * (1.0 + 3.0 * GELU_B * square)
            )
            units = (active * up).astype(BF)
            part = first + j
            r.units[part] = units
            r.active[part] = active
            r.slope_up[part] = slope * up
            r.acc[...] += mm(units, r.w_d[pl.ds(part * 4, 4)].reshape(512, D))
            return carry

        lax.fori_loop(0, 2, forward, 0)
    ffn_out = r.acc[...]
    ffn_inv = inv_of(ffn_out)
    ffn_unit = ffn_out * ffn_inv
    r.mixed[...] = (r.middle[...] + ffn_unit * r.mults[3:4]).astype(BF)
    grad_out = r.og[...].astype(F32)
    r.gain_sums[...] = jnp.zeros_like(r.gain_sums)
    r.gain_sums[3:4] = jnp.sum(grad_out * ffn_unit, axis=0, keepdims=True)
    r.g_ffn[...] = norm_back(grad_out * r.mults[3:4], ffn_unit, ffn_inv).astype(BF)
    net.finish()

    def sums(kind, name, *args):
        tags = ("g_", "b_", "f_", "n_", "t2_", "r2_", "t1_", "r1_", "total_", "swap_", "got_", "out_")
        if name == "d":
            tags = tags[:9] + tags[11:]
        return kind(net, *args, [getattr(r, tag + name) for tag in tags])

    sx1 = sums(RowSums, "x1", ("y", "z", "x"), WX1)
    sz1 = sums(RowSums, "z1", ("x", "y", "z"), WZ1)
    sx2 = sums(RowSums, "x2", ("y", "z", "x"), WX2)
    sz2 = sums(RowSums, "z2", ("x", "y", "z"), WZ2)
    so = sums(TileSums, "o", WO, False)
    sd = sums(TileSums, "d", WD, True)
    wide = (sx2, sz2, sd)
    for w, g, rows_in, first, total in (
        (r.w_x2, r.g_x2, r.mid, 0, r.acc),
        (r.w_z2, r.g_z2, r.mid_t, 2, r.acc_t),
    ):
        total[...] = jnp.zeros_like(total)

        def backward(j, carry, w=w, g=g, rows_in=rows_in, first=first, total=total):
            cols = pl.ds(pl.multiple_of(j * 512, 512), 512)
            part = first + j
            some = pl.ds(part * 4, 4)
            g_ffn = r.g_ffn[...]
            grad_hidden = mm_t(g_ffn, r.w_d[some].reshape(512, D))
            r.g_d[some] = t_mm(r.units[part], g_ffn).astype(BF).reshape(4, 4, 2, 16, D)
            grad_gate = (grad_hidden * r.slope_up[part]).astype(BF)
            grad_up = (grad_hidden * r.active[part]).astype(BF)
            total[...] += mm_t(grad_gate, w[0, :, cols]) + mm_t(grad_up, w[1, :, cols])
            g[0, :, cols] = t_mm(rows_in[...], grad_gate).astype(BF)
            g[1, :, cols] = t_mm(rows_in[...], grad_up).astype(BF)
            return carry

        lax.fori_loop(0, 2, backward, 0)
        if first == 0:
            for steps in (2, 1, 3, 0):
                sx2.give(steps)
    for steps in (2, 1, 3, 0):
        sz2.give(steps)
        sd.give(steps)

    grad_in = r.acc[...] + split_dot(r.acc_t[...], r.turn[...])
    mid_unit = r.mid_unit[...]
    r.gain_sums[2:3] = jnp.sum(grad_in * mid_unit, axis=0, keepdims=True)
    grad_middle = r.og[...].astype(F32) + norm_back(grad_in * r.mults[2:3], mid_unit, inv_of(r.middle[...]))
    r.g_middle[...] = grad_middle
    mix_unit = r.mix_unit[...]
    r.gain_sums[1:2] = jnp.sum(grad_middle * mix_unit, axis=0, keepdims=True)
    grad_mixer = norm_back(grad_middle * r.mults[1:2], mix_unit, mixer_inv).astype(BF)
    for s in wide:
        s.take(2)
    for h in range(HEADS):
        some = slice(4 * h, 4 * h + 4)
        r.g_att[h] = (
            mm_t(grad_mixer[:, 0:384], r.w_o[0, some].reshape(256, WO))
            + mm_t(grad_mixer[:, 384:640], r.w_o[1, some].reshape(256, WO)[:, 0:256])
        ).astype(BF)
        grad = t_mm(r.attended[h], grad_mixer).astype(BF)
        r.g_o[0, some] = grad[:, 0:384].reshape(4, 4, 16, 384)
        r.g_o[1, some, :, :, 0:256] = grad[:, 384:640].reshape(4, 4, 16, 256)
    for steps in (2, 1, 3, 0):
        so.give(steps)
    for s in wide:
        s.take(1)

    r.d_keys[...] = jnp.zeros_like(r.d_keys)
    r.d_values[...] = jnp.zeros_like(r.d_values)
    r.q_gain[...] = jnp.zeros_like(r.q_gain)

    def attend_back(h):
        probs = r.probs[h]
        g_att = r.g_att[h]
        grad_probs = mm_t(g_att, r.values[...])
        delta = jnp.sum(probs * grad_probs, axis=1, keepdims=True)
        grad_scores = (probs * (grad_probs - delta)).astype(BF)
        grad_q = mm(grad_scores, r.keys[...]) * SCALE
        r.d_keys[...] += t_mm(grad_scores, r.queries[h])
        r.d_values[...] += t_mm(probs.astype(BF), g_att)
        back = spin_back(grad_q, r.cosine[...], r.sine[...])
        unit = r.q_unit[h]
        r.q_gain[...] += jnp.sum(back * unit, axis=0, keepdims=True)
        r.g_q[h] = norm_back(back * r.mults[4:5, 0:HD], unit, r.q_inv[h]).astype(BF)

    attend_back(0)
    for s in wide:
        s.take(3)
    for h in range(1, HEADS):
        attend_back(h)
    back_halo = []
    for i, (whole, low) in enumerate(((r.d_keys, r.dk_low), (r.d_values, r.dv_low))):
        scale = SCALE if i == 0 else 1.0
        low[...] = (whole[0 : 2 * T] * scale).astype(BF)
        for steps, at in ((-1, T), (-2, 0)):
            back_halo.append(
                net.send(low.at[pl.ds(at, T)], r.halo_back.at[i, 0 if at else 1], net.along(steps))
            )

    normed, turned = r.normed[...], r.normed_t[...]
    for h in range(HEADS):
        if h < 2:
            r.g_x1[0, :, 256 * h : 256 * h + 256] = t_mm(normed, r.g_q[h]).astype(BF)
        elif h == 2:
            r.g_z1[0, :, 0:256] = t_mm(turned, r.g_q[h]).astype(BF)
        else:
            last = t_mm(turned, r.g_q[h]).astype(BF)
            r.g_z1[0, :, 256:384] = last[:, 0:128]
            r.g_z1[1, :, 0:128] = last[:, 128:256]
    for s in wide:
        s.step2()
    for copy in back_halo:
        copy.wait_recv()
    own_k = r.d_keys[2 * T :] * SCALE
    own_v = r.d_values[2 * T :]
    for i in range(2):
        own_k = own_k + r.halo_back[0, i].astype(F32)
        own_v = own_v + r.halo_back[1, i].astype(F32)
    key_back = spin_back(own_k, r.cosine[...], r.sine[...])
    k_unit = r.k_unit[...]
    key_gain = jnp.sum(key_back * k_unit, axis=0, keepdims=True)
    grad_k = norm_back(key_back * r.mults[5:6, 0:HD], k_unit, key_inv).astype(BF)
    grad_v = own_v.astype(BF)
    r.g_z1[1, :, 128:384] = t_mm(turned, grad_v).astype(BF)
    for steps in (2, 1, 3, 0):
        sz1.give(steps)
    r.g_x1[1, :, 0:256] = t_mm(normed, grad_k).astype(BF)
    r.g_x1[1, :, 384:512] = jnp.zeros((D, 128), BF)
    grad_natural = (
        mm_t(r.g_q[0], r.w_x1[0, :, 0:256])
        + mm_t(r.g_q[1], r.w_x1[0, :, 256:512])
        + mm_t(grad_k, r.w_x1[1, :, 0:256])
    )
    g_last = r.g_q[3]
    grad_turned = (
        mm_t(r.g_q[2], r.w_z1[0, :, 0:256])
        + mm_t(g_last[:, 0:128], r.w_z1[0, :, 256:384])
        + mm_t(g_last[:, 128:256], r.w_z1[1, :, 0:128])
        + mm_t(grad_v, r.w_z1[1, :, 128:384])
    )
    grad_normed = grad_natural + split_dot(grad_turned, r.turn[...])
    in_unit = r.in_unit[...]
    r.gain_sums[0:1] = jnp.sum(grad_normed * in_unit, axis=0, keepdims=True)
    both = jnp.concatenate([r.q_gain[...], key_gain, jnp.zeros((6, HD), F32)], axis=0).astype(BF)
    r.gain_sums[4:6] = mm_t(both, r.pick[...])[0:2]
    r.g_x1[1, :, 256:384] = mm_t(r.eye[...], r.gain_sums[...].astype(BF)).astype(BF)
    for steps in (2, 1, 3, 0):
        sx1.give(steps)
    slim = (so, sz1, sx1)
    for steps in (2, 1, 3):
        for s in slim:
            s.take(steps)
    for s in wide:
        s.take(0)
        s.step3()
    r.igrad[...] = r.g_middle[...] + norm_back(grad_normed * r.mults[0:1], in_unit, input_inv)
    for s in slim:
        s.step2()
    for s in wide:
        s.step4()
    for s in slim:
        s.take(0)
        s.step3()
    for s in wide:
        s.step5()
    for s in slim:
        s.step4()
    for s in wide:
        s.step6()
    for s in slim:
        s.step5()
    for s in slim:
        s.step6()
    net.finish()


def layer(*args):
    vmem = pltpu.VMEM
    ins = ("h", "q", "k", "v", "o", "g", "u", "d", *GAINS, "lens", "og")
    outs = {
        "mixed": ((T, D), BF),
        "igrad": ((T, D), F32),
        "out_x1": ((2, 8, WX1), F32),
        "out_z1": ((2, 8, WZ1), F32),
        "out_o": ((2, 8, WO), F32),
        "out_x2": ((2, 8, WX2), F32),
        "out_z2": ((2, 8, WZ2), F32),
        "out_d": ((16, WD), F32),
    }
    scratch = {}
    for name, w in (("x1", WX1), ("z1", WZ1), ("x2", WX2), ("z2", WZ2)):
        scratch |= {
            "own_" + name: ((2, 16, w), F32),
            "es_" + name: ((16, w), BF),
            "ed_" + name: ((16, w), BF),
            "s1_" + name: ((4, 16, w), BF),
            "s2_" + name: ((4, 48, w), BF),
            "b3_" + name: ((160, w), BF),
            "w_" + name: ((2, D, w), BF),
            "b_" + name: ((4, 160, w), BF),
            "f_" + name: ((2, 80, w), BF),
            "n_" + name: ((2, 160, w), BF),
            "r2_" + name: ((3, 48, w), BF),
            "r1_" + name: ((3, 16, w), BF),
            "swap_" + name: ((8, w), F32),
            "got_" + name: ((8, w), F32),
        }
    for name, w in (("o", WO), ("d", WD)):
        scratch |= {
            "b_" + name: ((4, 16, 16, w), BF),
            "f_" + name: ((2, 8, 16, w), BF),
            "n_" + name: ((2, 16, 16, w), BF),
            "t2_" + name: ((16, 16, w), BF),
            "r2_" + name: ((3, 4, 16, w), BF),
            "t1_" + name: ((4, 16, w), BF),
            "r1_" + name: ((3, 16, w), BF),
        }
    scratch |= {
        "g_x1": ((2, D, WX1), BF),
        "g_z1": ((2, D, WZ1), BF),
        "total_z2": ((160, WZ2), F32),
        "total_z1": ((160, WZ1), F32),
        "own_o": ((2, 16, WO), F32),
        "es_o": ((16, WO), BF),
        "ed_o": ((16, WO), BF),
        "s1_o": ((16, WO), BF),
        "swap_o": ((8, WO), F32),
        "got_o": ((8, WO), F32),
        "w_o": ((2, 16, 4, 16, WO), BF),
        "w_d": ((16, 4, 2, 16, WD), BF),
        "tmp": ((160, 1024), F32),
        "gain_rows": ((16, 128), F32),
        "turn": ((D, D), BF),
        "eye": ((D, D), BF),
        "pick": ((D, HD), BF),
        "cosine": ((T, 128), F32),
        "sine": ((T, 128), F32),
        "bias": ((T, SPAN), F32),
        "mults": ((8, D), F32),
        "gain_sums": ((128, D), F32),
        "in_unit": ((T, D), F32),
        "normed": ((T, D), BF),
        "normed_t": ((T, D), BF),
        "k_unit": ((T, HD), F32),
        "keys": ((SPAN, HD), BF),
        "values": ((SPAN, HD), BF),
        "queries": ((HEADS, T, HD), BF),
        "q_unit": ((HEADS, T, HD), F32),
        "q_inv": ((HEADS, T, 1), F32),
        "probs": ((HEADS, T, SPAN), F32),
        "attended": ((HEADS, T, HD), BF),
        "mix_unit": ((T, D), F32),
        "mid_unit": ((T, D), F32),
        "middle": ((T, D), F32),
        "mid": ((T, D), BF),
        "mid_t": ((T, D), BF),
        "units": ((4, T, 512), BF),
        "active": ((4, T, 512), F32),
        "slope_up": ((4, T, 512), F32),
        "acc": ((T, D), F32),
        "acc_t": ((T, D), F32),
        "g_ffn": ((T, D), BF),
        "g_att": ((HEADS, T, HD), BF),
        "g_q": ((HEADS, T, HD), BF),
        "d_keys": ((SPAN, HD), F32),
        "d_values": ((SPAN, HD), F32),
        "dk_low": ((2 * T, HD), BF),
        "dv_low": ((2 * T, HD), BF),
        "halo_back": ((2, 2, T, HD), BF),
        "q_gain": ((1, HD), F32),
    }
    inside = pl.BlockSpec(memory_space=vmem)
    names = (*ins, *outs, *scratch, "send_sems", "recv_sems")
    return pl.pallas_call(
        lambda *refs: layer_kernel(names, *refs),
        out_shape=[jax.ShapeDtypeStruct(*s) for s in outs.values()],
        in_specs=[inside] * len(ins),
        out_specs=[inside] * len(outs),
        scratch_shapes=[vmem(*s) for s in scratch.values()] + [pltpu.SemaphoreType.DMA((SEMS,))] * 2,
        compiler_params=pltpu.CompilerParams(
            collective_id=0, has_side_effects=True, vmem_limit_bytes=VMEM_CAP
        ),
        name="decoder_layer",
    )(*args)


def deliver_kernel(mixed, igrad, x1, z1, o, x2, z2, d, *outs):
    outs[0][...] = mixed[...]
    outs[1][...] = igrad[...]
    outs[2][:, 0:512] = x1[0, 0:5]
    outs[2][:, 512:896] = z1[0, 0:5]
    outs[2][:, 896:1024] = z1[1, 0:5, 0:128]
    outs[3][...] = x1[1, 0:5, 0:256]
    outs[4][...] = z1[1, 0:5, 128:384]
    outs[5][:, 0:384] = o[0]
    outs[5][:, 384:640] = o[1, :, 0:256]
    for i in range(2):
        outs[6 + i][:, 0:1024] = x2[i, 0:5]
        outs[6 + i][:, 1024:2048] = z2[i, 0:5]
    outs[8][...] = d[...]
    gains = x1[1, :, 256:384].T
    for at, row, n in ((9, 0, 5), (10, 4, 2), (11, 5, 2), (12, 1, 5), (13, 2, 5), (14, 3, 5)):
        outs[at][...] = gains[row : row + 1, 0:n].reshape(n)


def deliver(*parts):
    inside = pl.BlockSpec(memory_space=pltpu.VMEM)
    shapes = [(T, D), (5, 1024), (5, 256), (5, 256), (8, D), (5, 2048), (5, 2048), (16, D)]
    shapes += [(5,), (2,), (2,), (5,), (5,), (5,)]
    return pl.pallas_call(
        deliver_kernel,
        out_shape=[jax.ShapeDtypeStruct((T, D), BF)] + [jax.ShapeDtypeStruct(s, F32) for s in shapes],
        in_specs=[inside] * len(parts),
        out_specs=[inside] * 15,
        name="deliver",
    )(*parts)


def per_device(
    hidden_in,
    query_weight,
    key_weight,
    value_weight,
    output_weight,
    gate_weight,
    up_weight,
    down_weight,
    input_gain,
    query_gain,
    key_gain,
    mixer_gain,
    middle_gain,
    output_gain,
    seq_lengths,
    out_grad,
):
    gains = (input_gain, mixer_gain, middle_gain, output_gain, query_gain, key_gain)
    parts = layer(
        hidden_in,
        query_weight,
        key_weight,
        value_weight,
        output_weight,
        gate_weight,
        up_weight,
        down_weight,
        *[a.reshape(1, -1) for a in gains],
        seq_lengths.reshape(1, 64),
        out_grad,
    )
    return tuple(deliver(*parts))


def solution(mesh):
    return jax.shard_map(
        per_device,
        mesh=mesh,
        in_specs=(
            P("dp", None),
            P("dp", None),
            P("dp", None),
            P("dp", None),
            P("dp", None),
            P("dp", None),
            P("dp", None),
            P("dp", None),
            P("dp"),
            P("dp"),
            P("dp"),
            P("dp"),
            P("dp"),
            P("dp"),
            P(),
            P("dp", None),
        ),
        out_specs=(
            P("dp", None),
            P("dp", None),
            P("dp", None),
            P("dp", None),
            P("dp", None),
            P("dp", None),
            P("dp", None),
            P("dp", None),
            P("dp", None),
            P("dp"),
            P("dp"),
            P("dp"),
            P("dp"),
            P("dp"),
            P("dp"),
        ),
        check_vma=False,
    )
```

```python
import math

import jax
import jax.numpy as jnp
from jax import lax
from jax.experimental import pallas as pl
from jax.experimental.pallas import tpu as pltpu
from jax.sharding import PartitionSpec as P

MESH = pl.DeviceIdType.MESH
BF = jnp.bfloat16
F32 = jnp.float32
T = 256
D = 640
HD = 256
HEADS = 4
SPAN = 3 * T
WINDOW = 512
EPSILON = 1e-06
ROPE_BASE = 10000.0
NEG_FILL = -1e30
SCALE = 1.0 / math.sqrt(HD)
GELU_A = math.sqrt(2.0 / math.pi)
GELU_B = 0.044715
WX1, WZ1, WX2, WZ2, WD, WO = 512, 384, 1024, 1024, 640, 384
SEMS = 232
GAINS = ("n_in", "n_mix", "n_mid", "n_out", "n_q", "n_k")
VMEM_CAP = 62 << 20


def place(x, z, y, c):
    return ((x % 4) * 4 + (z % 4)) * 8 + (y % 4) * 2 + c


class Links:
    def __init__(self, send_sems, recv_sems):
        self.me = lax.axis_index("dp")
        self.at = {"x": self.me // 32, "z": (self.me // 8) % 4, "y": (self.me // 2) % 4}
        self.core = self.me % 2
        self.other = 1 - self.core
        self.sib = place(self.at["x"], self.at["z"], self.at["y"], self.other)
        self.xz = self.at["x"] * 4 + self.at["z"]
        self.send_sems, self.recv_sems, self.used, self.open = send_sems, recv_sems, 0, []

    def peer(self, axis, steps):
        moved = dict(self.at)
        moved[axis] = moved[axis] + steps
        return place(moved["x"], moved["z"], moved["y"], self.core)

    def along(self, steps):
        return (self.me + 128 + steps) % 128

    def slot(self, axis, steps):
        return (self.at[axis] + steps) % 4

    def greet(self):
        sem = pltpu.get_barrier_semaphore()
        partners = [self.sib] + [self.along(s) for s in (2, -2)]
        for axis in ("x", "z", "y"):
            partners += [self.peer(axis, o) for o in (1, 2, 3)]
        for p in partners:
            pl.semaphore_signal(sem, inc=1, device_id=(p,), device_id_type=MESH)
        self.greeted = len(partners)

    def meet(self):
        pl.semaphore_wait(pltpu.get_barrier_semaphore(), self.greeted)

    def send(self, src, dst, target):
        i = self.used
        self.used += 1
        copy = pltpu.make_async_remote_copy(
            src_ref=src,
            dst_ref=dst,
            send_sem=self.send_sems.at[i],
            recv_sem=self.recv_sems.at[i],
            device_id=(target,),
            device_id_type=MESH,
        )
        copy.start()
        self.open.append(copy.wait_send)
        return copy

    def local(self, src, dst):
        i = self.used
        self.used += 1
        copy = pltpu.make_async_copy(src, dst, self.send_sems.at[i])
        copy.start()
        return copy

    def finish(self):
        for wait in self.open:
            wait()
        self.open = []


class Rows:
    def __init__(self, net, axes, width, refs):
        self.net, self.axes, self.width = net, axes, width
        self.own, self.e_src, self.e_dst, self.s1, self.s2, self.b3, self.w, self.tmp = refs
        self.ends = []

    def view(self, slot, at, n):
        rows = pl.ds(pl.multiple_of(slot * 160 + at * 16, 16), n * 16)
        return self.w.at[self.net.core, rows]

    def step0(self):
        self.e_src[...] = self.own[self.net.other].astype(BF)

    def step0b(self):
        self.swap = self.net.send(self.e_src, self.e_dst, self.net.sib)

    def step1(self):
        net, wide = self.net, slice(0, self.width)
        self.swap.wait_recv()
        mine = self.own[net.core][0:5]
        theirs = self.e_dst[...].astype(F32)[0:5]
        first = net.core == 0
        self.tmp[0:5, wide] = jnp.where(first, mine, theirs)
        self.tmp[5:10, wide] = jnp.where(first, theirs, mine)
        slot = self.s1.at[net.at[self.axes[0]]]
        slot[...] = self.tmp[0:16, wide].astype(BF)
        self.p = [net.send(slot, slot, net.peer(self.axes[0], o)) for o in (1, 2, 3)]

    def step2(self):
        net, wide = self.net, slice(0, self.width)
        for copy in self.p:
            copy.wait_recv()
        for j in range(4):
            self.tmp[10 * j : 10 * j + 10, wide] = self.s1[j].astype(F32)[0:10]
        slot = self.s2.at[net.at[self.axes[1]]]
        slot[...] = self.tmp[0:48, wide].astype(BF)
        self.p = [net.send(slot, slot, net.peer(self.axes[1], o)) for o in (1, 2, 3)]

    def step3(self):
        net, wide = self.net, slice(0, self.width)
        for copy in self.p:
            copy.wait_recv()
        for j in range(4):
            self.tmp[40 * j : 40 * j + 40, wide] = self.s2[j].astype(F32)[0:40]
        self.b3[...] = self.tmp[0:160, wide].astype(BF)
        axis = self.axes[2]
        dst = self.view(net.at[axis], 0, 10)
        self.up = net.send(self.b3, dst, net.peer(axis, 1))
        self.down = net.send(self.b3, dst, net.peer(axis, 3))
        self.ends.append(net.send(self.b3, dst, net.sib).wait_recv)
        self.ends.append(net.local(self.b3, dst).wait)

    blocks = 10

    def step4(self):
        net, axis, n = self.net, self.axes[2], self.blocks
        half = n // 2
        self.up.wait_recv()
        part = self.view(net.slot(axis, 3), 0, half)
        self.far_up = net.send(part, part, net.peer(axis, 1))
        self.down.wait_recv()
        part = self.view(net.slot(axis, 1), half, half)
        self.far_down = net.send(part, part, net.peer(axis, 3))
        for steps in (3, 1):
            whole = self.view(net.slot(axis, steps), 0, n)
            self.ends.append(net.send(whole, whole, net.sib).wait_recv)

    def step5(self):
        net, axis, half = self.net, self.axes[2], self.blocks // 2
        for copy, at in ((self.far_up, 0), (self.far_down, half)):
            copy.wait_recv()
            part = self.view(net.slot(axis, 2), at, half)
            self.ends.append(net.send(part, part, net.sib).wait_recv)

    def step6(self):
        for wait in self.ends:
            wait()


class Tiles(Rows):
    blocks = 16

    def __init__(self, net, axes, w, by_core):
        self.net, self.axes, self.w, self.by_core = net, axes, w, by_core
        self.ends = []

    def view(self, slot, at, n):
        if self.by_core:
            return self.w.at[pl.ds(at, n), slot, self.net.core]
        return self.w.at[self.net.core, slot, pl.ds(at, n)]

    def first(self, src):
        net = self.net
        a, b, c = (net.at[axis] for axis in self.axes)
        dst = self.w.at[b * 4 + a, c, net.core] if self.by_core else self.w.at[net.core, c, b * 4 + a]
        self.p = [net.send(src, dst, net.peer(self.axes[0], o)) for o in (1, 2, 3)]
        self.kept = net.local(src, dst)

    def step2(self):
        net = self.net
        for copy in self.p:
            copy.wait_recv()
        self.kept.wait()
        part = self.view(net.at[self.axes[2]], net.at[self.axes[1]] * 4, 4)
        self.p = [net.send(part, part, net.peer(self.axes[1], o)) for o in (1, 2, 3)]

    def step3(self):
        net, axis = self.net, self.axes[2]
        for copy in self.p:
            copy.wait_recv()
        part = self.view(net.at[axis], 0, 16)
        self.up = net.send(part, part, net.peer(axis, 1))
        self.down = net.send(part, part, net.peer(axis, 3))
        self.ends.append(net.send(part, part, net.sib).wait_recv)


class RowSums:
    blocks = 10

    def __init__(self, net, axes, width, refs):
        self.net, self.axes, self.width = net, axes, width
        (self.g, self.b, self.f, self.n, self.t2, self.r2, self.t1, self.r1, self.total) = refs[:9]
        self.rest = refs[9:]
        self.swaps, self.onward, self.near = {}, {}, {}

    def view(self, steps, at, n, which):
        slot = self.net.slot(self.axes[2], steps)
        rows = pl.ds(pl.multiple_of(slot * 160 + at * 16, 16), n * 16)
        return self.g.at[which, rows]

    def rows(self, at, n):
        return pl.ds(at * 16, n * 16)

    def tile(self, steps, i):
        slot = self.net.slot(self.axes[2], steps)
        return (self.net.core, pl.ds(pl.multiple_of(slot * 160 + i * 16, 16), 16))

    def block(self, i):
        return pl.ds(pl.multiple_of(i * 16, 16), 16)

    def give(self, steps):
        src = self.view(steps, 0, self.blocks, self.net.other)
        self.swaps[steps] = self.net.send(src, self.b.at[steps], self.net.sib)

    def add(self, steps, held, at, count):
        def body(i, carry):
            where = self.tile(steps, i + at)
            self.g[where] = self.g[where] + held[self.block(i)]
            return carry

        lax.fori_loop(0, count, body, 0)

    def take(self, steps):
        net, axis, n, core = self.net, self.axes[2], self.blocks, self.net.core
        half = n // 2
        self.swaps[steps].wait_recv()
        if steps == 0:
            return
        self.add(steps, self.b.at[steps], 0, n)
        if steps == 2:
            self.onward[1] = net.send(self.view(2, 0, half, core), self.f.at[0], net.peer(axis, 1))
            self.onward[3] = net.send(self.view(2, half, half, core), self.f.at[1], net.peer(axis, 3))
        elif steps == 1:
            self.near["a"] = net.send(
                self.view(1, half, half, core), self.n.at[0, self.rows(half, half)], net.peer(axis, 1)
            )
        else:
            self.near["b"] = net.send(
                self.view(3, 0, half, core), self.n.at[1, self.rows(0, half)], net.peer(axis, 3)
            )

    def step2(self):
        net, axis, core = self.net, self.axes[2], self.net.core
        half = self.blocks // 2
        self.onward[1].wait_recv()
        self.add(1, self.f.at[0], 0, half)
        self.near["c"] = net.send(self.view(1, 0, half, core), self.n.at[0, self.rows(0, half)], net.peer(axis, 1))
        self.onward[3].wait_recv()
        self.add(3, self.f.at[1], half, half)
        self.near["d"] = net.send(
            self.view(3, half, half, core), self.n.at[1, self.rows(half, half)], net.peer(axis, 3)
        )

    def total3(self, i):
        at = self.block(i)
        own = self.g[self.tile(0, i)].astype(F32) + self.b[0, at].astype(F32)
        return own + self.n[0, at].astype(F32) + self.n[1, at].astype(F32)

    def step3(self):
        net, width, axis = self.net, self.width, self.axes[1]
        for part in "abcd":
            self.near[part].wait_recv()

        def body(i, carry):
            self.total[self.block(i), 0 : self.width] = self.total3(i)
            return carry

        lax.fori_loop(0, 10, body, 0)
        for j in range(4):
            part = self.total[40 * j : 40 * j + 40, 0:width]
            self.t2[j] = jnp.concatenate([part, jnp.zeros((8, width), F32)], axis=0).astype(BF)
        self.p = [net.send(self.t2.at[net.slot(axis, o)], self.r2.at[o - 1], net.peer(axis, o)) for o in (1, 2, 3)]

    def step4(self):
        net, width, axis = self.net, self.width, self.axes[0]
        for copy in self.p:
            copy.wait_recv()
        own = self.t2[net.at[self.axes[1]]].astype(F32)
        for o in range(3):
            own = own + self.r2[o].astype(F32)
        self.total[0:48, 0:width] = own
        for j in range(4):
            part = self.total[10 * j : 10 * j + 10, 0:width]
            self.t1[j] = jnp.concatenate([part, jnp.zeros((6, width), F32)], axis=0).astype(BF)
        self.p = [net.send(self.t1.at[net.slot(axis, o)], self.r1.at[o - 1], net.peer(axis, o)) for o in (1, 2, 3)]

    def step5(self):
        net = self.net
        swap, got, out = self.rest
        for copy in self.p:
            copy.wait_recv()
        own = self.t1[net.at[self.axes[0]]].astype(F32)
        for o in range(3):
            own = own + self.r1[o].astype(F32)
        self.total[0:16, 0 : self.width] = own
        low_rows = self.total[0:8, 0 : self.width]
        high_rows = self.total[5:13, 0 : self.width]
        first = net.core == 0
        swap[...] = jnp.where(first, high_rows, low_rows)
        out[net.core] = jnp.where(first, low_rows, high_rows)
        self.last = net.send(swap, got, net.sib)

    def step6(self):
        swap, got, out = self.rest
        self.last.wait_recv()
        out[self.net.other] = got[...]


class TileSums(RowSums):
    blocks = 16

    def __init__(self, net, axes, width, by_core, refs):
        self.by_core = by_core
        super().__init__(net, axes, width, refs)

    def view(self, steps, at, n, which):
        slot = self.net.slot(self.axes[2], steps)
        if self.by_core:
            return self.g.at[pl.ds(at, n), slot, which]
        return self.g.at[which, slot, pl.ds(at, n)]

    def rows(self, at, n):
        return pl.ds(at, n)

    def tile(self, steps, i):
        slot = self.net.slot(self.axes[2], steps)
        return (i, slot, self.net.core) if self.by_core else (self.net.core, slot, i)

    def block(self, i):
        return i

    def step3(self):
        net = self.net
        for part in "abcd":
            self.near[part].wait_recv()

        def body(i, carry):
            self.t2[i] = self.total3(i).astype(BF)
            return carry

        lax.fori_loop(0, 16, body, 0)
        self.p = [
            net.send(
                self.t2.at[pl.ds(net.slot(self.axes[1], o) * 4, 4)], self.r2.at[o - 1], net.peer(self.axes[1], o)
            )
            for o in (1, 2, 3)
        ]

    def step4(self):
        net = self.net
        for copy in self.p:
            copy.wait_recv()
        for j in range(4):
            value = self.t2[net.at[self.axes[1]] * 4 + j].astype(F32)
            for o in range(3):
                value = value + self.r2[o, j].astype(F32)
            self.t1[j] = value.astype(BF)
        axis = self.axes[0]
        self.p = [net.send(self.t1.at[net.slot(axis, o)], self.r1.at[o - 1], net.peer(axis, o)) for o in (1, 2, 3)]

    def step5(self):
        net = self.net
        for copy in self.p:
            copy.wait_recv()
        own = self.t1[net.at[self.axes[0]]].astype(F32)
        for o in range(3):
            own = own + self.r1[o].astype(F32)
        if self.by_core:
            self.rest[0][...] = own
            return
        swap, got, out = self.rest
        first = net.core == 0
        swap[...] = jnp.where(first, own[8:16], own[0:8])
        out[net.core] = jnp.where(first, own[0:8], own[8:16])
        self.last = net.send(swap, got, net.sib)

    def step6(self):
        if not self.by_core:
            super().step6()


def mm(left, right):
    return jnp.dot(left, right, preferred_element_type=F32)


def mm_t(left, right):
    return lax.dot_general(left, right, (((1,), (1,)), ((), ())), preferred_element_type=F32)


def t_mm(left, right):
    return lax.dot_general(left, right, (((0,), (0,)), ((), ())), preferred_element_type=F32)


def inv_of(values):
    return lax.rsqrt(jnp.mean(values * values, axis=-1, keepdims=True) + EPSILON)


def norm_back(upstream, unit_rows, inv_rms):
    return inv_rms * (upstream - unit_rows * jnp.mean(unit_rows * upstream, axis=-1, keepdims=True))


def spin(values, cosine, sine):
    a, b = values[:, :128], values[:, 128:]
    return jnp.concatenate([a * cosine - b * sine, b * cosine + a * sine], axis=1)


def spin_back(values, cosine, sine):
    a, b = values[:, :128], values[:, 128:]
    return jnp.concatenate([a * cosine + b * sine, b * cosine - a * sine], axis=1)


def count(shape, dim):
    return lax.broadcasted_iota(jnp.int32, shape, dim)


def hot(condition):
    return jnp.where(condition, 1.0, 0.0).astype(BF)


def split_dot(value, fixed):
    high = value.astype(BF)
    low = (value - high.astype(F32)).astype(BF)
    return mm_t(high, fixed) + mm_t(low, fixed)


class Refs:
    pass


def gather_setup(net, r):
    for ref in (r.own_x1, r.own_z1, r.own_x2, r.own_z2, r.own_o):
        ref[...] = jnp.zeros_like(ref)
    q = r.q[...].astype(F32)
    r.own_x1[0, 0:5] = q[:, 0:512]
    r.own_x1[1, 0:5, 0:256] = r.k[...].astype(F32)
    r.gain_rows[...] = jnp.zeros_like(r.gain_rows)
    for i, gain in enumerate((r.n_in, r.n_mix, r.n_mid, r.n_out, r.n_q, r.n_k)):
        r.gain_rows[i : i + 1, 0 : gain.shape[1]] = gain[...].astype(F32)
    tile = t_mm(r.gain_rows[...].astype(BF), hot(count((16, 128), 0) == count((16, 128), 1)))
    r.own_x1[1, 0:5, 256:384] = tile[0:5]
    r.own_z1[0, 0:5] = q[:, 512:896]
    r.own_z1[1, 0:5, 0:128] = q[:, 896:1024]
    r.own_z1[1, 0:5, 128:384] = r.v[...].astype(F32)
    g, u = r.g[...].astype(F32), r.u[...].astype(F32)
    r.own_x2[0, 0:5] = g[:, 0:1024]
    r.own_x2[1, 0:5] = u[:, 0:1024]
    r.own_z2[0, 0:5] = g[:, 1024:2048]
    r.own_z2[1, 0:5] = u[:, 1024:2048]
    o = r.o[...].astype(F32)
    r.own_o[0, 0:8] = o[:, 0:384]
    r.own_o[1, 0:8, 0:256] = o[:, 384:640]

    def rows(name, axes, width):
        names = ("own_", "es_", "ed_", "s1_", "s2_", "b3_", "w_")
        return Rows(net, axes, width, [getattr(r, n + name) for n in names] + [r.tmp])

    x1 = rows("x1", ("y", "z", "x"), WX1)
    z1 = rows("z1", ("x", "y", "z"), WZ1)
    x2 = rows("x2", ("y", "z", "x"), WX2)
    z2 = rows("z2", ("x", "y", "z"), WZ2)
    for s in (x1, z1, x2, z2):
        s.step0()
    r.es_o[...] = r.own_o[net.other].astype(BF)
    return x1, z1, x2, z2, Tiles(net, ("y", "x", "z"), r.w_o, False), Tiles(net, ("z", "x", "y"), r.w_d, True)


def layer_kernel(names, *refs):
    r = Refs()
    for name, ref in zip(names, refs):
        setattr(r, name, ref)
    r.g_x2, r.g_z2, r.g_d, r.g_o = r.w_x2, r.w_z2, r.w_d, r.w_o
    for name in ("x1", "z1", "x2", "z2"):
        setattr(r, "t2_" + name, getattr(r, "s2_" + name))
        setattr(r, "t1_" + name, getattr(r, "s1_" + name))
    r.total_x2 = r.total_x1 = r.total_o = r.total_d = r.tmp
    r.g_middle = r.igrad
    net = Links(r.send_sems, r.recv_sems)
    net.greet()
    x1, z1, x2, z2, ow, dw = gather_setup(net, r)
    r.rows_in[0] = r.h[...]
    net.meet()
    x1.step0b()
    z1.step0b()
    swap_o = net.send(r.es_o, r.ed_o, net.sib)
    x2.step0b()
    z2.step0b()
    ahead_copy = net.send(r.rows_in.at[0], r.rows_in.at[1], net.along(2))
    x1.step1()
    z1.step1()
    swap_o.wait_recv()
    mine, theirs = r.own_o[net.core][0:8], r.ed_o[...].astype(F32)[0:8]
    r.tmp[0:8, 0:WO] = jnp.where(net.core == 0, mine, theirs)
    r.tmp[8:16, 0:WO] = jnp.where(net.core == 0, theirs, mine)
    r.s1_o[...] = r.tmp[0:16, 0:WO].astype(BF)
    ow.first(r.s1_o)
    x2.step1()
    z2.step1()
    dw.first(r.d)

    k_dim, j_dim = count((D, D), 0), count((D, D), 1)
    tens = (j_dim * 52429) >> 19
    source = (tens & 3) * 160 + (tens >> 4) * 40 + ((tens >> 2) & 3) * 10 + (j_dim - 10 * tens)
    r.turn[...] = hot(k_dim == source)
    r.eye[...] = hot(k_dim == j_dim)
    spot = count((64, 64), 0)
    lens = jnp.broadcast_to(r.lens[...].astype(F32), (64, 64))
    column = jnp.sum(jnp.where(spot == count((64, 64), 1), lens, 0.0), axis=1, keepdims=True)
    ends = jnp.sum(jnp.where(spot <= count((64, 64), 1), column, 0.0), axis=0, keepdims=True)
    offset = net.me * T
    token = (count((SPAN, 64), 0) + (offset - 2 * T)).astype(F32)
    start = jnp.max(jnp.where(ends <= token, ends, 0.0), axis=1, keepdims=True)
    position = token[:, 0:1] - start
    pair = count((1, 128), 1).astype(F32)
    angle = position * jnp.exp(pair * (-2.0 * math.log(ROPE_BASE) / HD))
    r.cosine[...] = jnp.cos(angle)
    r.sine[...] = jnp.sin(angle)
    ahead = count((T, SPAN), 1) - 2 * T
    distance = count((T, SPAN), 0) - ahead
    inside = (distance >= 0) & (distance < WINDOW) & ((ahead + offset).astype(F32) >= start[2 * T :])
    r.bias[...] = jnp.where(inside, 0.0, NEG_FILL)
    hidden = r.h[...].astype(F32)
    input_inv = inv_of(hidden)
    r.in_unit[...] = hidden * input_inv

    early, late = (x1, z1, ow), (x2, z2, dw)
    for s in early:
        s.step2()
    for s in late:
        s.step2()
    ahead_copy.wait_recv()
    side_copy = net.send(r.rows_in.at[net.core], r.rows_side, net.sib)
    for s in (*early, *late):
        s.step3()
    for s in (*early, *late):
        s.step4()
    for s in early:
        s.step5()
    x1.step6()
    z1.step6()

    gain_tile = r.w_x1[1, :, 256:384]
    gain_rows = t_mm(gain_tile, r.eye[...])
    far, near = count((D, HD), 0), count((D, HD), 1)
    r.pick[...] = hot(far == 5 * (near >> 1) + (near & 1))
    head_rows = t_mm(gain_tile, r.pick[...])
    r.mults[0:4] = 1.0 + gain_rows[0:4]
    r.mults[4:6, 0:HD] = 1.0 + head_rows[4:6]
    normed = (r.in_unit[...] * r.mults[0:1]).astype(BF)
    r.normed[...] = normed
    turned = mm(normed, r.turn[...]).astype(BF)
    r.normed_t[...] = turned
    cosine, sine = r.cosine[2 * T :], r.sine[2 * T :]
    side_copy.wait_recv()
    for i in range(3):
        some = slice(T * i, T * i + T)
        if i < 2:
            rows = (r.rows_in[1] if i == 0 else r.rows_side[...]).astype(F32)
            here = (rows * inv_of(rows) * r.mults[0:1]).astype(BF)
            there = mm(here, r.turn[...]).astype(BF)
        else:
            here, there = normed, turned
        key_raw = mm(here, r.w_x1[1, :, 0:256])
        key_inv = inv_of(key_raw)
        key_unit = key_raw * key_inv
        r.keys[some] = spin(key_unit * r.mults[5:6, 0:HD], r.cosine[some], r.sine[some]).astype(BF)
        r.values[some] = mm(there, r.w_z1[1, :, 128:384]).astype(BF)
    r.k_unit[...] = key_unit
    for h in range(HEADS):
        if h < 2:
            raw = mm(normed, r.w_x1[0, :, 256 * h : 256 * h + 256])
        elif h == 2:
            raw = mm(turned, r.w_z1[0, :, 0:256])
        else:
            raw = jnp.concatenate(
                [mm(turned, r.w_z1[0, :, 256:384]), mm(turned, r.w_z1[1, :, 0:128])], axis=1
            )
        inv = inv_of(raw)
        r.q_inv[h] = inv
        r.q_unit[h] = raw * inv
        r.queries[h] = spin(raw * inv * r.mults[4:5, 0:HD], cosine, sine).astype(BF)
    for s in late:
        s.step5()

    def attend(h):
        scores = mm_t(r.queries[h], r.keys[...]) * SCALE + r.bias[...]
        row_max = jnp.max(scores, axis=1, keepdims=True)
        weights = jnp.exp(scores - row_max)
        probs = weights / jnp.sum(weights, axis=1, keepdims=True)
        r.probs[h] = probs
        r.attended[h] = mm(probs.astype(BF), r.values[...]).astype(BF)

    for h in range(HEADS):
        attend(h)

    ow.step6()
    left = jnp.zeros((T, 384), F32)
    right = jnp.zeros((T, 256), F32)
    for h in range(HEADS):
        some = slice(4 * h, 4 * h + 4)
        left = left + mm(r.attended[h], r.w_o[0, :, some].reshape(256, WO))
        right = right + mm(r.attended[h], r.w_o[1, :, some].reshape(256, WO)[:, 0:256])
    mixer_out = jnp.concatenate([left, right], axis=1)
    mixer_inv = inv_of(mixer_out)
    r.mix_unit[...] = mixer_out * mixer_inv
    middle = r.h[...].astype(F32) + r.mix_unit[...] * r.mults[1:2]
    middle_inv = inv_of(middle)
    r.mid_unit[...] = middle * middle_inv
    r.middle[...] = middle
    r.mid[...] = (r.mid_unit[...] * r.mults[2:3]).astype(BF)
    r.mid_t[...] = mm(r.mid[...], r.turn[...]).astype(BF)
    for s in late:
        s.step6()

    r.acc[...] = jnp.zeros_like(r.acc)
    for w, rows_in, first in ((r.w_x2, r.mid, 0), (r.w_z2, r.mid_t, 2)):

        def forward(j, carry, w=w, rows_in=rows_in, first=first):
            cols = pl.ds(pl.multiple_of(j * 512, 512), 512)
            gate = mm(rows_in[...], w[0, :, cols])
            up = mm(rows_in[...], w[1, :, cols])
            square = gate * gate
            tanh = jnp.tanh(GELU_A * gate * (1.0 + GELU_B * square))
            active = 0.5 * gate * (1.0 + tanh)
            slope = 0.5 * (1.0 + tanh) + 0.5 * gate * (1.0 - tanh * tanh) * (
                GELU_A * (1.0 + 3.0 * GELU_B * square)
            )
            units = (active * up).astype(BF)
            part = first + j
            r.units[part] = units
            r.active[part] = active
            r.slope_up[part] = slope * up
            r.acc[...] += mm(units, r.w_d[pl.ds(part * 4, 4)].reshape(512, D))
            return carry

        lax.fori_loop(0, 2, forward, 0)
    ffn_out = r.acc[...]
    ffn_inv = inv_of(ffn_out)
    ffn_unit = ffn_out * ffn_inv
    r.mixed[...] = (r.middle[...] + ffn_unit * r.mults[3:4]).astype(BF)
    grad_out = r.og[...].astype(F32)
    r.gain_sums[...] = jnp.zeros_like(r.gain_sums)
    r.gain_sums[3:4] = jnp.sum(grad_out * ffn_unit, axis=0, keepdims=True)
    r.g_ffn[...] = norm_back(grad_out * r.mults[3:4], ffn_unit, ffn_inv).astype(BF)
    net.finish()

    def sums(kind, name, *args):
        tags = ("g_", "b_", "f_", "n_", "t2_", "r2_", "t1_", "r1_", "total_", "swap_", "got_", "out_")
        if name == "d":
            tags = tags[:9] + tags[11:]
        return kind(net, *args, [getattr(r, tag + name) for tag in tags])

    sx1 = sums(RowSums, "x1", ("y", "z", "x"), WX1)
    sz1 = sums(RowSums, "z1", ("x", "y", "z"), WZ1)
    sx2 = sums(RowSums, "x2", ("y", "z", "x"), WX2)
    sz2 = sums(RowSums, "z2", ("x", "y", "z"), WZ2)
    so = sums(TileSums, "o", ("y", "x", "z"), WO, False)
    sd = sums(TileSums, "d", ("z", "x", "y"), WD, True)
    wide = (sx2, sz2, sd)
    for w, g, rows_in, first, total in (
        (r.w_x2, r.g_x2, r.mid, 0, r.acc),
        (r.w_z2, r.g_z2, r.mid_t, 2, r.acc_t),
    ):
        total[...] = jnp.zeros_like(total)

        def backward(j, carry, w=w, g=g, rows_in=rows_in, first=first, total=total):
            cols = pl.ds(pl.multiple_of(j * 512, 512), 512)
            part = first + j
            some = pl.ds(part * 4, 4)
            g_ffn = r.g_ffn[...]
            grad_hidden = mm_t(g_ffn, r.w_d[some].reshape(512, D))
            r.g_d[some] = t_mm(r.units[part], g_ffn).astype(BF).reshape(4, 4, 2, 16, D)
            grad_gate = (grad_hidden * r.slope_up[part]).astype(BF)
            grad_up = (grad_hidden * r.active[part]).astype(BF)
            total[...] += mm_t(grad_gate, w[0, :, cols]) + mm_t(grad_up, w[1, :, cols])
            g[0, :, cols] = t_mm(rows_in[...], grad_gate).astype(BF)
            g[1, :, cols] = t_mm(rows_in[...], grad_up).astype(BF)
            return carry

        lax.fori_loop(0, 2, backward, 0)
        if first == 0:
            for steps in (2, 1, 3, 0):
                sx2.give(steps)
    for steps in (2, 1, 3, 0):
        sz2.give(steps)
        sd.give(steps)

    grad_in = r.acc[...] + split_dot(r.acc_t[...], r.turn[...])
    mid_unit = r.mid_unit[...]
    r.gain_sums[2:3] = jnp.sum(grad_in * mid_unit, axis=0, keepdims=True)
    grad_middle = r.og[...].astype(F32) + norm_back(grad_in * r.mults[2:3], mid_unit, inv_of(r.middle[...]))
    r.g_middle[...] = grad_middle
    mix_unit = r.mix_unit[...]
    r.gain_sums[1:2] = jnp.sum(grad_middle * mix_unit, axis=0, keepdims=True)
    grad_mixer = norm_back(grad_middle * r.mults[1:2], mix_unit, mixer_inv).astype(BF)
    for s in wide:
        s.take(2)
    for h in range(HEADS):
        some = slice(4 * h, 4 * h + 4)
        r.g_att[h] = (
            mm_t(grad_mixer[:, 0:384], r.w_o[0, :, some].reshape(256, WO))
            + mm_t(grad_mixer[:, 384:640], r.w_o[1, :, some].reshape(256, WO)[:, 0:256])
        ).astype(BF)
        grad = t_mm(r.attended[h], grad_mixer).astype(BF)
        r.g_o[0, :, some] = grad[:, 0:384].reshape(4, 4, 16, 384)
        r.g_o[1, :, some, :, 0:256] = grad[:, 384:640].reshape(4, 4, 16, 256)
    for steps in (2, 1, 3, 0):
        so.give(steps)
    r.d_values[...] = t_mm(r.probs[0].astype(BF), r.g_att[0])
    for h in range(1, HEADS):
        r.d_values[...] += t_mm(r.probs[h].astype(BF), r.g_att[h])

    def halo_aside(i, whole, scale):
        r.low[i] = (whole[0 : 2 * T] * scale).astype(BF)
        return net.send(r.low.at[i, pl.ds(T, T)], r.side.at[i], net.sib)

    def halo_back(i, copy):
        copy.wait_recv()
        far = r.low[i, 0:T]
        r.onward[i] = jnp.where(net.core == 1, far + r.side[i], far)
        return net.send(r.onward.at[i], r.back.at[i], net.along(-2))

    def halo_sum(i, whole, scale, copy):
        copy.wait_recv()
        side = jnp.where(net.core == 0, r.side[i].astype(F32), 0.0)
        return whole[2 * T :] * scale + r.back[i].astype(F32) + side

    aside_v = halo_aside(1, r.d_values, 1.0)
    for s in wide:
        s.take(1)

    r.d_keys[...] = jnp.zeros_like(r.d_keys)
    r.q_gain[...] = jnp.zeros_like(r.q_gain)

    def attend_back(h):
        probs = r.probs[h]
        g_att = r.g_att[h]
        grad_probs = mm_t(g_att, r.values[...])
        delta = jnp.sum(probs * grad_probs, axis=1, keepdims=True)
        grad_scores = (probs * (grad_probs - delta)).astype(BF)
        grad_q = mm(grad_scores, r.keys[...]) * SCALE
        r.d_keys[...] += t_mm(grad_scores, r.queries[h])
        back = spin_back(grad_q, r.cosine[2 * T :], r.sine[2 * T :])
        unit = r.q_unit[h]
        r.q_gain[...] += jnp.sum(back * unit, axis=0, keepdims=True)
        r.g_q[h] = norm_back(back * r.mults[4:5, 0:HD], unit, r.q_inv[h]).astype(BF)

    attend_back(0)
    back_v = halo_back(1, aside_v)
    for s in (sx2, sz2):
        s.take(3)
    for h in range(1, HEADS):
        attend_back(h)
    aside_k = halo_aside(0, r.d_keys, SCALE)

    normed, turned = r.normed[...], r.normed_t[...]
    back_k = halo_back(0, aside_k)
    sd.take(3)
    for h in range(HEADS):
        if h < 2:
            r.g_x1[0, :, 256 * h : 256 * h + 256] = t_mm(normed, r.g_q[h]).astype(BF)
        elif h == 2:
            r.g_z1[0, :, 0:256] = t_mm(turned, r.g_q[h]).astype(BF)
        else:
            last = t_mm(turned, r.g_q[h]).astype(BF)
            r.g_z1[0, :, 256:384] = last[:, 0:128]
            r.g_z1[1, :, 0:128] = last[:, 128:256]
    for s in wide:
        s.step2()
    own_k = halo_sum(0, r.d_keys, SCALE, back_k)
    own_v = halo_sum(1, r.d_values, 1.0, back_v)
    key_back = spin_back(own_k, cosine, sine)
    k_unit = r.k_unit[...]
    key_gain = jnp.sum(key_back * k_unit, axis=0, keepdims=True)
    grad_k = norm_back(key_back * r.mults[5:6, 0:HD], k_unit, key_inv).astype(BF)
    grad_v = own_v.astype(BF)
    r.g_z1[1, :, 128:384] = t_mm(turned, grad_v).astype(BF)
    for steps in (2, 1, 3, 0):
        sz1.give(steps)
    r.g_x1[1, :, 0:256] = t_mm(normed, grad_k).astype(BF)
    r.g_x1[1, :, 384:512] = jnp.zeros((D, 128), BF)
    grad_natural = (
        mm_t(r.g_q[0], r.w_x1[0, :, 0:256])
        + mm_t(r.g_q[1], r.w_x1[0, :, 256:512])
        + mm_t(grad_k, r.w_x1[1, :, 0:256])
    )
    g_last = r.g_q[3]
    grad_turned = (
        mm_t(r.g_q[2], r.w_z1[0, :, 0:256])
        + mm_t(g_last[:, 0:128], r.w_z1[0, :, 256:384])
        + mm_t(g_last[:, 128:256], r.w_z1[1, :, 0:128])
        + mm_t(grad_v, r.w_z1[1, :, 128:384])
    )
    grad_normed = grad_natural + split_dot(grad_turned, r.turn[...])
    in_unit = r.in_unit[...]
    r.gain_sums[0:1] = jnp.sum(grad_normed * in_unit, axis=0, keepdims=True)
    both = jnp.concatenate([r.q_gain[...], key_gain, jnp.zeros((6, HD), F32)], axis=0).astype(BF)
    r.gain_sums[4:6] = mm_t(both, r.pick[...])[0:2]
    r.g_x1[1, :, 256:384] = mm_t(r.eye[...], r.gain_sums[...].astype(BF)).astype(BF)
    for steps in (2, 1, 3, 0):
        sx1.give(steps)
    slim = (so, sz1, sx1)
    for steps in (2, 1, 3):
        for s in slim:
            s.take(steps)
    for s in wide:
        s.take(0)
        s.step3()
    r.igrad[...] = r.g_middle[...] + norm_back(grad_normed * r.mults[0:1], in_unit, input_inv)
    for s in slim:
        s.step2()
    for s in wide:
        s.step4()
    for s in slim:
        s.take(0)
        s.step3()
    for s in wide:
        s.step5()
    for s in slim:
        s.step4()
    for s in wide:
        s.step6()
    for s in slim:
        s.step5()
    for s in slim:
        s.step6()
    net.finish()


def layer(*args):
    vmem = pltpu.VMEM
    ins = ("h", "q", "k", "v", "o", "g", "u", "d", *GAINS, "lens", "og")
    outs = {
        "mixed": ((T, D), BF),
        "igrad": ((T, D), F32),
        "out_x1": ((2, 8, WX1), F32),
        "out_z1": ((2, 8, WZ1), F32),
        "out_o": ((2, 8, WO), F32),
        "out_x2": ((2, 8, WX2), F32),
        "out_z2": ((2, 8, WZ2), F32),
        "out_d": ((16, WD), F32),
    }
    scratch = {}
    for name, w in (("x1", WX1), ("z1", WZ1), ("x2", WX2), ("z2", WZ2)):
        scratch |= {
            "own_" + name: ((2, 16, w), F32),
            "es_" + name: ((16, w), BF),
            "ed_" + name: ((16, w), BF),
            "s1_" + name: ((4, 16, w), BF),
            "s2_" + name: ((4, 48, w), BF),
            "b3_" + name: ((160, w), BF),
            "w_" + name: ((2, D, w), BF),
            "b_" + name: ((4, 160, w), BF),
            "f_" + name: ((2, 80, w), BF),
            "n_" + name: ((2, 160, w), BF),
            "r2_" + name: ((3, 48, w), BF),
            "r1_" + name: ((3, 16, w), BF),
            "swap_" + name: ((8, w), F32),
            "got_" + name: ((8, w), F32),
        }
    for name, w in (("o", WO), ("d", WD)):
        scratch |= {
            "b_" + name: ((4, 16, 16, w), BF),
            "f_" + name: ((2, 8, 16, w), BF),
            "n_" + name: ((2, 16, 16, w), BF),
            "t2_" + name: ((16, 16, w), BF),
            "r2_" + name: ((3, 4, 16, w), BF),
            "t1_" + name: ((4, 16, w), BF),
            "r1_" + name: ((3, 16, w), BF),
        }
    scratch |= {
        "g_x1": ((2, D, WX1), BF),
        "g_z1": ((2, D, WZ1), BF),
        "total_z2": ((160, WZ2), F32),
        "total_z1": ((160, WZ1), F32),
        "own_o": ((2, 16, WO), F32),
        "es_o": ((16, WO), BF),
        "ed_o": ((16, WO), BF),
        "s1_o": ((16, WO), BF),
        "swap_o": ((8, WO), F32),
        "got_o": ((8, WO), F32),
        "w_o": ((2, 4, 16, 16, WO), BF),
        "w_d": ((16, 4, 2, 16, WD), BF),
        "tmp": ((160, 1024), F32),
        "gain_rows": ((16, 128), F32),
        "turn": ((D, D), BF),
        "eye": ((D, D), BF),
        "pick": ((D, HD), BF),
        "cosine": ((SPAN, 128), F32),
        "sine": ((SPAN, 128), F32),
        "rows_in": ((2, T, D), BF),
        "rows_side": ((T, D), BF),
        "bias": ((T, SPAN), F32),
        "mults": ((8, D), F32),
        "gain_sums": ((128, D), F32),
        "in_unit": ((T, D), F32),
        "normed": ((T, D), BF),
        "normed_t": ((T, D), BF),
        "k_unit": ((T, HD), F32),
        "keys": ((SPAN, HD), BF),
        "values": ((SPAN, HD), BF),
        "queries": ((HEADS, T, HD), BF),
        "q_unit": ((HEADS, T, HD), F32),
        "q_inv": ((HEADS, T, 1), F32),
        "probs": ((HEADS, T, SPAN), F32),
        "attended": ((HEADS, T, HD), BF),
        "mix_unit": ((T, D), F32),
        "mid_unit": ((T, D), F32),
        "middle": ((T, D), F32),
        "mid": ((T, D), BF),
        "mid_t": ((T, D), BF),
        "units": ((4, T, 512), BF),
        "active": ((4, T, 512), F32),
        "slope_up": ((4, T, 512), F32),
        "acc": ((T, D), F32),
        "acc_t": ((T, D), F32),
        "g_ffn": ((T, D), BF),
        "g_att": ((HEADS, T, HD), BF),
        "g_q": ((HEADS, T, HD), BF),
        "d_keys": ((SPAN, HD), F32),
        "d_values": ((SPAN, HD), F32),
        "low": ((2, 2 * T, HD), BF),
        "side": ((2, T, HD), BF),
        "onward": ((2, T, HD), BF),
        "back": ((2, T, HD), BF),
        "q_gain": ((1, HD), F32),
    }
    inside = pl.BlockSpec(memory_space=vmem)
    names = (*ins, *outs, *scratch, "send_sems", "recv_sems")
    return pl.pallas_call(
        lambda *refs: layer_kernel(names, *refs),
        out_shape=[jax.ShapeDtypeStruct(*s) for s in outs.values()],
        in_specs=[inside] * len(ins),
        out_specs=[inside] * len(outs),
        scratch_shapes=[vmem(*s) for s in scratch.values()] + [pltpu.SemaphoreType.DMA((SEMS,))] * 2,
        compiler_params=pltpu.CompilerParams(
            collective_id=0, has_side_effects=True, vmem_limit_bytes=VMEM_CAP
        ),
        name="decoder_layer",
    )(*args)


def deliver_kernel(mixed, igrad, x1, z1, o, x2, z2, d, *outs):
    outs[0][...] = mixed[...]
    outs[1][...] = igrad[...]
    outs[2][:, 0:512] = x1[0, 0:5]
    outs[2][:, 512:896] = z1[0, 0:5]
    outs[2][:, 896:1024] = z1[1, 0:5, 0:128]
    outs[3][...] = x1[1, 0:5, 0:256]
    outs[4][...] = z1[1, 0:5, 128:384]
    outs[5][:, 0:384] = o[0]
    outs[5][:, 384:640] = o[1, :, 0:256]
    for i in range(2):
        outs[6 + i][:, 0:1024] = x2[i, 0:5]
        outs[6 + i][:, 1024:2048] = z2[i, 0:5]
    outs[8][...] = d[...]
    gains = x1[1, :, 256:384].T
    for at, row, n in ((9, 0, 5), (10, 4, 2), (11, 5, 2), (12, 1, 5), (13, 2, 5), (14, 3, 5)):
        outs[at][...] = gains[row : row + 1, 0:n].reshape(n)


def deliver(*parts):
    inside = pl.BlockSpec(memory_space=pltpu.VMEM)
    shapes = [(T, D), (5, 1024), (5, 256), (5, 256), (8, D), (5, 2048), (5, 2048), (16, D)]
    shapes += [(5,), (2,), (2,), (5,), (5,), (5,)]
    return pl.pallas_call(
        deliver_kernel,
        out_shape=[jax.ShapeDtypeStruct((T, D), BF)] + [jax.ShapeDtypeStruct(s, F32) for s in shapes],
        in_specs=[inside] * len(parts),
        out_specs=[inside] * 15,
        name="deliver",
    )(*parts)


def per_device(
    hidden_in,
    query_weight,
    key_weight,
    value_weight,
    output_weight,
    gate_weight,
    up_weight,
    down_weight,
    input_gain,
    query_gain,
    key_gain,
    mixer_gain,
    middle_gain,
    output_gain,
    seq_lengths,
    out_grad,
):
    gains = (input_gain, mixer_gain, middle_gain, output_gain, query_gain, key_gain)
    parts = layer(
        hidden_in,
        query_weight,
        key_weight,
        value_weight,
        output_weight,
        gate_weight,
        up_weight,
        down_weight,
        *[a.reshape(1, -1) for a in gains],
        seq_lengths.reshape(1, 64),
        out_grad,
    )
    return tuple(deliver(*parts))


def solution(mesh):
    return jax.shard_map(
        per_device,
        mesh=mesh,
        in_specs=(
            P("dp", None),
            P("dp", None),
            P("dp", None),
            P("dp", None),
            P("dp", None),
            P("dp", None),
            P("dp", None),
            P("dp", None),
            P("dp"),
            P("dp"),
            P("dp"),
            P("dp"),
            P("dp"),
            P("dp"),
            P(),
            P("dp", None),
        ),
        out_specs=(
            P("dp", None),
            P("dp", None),
            P("dp", None),
            P("dp", None),
            P("dp", None),
            P("dp", None),
            P("dp", None),
            P("dp", None),
            P("dp", None),
            P("dp"),
            P("dp"),
            P("dp"),
            P("dp"),
            P("dp"),
            P("dp"),
        ),
        check_vma=False,
    )
```

```python
import math

import jax
import jax.numpy as jnp
from jax import lax
from jax.experimental import pallas as pl
from jax.experimental.pallas import tpu as pltpu
from jax.sharding import PartitionSpec as P

MESH = pl.DeviceIdType.MESH
BF = jnp.bfloat16
F32 = jnp.float32
T = 256
D = 640
HD = 256
HEADS = 4
SPAN = 3 * T
WINDOW = 512
EPSILON = 1e-06
ROPE_BASE = 10000.0
NEG_FILL = -1e30
SCALE = 1.0 / math.sqrt(HD)
GELU_A = math.sqrt(2.0 / math.pi)
GELU_B = 0.044715
WX1, WZ1, WX2, WZ2, WD, WO = 512, 384, 1024, 1024, 640, 384
SEMS = 232
GAINS = ("n_in", "n_mix", "n_mid", "n_out", "n_q", "n_k")
VMEM_CAP = 62 << 20


def place(x, z, y, c):
    return ((x % 4) * 4 + (z % 4)) * 8 + (y % 4) * 2 + c


class Links:
    def __init__(self, send_sems, recv_sems):
        self.me = lax.axis_index("dp")
        self.at = {"x": self.me // 32, "z": (self.me // 8) % 4, "y": (self.me // 2) % 4}
        self.core = self.me % 2
        self.other = 1 - self.core
        self.sib = place(self.at["x"], self.at["z"], self.at["y"], self.other)
        self.xz = self.at["x"] * 4 + self.at["z"]
        self.send_sems, self.recv_sems, self.used, self.open = send_sems, recv_sems, 0, []

    def peer(self, axis, steps):
        moved = dict(self.at)
        moved[axis] = moved[axis] + steps
        return place(moved["x"], moved["z"], moved["y"], self.core)

    def along(self, steps):
        return (self.me + 128 + steps) % 128

    def slot(self, axis, steps):
        return (self.at[axis] + steps) % 4

    def greet(self):
        sem = pltpu.get_barrier_semaphore()
        partners = [self.sib] + [self.along(s) for s in (2, -2)]
        for axis in ("x", "z", "y"):
            partners += [self.peer(axis, o) for o in (1, 2, 3)]
        for p in partners:
            pl.semaphore_signal(sem, inc=1, device_id=(p,), device_id_type=MESH)
        self.greeted = len(partners)

    def meet(self):
        pl.semaphore_wait(pltpu.get_barrier_semaphore(), self.greeted)

    def send(self, src, dst, target):
        i = self.used
        self.used += 1
        copy = pltpu.make_async_remote_copy(
            src_ref=src,
            dst_ref=dst,
            send_sem=self.send_sems.at[i],
            recv_sem=self.recv_sems.at[i],
            device_id=(target,),
            device_id_type=MESH,
        )
        copy.start()
        self.open.append(copy.wait_send)
        return copy

    def local(self, src, dst):
        i = self.used
        self.used += 1
        copy = pltpu.make_async_copy(src, dst, self.send_sems.at[i])
        copy.start()
        return copy

    def finish(self):
        for wait in self.open:
            wait()
        self.open = []


class Rows:
    def __init__(self, net, axes, width, refs):
        self.net, self.axes, self.width = net, axes, width
        self.own, self.e_src, self.e_dst, self.s1, self.s2, self.b3, self.w, self.tmp = refs
        self.ends = []

    def view(self, slot, at, n):
        rows = pl.ds(pl.multiple_of(slot * 160 + at * 16, 16), n * 16)
        return self.w.at[self.net.core, rows]

    def step0(self):
        self.e_src[...] = self.own[self.net.other].astype(BF)

    def step0b(self):
        self.swap = self.net.send(self.e_src, self.e_dst, self.net.sib)

    def step1(self):
        net, wide = self.net, slice(0, self.width)
        self.swap.wait_recv()
        mine = self.own[net.core][0:5]
        theirs = self.e_dst[...].astype(F32)[0:5]
        first = net.core == 0
        self.tmp[0:5, wide] = jnp.where(first, mine, theirs)
        self.tmp[5:10, wide] = jnp.where(first, theirs, mine)
        slot = self.s1.at[net.at[self.axes[0]]]
        slot[...] = self.tmp[0:16, wide].astype(BF)
        self.p = [net.send(slot, slot, net.peer(self.axes[0], o)) for o in (1, 2, 3)]

    def step2(self):
        net, wide = self.net, slice(0, self.width)
        for copy in self.p:
            copy.wait_recv()
        for j in range(4):
            self.tmp[10 * j : 10 * j + 10, wide] = self.s1[j].astype(F32)[0:10]
        slot = self.s2.at[net.at[self.axes[1]]]
        slot[...] = self.tmp[0:48, wide].astype(BF)
        self.p = [net.send(slot, slot, net.peer(self.axes[1], o)) for o in (1, 2, 3)]

    def step3(self):
        net, wide = self.net, slice(0, self.width)
        for copy in self.p:
            copy.wait_recv()
        for j in range(4):
            self.tmp[40 * j : 40 * j + 40, wide] = self.s2[j].astype(F32)[0:40]
        self.b3[...] = self.tmp[0:160, wide].astype(BF)
        axis = self.axes[2]
        dst = self.view(net.at[axis], 0, 10)
        self.up = net.send(self.b3, dst, net.peer(axis, 1))
        self.down = net.send(self.b3, dst, net.peer(axis, 3))
        self.ends.append(net.send(self.b3, dst, net.sib).wait_recv)
        self.ends.append(net.local(self.b3, dst).wait)

    blocks = 10

    def step4(self):
        net, axis, n = self.net, self.axes[2], self.blocks
        half = n // 2
        self.up.wait_recv()
        part = self.view(net.slot(axis, 3), 0, half)
        self.far_up = net.send(part, part, net.peer(axis, 1))
        self.down.wait_recv()
        part = self.view(net.slot(axis, 1), half, half)
        self.far_down = net.send(part, part, net.peer(axis, 3))
        for steps in (3, 1):
            whole = self.view(net.slot(axis, steps), 0, n)
            self.ends.append(net.send(whole, whole, net.sib).wait_recv)

    def step5(self):
        net, axis, half = self.net, self.axes[2], self.blocks // 2
        for copy, at in ((self.far_up, 0), (self.far_down, half)):
            copy.wait_recv()
            part = self.view(net.slot(axis, 2), at, half)
            self.ends.append(net.send(part, part, net.sib).wait_recv)

    def step6(self):
        for wait in self.ends:
            wait()


class Tiles(Rows):
    blocks = 16

    def __init__(self, net, axes, w, by_core):
        self.net, self.axes, self.w, self.by_core = net, axes, w, by_core
        self.ends = []

    def view(self, slot, at, n):
        if self.by_core:
            return self.w.at[pl.ds(at, n), slot, self.net.core]
        return self.w.at[self.net.core, slot, pl.ds(at, n)]

    def first(self, src):
        net = self.net
        a, b, c = (net.at[axis] for axis in self.axes)
        dst = self.w.at[b * 4 + a, c, net.core] if self.by_core else self.w.at[net.core, c, b * 4 + a]
        self.p = [net.send(src, dst, net.peer(self.axes[0], o)) for o in (1, 2, 3)]
        self.kept = net.local(src, dst)

    def step2(self):
        net = self.net
        for copy in self.p:
            copy.wait_recv()
        self.kept.wait()
        part = self.view(net.at[self.axes[2]], net.at[self.axes[1]] * 4, 4)
        self.p = [net.send(part, part, net.peer(self.axes[1], o)) for o in (1, 2, 3)]

    def step3(self):
        net, axis = self.net, self.axes[2]
        for copy in self.p:
            copy.wait_recv()
        part = self.view(net.at[axis], 0, 16)
        self.up = net.send(part, part, net.peer(axis, 1))
        self.down = net.send(part, part, net.peer(axis, 3))
        self.ends.append(net.send(part, part, net.sib).wait_recv)


class RowSums:
    blocks = 10

    def __init__(self, net, axes, width, refs):
        self.net, self.axes, self.width = net, axes, width
        (self.g, self.b, self.f, self.n, self.t2, self.r2, self.t1, self.r1, self.total) = refs[:9]
        self.rest = refs[9:]
        self.swaps, self.onward, self.near = {}, {}, {}

    def view(self, steps, at, n, which):
        slot = self.net.slot(self.axes[2], steps)
        rows = pl.ds(pl.multiple_of(slot * 160 + at * 16, 16), n * 16)
        return self.g.at[which, rows]

    def rows(self, at, n):
        return pl.ds(at * 16, n * 16)

    def tile(self, steps, i):
        slot = self.net.slot(self.axes[2], steps)
        return (self.net.core, pl.ds(pl.multiple_of(slot * 160 + i * 16, 16), 16))

    def block(self, i):
        return pl.ds(pl.multiple_of(i * 16, 16), 16)

    def give(self, steps):
        src = self.view(steps, 0, self.blocks, self.net.other)
        self.swaps[steps] = self.net.send(src, self.b.at[steps], self.net.sib)

    def add(self, steps, held, at, count):
        def body(i, carry):
            where = self.tile(steps, i + at)
            self.g[where] = self.g[where] + held[self.block(i)]
            return carry

        lax.fori_loop(0, count, body, 0)

    def take(self, steps):
        net, axis, n, core = self.net, self.axes[2], self.blocks, self.net.core
        half = n // 2
        self.swaps[steps].wait_recv()
        if steps == 0:
            return
        self.add(steps, self.b.at[steps], 0, n)
        if steps == 2:
            self.onward[1] = net.send(self.view(2, 0, half, core), self.f.at[0], net.peer(axis, 1))
            self.onward[3] = net.send(self.view(2, half, half, core), self.f.at[1], net.peer(axis, 3))
        elif steps == 1:
            self.near["a"] = net.send(
                self.view(1, half, half, core), self.n.at[0, self.rows(half, half)], net.peer(axis, 1)
            )
        else:
            self.near["b"] = net.send(
                self.view(3, 0, half, core), self.n.at[1, self.rows(0, half)], net.peer(axis, 3)
            )

    def step2(self):
        net, axis, core = self.net, self.axes[2], self.net.core
        half = self.blocks // 2
        self.onward[1].wait_recv()
        self.add(1, self.f.at[0], 0, half)
        self.near["c"] = net.send(self.view(1, 0, half, core), self.n.at[0, self.rows(0, half)], net.peer(axis, 1))
        self.onward[3].wait_recv()
        self.add(3, self.f.at[1], half, half)
        self.near["d"] = net.send(
            self.view(3, half, half, core), self.n.at[1, self.rows(half, half)], net.peer(axis, 3)
        )

    def total3(self, i):
        at = self.block(i)
        own = self.g[self.tile(0, i)].astype(F32) + self.b[0, at].astype(F32)
        return own + self.n[0, at].astype(F32) + self.n[1, at].astype(F32)

    def step3(self):
        net, width, axis = self.net, self.width, self.axes[1]
        for part in "abcd":
            self.near[part].wait_recv()

        def body(i, carry):
            self.total[self.block(i), 0 : self.width] = self.total3(i)
            return carry

        lax.fori_loop(0, 10, body, 0)
        for j in range(4):
            part = self.total[40 * j : 40 * j + 40, 0:width]
            self.t2[j] = jnp.concatenate([part, jnp.zeros((8, width), F32)], axis=0).astype(BF)
        self.p = [net.send(self.t2.at[net.slot(axis, o)], self.r2.at[o - 1], net.peer(axis, o)) for o in (1, 2, 3)]

    def step4(self):
        net, width, axis = self.net, self.width, self.axes[0]
        for copy in self.p:
            copy.wait_recv()
        own = self.t2[net.at[self.axes[1]]].astype(F32)
        for o in range(3):
            own = own + self.r2[o].astype(F32)
        self.total[0:48, 0:width] = own
        for j in range(4):
            part = self.total[10 * j : 10 * j + 10, 0:width]
            self.t1[j] = jnp.concatenate([part, jnp.zeros((6, width), F32)], axis=0).astype(BF)
        self.p = [net.send(self.t1.at[net.slot(axis, o)], self.r1.at[o - 1], net.peer(axis, o)) for o in (1, 2, 3)]

    def step5(self):
        net = self.net
        swap, got, out = self.rest
        for copy in self.p:
            copy.wait_recv()
        own = self.t1[net.at[self.axes[0]]].astype(F32)
        for o in range(3):
            own = own + self.r1[o].astype(F32)
        self.total[0:16, 0 : self.width] = own
        low_rows = self.total[0:8, 0 : self.width]
        high_rows = self.total[5:13, 0 : self.width]
        first = net.core == 0
        swap[...] = jnp.where(first, high_rows, low_rows)
        out[net.core] = jnp.where(first, low_rows, high_rows)
        self.last = net.send(swap, got, net.sib)

    def step6(self):
        swap, got, out = self.rest
        self.last.wait_recv()
        out[self.net.other] = got[...]


class TileSums(RowSums):
    blocks = 16

    def __init__(self, net, axes, width, by_core, refs):
        self.by_core = by_core
        super().__init__(net, axes, width, refs)

    def view(self, steps, at, n, which):
        slot = self.net.slot(self.axes[2], steps)
        if self.by_core:
            return self.g.at[pl.ds(at, n), slot, which]
        return self.g.at[which, slot, pl.ds(at, n)]

    def rows(self, at, n):
        return pl.ds(at, n)

    def tile(self, steps, i):
        slot = self.net.slot(self.axes[2], steps)
        return (i, slot, self.net.core) if self.by_core else (self.net.core, slot, i)

    def block(self, i):
        return i

    def step3(self):
        net = self.net
        for part in "abcd":
            self.near[part].wait_recv()

        def body(i, carry):
            self.t2[i] = self.total3(i).astype(BF)
            return carry

        lax.fori_loop(0, 16, body, 0)
        self.p = [
            net.send(
                self.t2.at[pl.ds(net.slot(self.axes[1], o) * 4, 4)], self.r2.at[o - 1], net.peer(self.axes[1], o)
            )
            for o in (1, 2, 3)
        ]

    def step4(self):
        net = self.net
        for copy in self.p:
            copy.wait_recv()
        for j in range(4):
            value = self.t2[net.at[self.axes[1]] * 4 + j].astype(F32)
            for o in range(3):
                value = value + self.r2[o, j].astype(F32)
            self.t1[j] = value.astype(BF)
        axis = self.axes[0]
        self.p = [net.send(self.t1.at[net.slot(axis, o)], self.r1.at[o - 1], net.peer(axis, o)) for o in (1, 2, 3)]

    def step5(self):
        net = self.net
        for copy in self.p:
            copy.wait_recv()
        own = self.t1[net.at[self.axes[0]]].astype(F32)
        for o in range(3):
            own = own + self.r1[o].astype(F32)
        if self.by_core:
            self.rest[0][...] = own
            return
        swap, got, out = self.rest
        first = net.core == 0
        swap[...] = jnp.where(first, own[8:16], own[0:8])
        out[net.core] = jnp.where(first, own[0:8], own[8:16])
        self.last = net.send(swap, got, net.sib)

    def step6(self):
        if not self.by_core:
            super().step6()


def mm(left, right):
    return jnp.dot(left, right, preferred_element_type=F32)


def mm_t(left, right):
    return lax.dot_general(left, right, (((1,), (1,)), ((), ())), preferred_element_type=F32)


def t_mm(left, right):
    return lax.dot_general(left, right, (((0,), (0,)), ((), ())), preferred_element_type=F32)


def inv_of(values):
    return lax.rsqrt(jnp.mean(values * values, axis=-1, keepdims=True) + EPSILON)


def norm_back(upstream, unit_rows, inv_rms):
    return inv_rms * (upstream - unit_rows * jnp.mean(unit_rows * upstream, axis=-1, keepdims=True))


def spin(values, cosine, sine):
    a, b = values[:, :128], values[:, 128:]
    return jnp.concatenate([a * cosine - b * sine, b * cosine + a * sine], axis=1)


def spin_back(values, cosine, sine):
    a, b = values[:, :128], values[:, 128:]
    return jnp.concatenate([a * cosine + b * sine, b * cosine - a * sine], axis=1)


def count(shape, dim):
    return lax.broadcasted_iota(jnp.int32, shape, dim)


def hot(condition):
    return jnp.where(condition, 1.0, 0.0).astype(BF)


def split_dot(value, fixed):
    high = value.astype(BF)
    low = (value - high.astype(F32)).astype(BF)
    return mm_t(high, fixed) + mm_t(low, fixed)


class Refs:
    pass


def gather_setup(net, r):
    for ref in (r.own_x1, r.own_z1, r.own_x2, r.own_z2, r.own_o):
        ref[...] = jnp.zeros_like(ref)
    q = r.q[...].astype(F32)
    r.own_x1[0, 0:5] = q[:, 0:512]
    r.own_x1[1, 0:5] = q[:, 512:1024]
    r.gain_rows[...] = jnp.zeros_like(r.gain_rows)
    for i, gain in enumerate((r.n_in, r.n_mix, r.n_mid, r.n_out, r.n_q, r.n_k)):
        r.gain_rows[i : i + 1, 0 : gain.shape[1]] = gain[...].astype(F32)
    tile = t_mm(r.gain_rows[...].astype(BF), hot(count((16, 128), 0) == count((16, 128), 1)))
    r.own_z1[0, 0:5, 256:384] = tile[0:5]
    r.own_z1[0, 0:5, 0:256] = r.k[...].astype(F32)
    r.own_z1[1, 0:5, 0:256] = r.v[...].astype(F32)
    g, u = r.g[...].astype(F32), r.u[...].astype(F32)
    r.own_x2[0, 0:5] = g[:, 0:1024]
    r.own_x2[1, 0:5] = u[:, 0:1024]
    r.own_z2[0, 0:5] = g[:, 1024:2048]
    r.own_z2[1, 0:5] = u[:, 1024:2048]
    o = r.o[...].astype(F32)
    r.own_o[0, 0:8] = o[:, 0:384]
    r.own_o[1, 0:8, 0:256] = o[:, 384:640]

    def rows(name, axes, width):
        names = ("own_", "es_", "ed_", "s1_", "s2_", "b3_", "w_")
        return Rows(net, axes, width, [getattr(r, n + name) for n in names] + [r.tmp])

    x1 = rows("x1", ("y", "z", "x"), WX1)
    z1 = rows("z1", ("x", "y", "z"), WZ1)
    x2 = rows("x2", ("y", "z", "x"), WX2)
    z2 = rows("z2", ("x", "y", "z"), WZ2)
    for s in (x1, z1, x2, z2):
        s.step0()
    r.es_o[...] = r.own_o[net.other].astype(BF)
    return x1, z1, x2, z2, Tiles(net, ("y", "x", "z"), r.w_o, False), Tiles(net, ("z", "x", "y"), r.w_d, True)


def layer_kernel(names, *refs):
    r = Refs()
    for name, ref in zip(names, refs):
        setattr(r, name, ref)
    r.g_x2, r.g_z2, r.g_d, r.g_o = r.w_x2, r.w_z2, r.w_d, r.w_o
    for name in ("x1", "z1", "x2", "z2"):
        setattr(r, "t2_" + name, getattr(r, "s2_" + name))
        setattr(r, "t1_" + name, getattr(r, "s1_" + name))
    r.total_x2 = r.total_x1 = r.total_o = r.total_d = r.tmp
    r.g_middle = r.igrad
    net = Links(r.send_sems, r.recv_sems)
    net.greet()
    x1, z1, x2, z2, ow, dw = gather_setup(net, r)
    r.rows_in[0] = r.h[...]
    net.meet()
    x1.step0b()
    z1.step0b()
    swap_o = net.send(r.es_o, r.ed_o, net.sib)
    x2.step0b()
    z2.step0b()
    x1.step1()
    z1.step1()
    swap_o.wait_recv()
    mine, theirs = r.own_o[net.core][0:8], r.ed_o[...].astype(F32)[0:8]
    r.tmp[0:8, 0:WO] = jnp.where(net.core == 0, mine, theirs)
    r.tmp[8:16, 0:WO] = jnp.where(net.core == 0, theirs, mine)
    r.s1_o[...] = r.tmp[0:16, 0:WO].astype(BF)
    ow.first(r.s1_o)
    x2.step1()
    z2.step1()
    dw.first(r.d)

    k_dim, j_dim = count((D, D), 0), count((D, D), 1)
    tens = (j_dim * 52429) >> 19
    source = (tens & 3) * 160 + (tens >> 4) * 40 + ((tens >> 2) & 3) * 10 + (j_dim - 10 * tens)
    r.turn[...] = hot(k_dim == source)
    spot = count((64, 64), 0)
    lens = jnp.broadcast_to(r.lens[...].astype(F32), (64, 64))
    column = jnp.sum(jnp.where(spot == count((64, 64), 1), lens, 0.0), axis=1, keepdims=True)
    ends = jnp.sum(jnp.where(spot <= count((64, 64), 1), column, 0.0), axis=0, keepdims=True)
    offset = net.me * T
    token = (count((SPAN, 64), 0) + (offset - 2 * T)).astype(F32)
    start = jnp.max(jnp.where(ends <= token, ends, 0.0), axis=1, keepdims=True)
    position = token[:, 0:1] - start
    pair = count((1, 128), 1).astype(F32)
    angle = position * jnp.exp(pair * (-2.0 * math.log(ROPE_BASE) / HD))
    r.cosine[...] = jnp.cos(angle)
    r.sine[...] = jnp.sin(angle)
    ahead = count((T, SPAN), 1) - 2 * T
    distance = count((T, SPAN), 0) - ahead
    inside = (distance >= 0) & (distance < WINDOW) & ((ahead + offset).astype(F32) >= start[2 * T :])
    r.bias[...] = jnp.where(inside, 0.0, NEG_FILL)
    hidden = r.h[...].astype(F32)
    input_inv = inv_of(hidden)
    r.in_unit[...] = hidden * input_inv

    early, late = (x1, z1, ow), (x2, z2, dw)
    for s in early:
        s.step2()
    for s in late:
        s.step2()
    ahead_copy = net.send(r.rows_in.at[0], r.rows_in.at[1], net.along(2))
    for s in (*early, *late):
        s.step3()
    ahead_copy.wait_recv()
    side_copy = net.send(r.rows_in.at[net.core], r.rows_side, net.sib)
    for s in (*early, *late):
        s.step4()
    for s in early:
        s.step5()
    x1.step6()
    z1.step6()

    gain_rows = lax.dot_general(
        r.w_z1[0, :, 256:384], r.turn[...], (((0,), (1,)), ((), ())), preferred_element_type=F32
    )
    far, near = count((D, HD), 0), count((D, HD), 1)
    r.pick[...] = hot(far == 5 * (near >> 1) + (near & 1))
    head_rows = mm(gain_rows.astype(BF), r.pick[...])
    r.mults[0:4] = 1.0 + gain_rows[0:4]
    r.mults[4:6, 0:HD] = 1.0 + head_rows[4:6]
    normed = (r.in_unit[...] * r.mults[0:1]).astype(BF)
    r.normed[...] = normed
    turned = mm(normed, r.turn[...]).astype(BF)
    r.normed_t[...] = turned
    cosine, sine = r.cosine[2 * T :], r.sine[2 * T :]
    for h in range(HEADS):
        raw = mm(normed, r.w_x1[h // 2, :, 256 * (h % 2) : 256 * (h % 2) + 256])
        inv = inv_of(raw)
        r.q_inv[h] = inv
        r.q_unit[h] = raw * inv
        r.queries[h] = spin(raw * inv * r.mults[4:5, 0:HD], cosine, sine).astype(BF)
    side_copy.wait_recv()
    for i in range(3):
        some = slice(T * i, T * i + T)
        if i < 2:
            rows = (r.rows_in[1] if i == 0 else r.rows_side[...]).astype(F32)
            here = (rows * inv_of(rows) * r.mults[0:1]).astype(BF)
            there = mm(here, r.turn[...]).astype(BF)
        else:
            there = turned
        key_raw = mm(there, r.w_z1[0, :, 0:256])
        key_inv = inv_of(key_raw)
        key_unit = key_raw * key_inv
        r.keys[some] = spin(key_unit * r.mults[5:6, 0:HD], r.cosine[some], r.sine[some]).astype(BF)
        r.values[some] = mm(there, r.w_z1[1, :, 0:256]).astype(BF)
    r.k_unit[...] = key_unit
    for s in late:
        s.step5()

    def attend(h):
        scores = mm_t(r.queries[h], r.keys[...]) * SCALE + r.bias[...]
        row_max = jnp.max(scores, axis=1, keepdims=True)
        weights = jnp.exp(scores - row_max)
        probs = weights / jnp.sum(weights, axis=1, keepdims=True)
        r.probs[h] = probs
        r.attended[h] = mm(probs.astype(BF), r.values[...]).astype(BF)

    for h in range(HEADS):
        attend(h)

    ow.step6()
    left = jnp.zeros((T, 384), F32)
    right = jnp.zeros((T, 256), F32)
    for h in range(HEADS):
        some = slice(4 * h, 4 * h + 4)
        left = left + mm(r.attended[h], r.w_o[0, :, some].reshape(256, WO))
        right = right + mm(r.attended[h], r.w_o[1, :, some].reshape(256, WO)[:, 0:256])
    mixer_out = jnp.concatenate([left, right], axis=1)
    mixer_inv = inv_of(mixer_out)
    r.mix_unit[...] = mixer_out * mixer_inv
    middle = r.h[...].astype(F32) + r.mix_unit[...] * r.mults[1:2]
    middle_inv = inv_of(middle)
    r.mid_unit[...] = middle * middle_inv
    r.middle[...] = middle
    r.mid[...] = (r.mid_unit[...] * r.mults[2:3]).astype(BF)
    r.mid_t[...] = mm(r.mid[...], r.turn[...]).astype(BF)
    for s in late:
        s.step6()

    r.acc[...] = jnp.zeros_like(r.acc)
    for w, rows_in, first in ((r.w_x2, r.mid, 0), (r.w_z2, r.mid_t, 2)):

        def forward(j, carry, w=w, rows_in=rows_in, first=first):
            cols = pl.ds(pl.multiple_of(j * 512, 512), 512)
            gate = mm(rows_in[...], w[0, :, cols])
            up = mm(rows_in[...], w[1, :, cols])
            square = gate * gate
            tanh = jnp.tanh(GELU_A * gate * (1.0 + GELU_B * square))
            active = 0.5 * gate * (1.0 + tanh)
            slope = 0.5 * (1.0 + tanh) + 0.5 * gate * (1.0 - tanh * tanh) * (
                GELU_A * (1.0 + 3.0 * GELU_B * square)
            )
            units = (active * up).astype(BF)
            part = first + j
            r.units[part] = units
            r.active[part] = active
            r.slope_up[part] = slope * up
            r.acc[...] += mm(units, r.w_d[pl.ds(part * 4, 4)].reshape(512, D))
            return carry

        lax.fori_loop(0, 2, forward, 0)
    ffn_out = r.acc[...]
    ffn_inv = inv_of(ffn_out)
    ffn_unit = ffn_out * ffn_inv
    r.mixed[...] = (r.middle[...] + ffn_unit * r.mults[3:4]).astype(BF)
    grad_out = r.og[...].astype(F32)
    r.gain_sums[...] = jnp.zeros_like(r.gain_sums)
    r.gain_sums[3:4] = jnp.sum(grad_out * ffn_unit, axis=0, keepdims=True)
    r.g_ffn[...] = norm_back(grad_out * r.mults[3:4], ffn_unit, ffn_inv).astype(BF)
    net.finish()

    def sums(kind, name, *args):
        tags = ("g_", "b_", "f_", "n_", "t2_", "r2_", "t1_", "r1_", "total_", "swap_", "got_", "out_")
        if name == "d":
            tags = tags[:9] + tags[11:]
        return kind(net, *args, [getattr(r, tag + name) for tag in tags])

    sx1 = sums(RowSums, "x1", ("y", "z", "x"), WX1)
    sz1 = sums(RowSums, "z1", ("x", "y", "z"), WZ1)
    sx2 = sums(RowSums, "x2", ("y", "z", "x"), WX2)
    sz2 = sums(RowSums, "z2", ("x", "y", "z"), WZ2)
    so = sums(TileSums, "o", ("y", "x", "z"), WO, False)
    sd = sums(TileSums, "d", ("z", "x", "y"), WD, True)
    wide = (sx2, sz2, sd)
    for w, g, rows_in, first, total in (
        (r.w_x2, r.g_x2, r.mid, 0, r.acc),
        (r.w_z2, r.g_z2, r.mid_t, 2, r.acc_t),
    ):
        total[...] = jnp.zeros_like(total)

        def backward(j, carry, w=w, g=g, rows_in=rows_in, first=first, total=total):
            cols = pl.ds(pl.multiple_of(j * 512, 512), 512)
            part = first + j
            some = pl.ds(part * 4, 4)
            g_ffn = r.g_ffn[...]
            grad_hidden = mm_t(g_ffn, r.w_d[some].reshape(512, D))
            r.g_d[some] = t_mm(r.units[part], g_ffn).astype(BF).reshape(4, 4, 2, 16, D)
            grad_gate = (grad_hidden * r.slope_up[part]).astype(BF)
            grad_up = (grad_hidden * r.active[part]).astype(BF)
            total[...] += mm_t(grad_gate, w[0, :, cols]) + mm_t(grad_up, w[1, :, cols])
            g[0, :, cols] = t_mm(rows_in[...], grad_gate).astype(BF)
            g[1, :, cols] = t_mm(rows_in[...], grad_up).astype(BF)
            return carry

        lax.fori_loop(0, 2, backward, 0)
        if first == 0:
            for steps in (2, 1, 3, 0):
                sx2.give(steps)
    for steps in (2, 1, 3, 0):
        sz2.give(steps)
        sd.give(steps)

    grad_in = r.acc[...] + split_dot(r.acc_t[...], r.turn[...])
    mid_unit = r.mid_unit[...]
    r.gain_sums[2:3] = jnp.sum(grad_in * mid_unit, axis=0, keepdims=True)
    grad_middle = r.og[...].astype(F32) + norm_back(grad_in * r.mults[2:3], mid_unit, inv_of(r.middle[...]))
    r.g_middle[...] = grad_middle
    mix_unit = r.mix_unit[...]
    r.gain_sums[1:2] = jnp.sum(grad_middle * mix_unit, axis=0, keepdims=True)
    grad_mixer = norm_back(grad_middle * r.mults[1:2], mix_unit, mixer_inv).astype(BF)
    for s in wide:
        s.take(2)
    for h in range(HEADS):
        some = slice(4 * h, 4 * h + 4)
        r.g_att[h] = (
            mm_t(grad_mixer[:, 0:384], r.w_o[0, :, some].reshape(256, WO))
            + mm_t(grad_mixer[:, 384:640], r.w_o[1, :, some].reshape(256, WO)[:, 0:256])
        ).astype(BF)
        grad = t_mm(r.attended[h], grad_mixer).astype(BF)
        r.g_o[0, :, some] = grad[:, 0:384].reshape(4, 4, 16, 384)
        r.g_o[1, :, some, :, 0:256] = grad[:, 384:640].reshape(4, 4, 16, 256)
    for steps in (2, 1, 3, 0):
        so.give(steps)
    r.d_values[...] = t_mm(r.probs[0].astype(BF), r.g_att[0])
    for h in range(1, HEADS):
        r.d_values[...] += t_mm(r.probs[h].astype(BF), r.g_att[h])

    def halo_aside(i, whole, scale):
        r.low[i] = (whole[0 : 2 * T] * scale).astype(BF)
        return net.send(r.low.at[i, pl.ds(T, T)], r.side.at[i], net.sib)

    def halo_back(i, copy):
        copy.wait_recv()
        far = r.low[i, 0:T]
        r.onward[i] = jnp.where(net.core == 1, far + r.side[i], far)
        return net.send(r.onward.at[i], r.back.at[i], net.along(-2))

    def halo_sum(i, whole, scale, copy):
        copy.wait_recv()
        side = jnp.where(net.core == 0, r.side[i].astype(F32), 0.0)
        return whole[2 * T :] * scale + r.back[i].astype(F32) + side

    aside_v = halo_aside(1, r.d_values, 1.0)
    for s in wide:
        s.take(1)

    r.d_keys[...] = jnp.zeros_like(r.d_keys)
    r.q_gain[...] = jnp.zeros_like(r.q_gain)

    def attend_back(h):
        probs = r.probs[h]
        g_att = r.g_att[h]
        grad_probs = mm_t(g_att, r.values[...])
        delta = jnp.sum(probs * grad_probs, axis=1, keepdims=True)
        grad_scores = (probs * (grad_probs - delta)).astype(BF)
        grad_q = mm(grad_scores, r.keys[...]) * SCALE
        r.d_keys[...] += t_mm(grad_scores, r.queries[h])
        back = spin_back(grad_q, r.cosine[2 * T :], r.sine[2 * T :])
        unit = r.q_unit[h]
        r.q_gain[...] += jnp.sum(back * unit, axis=0, keepdims=True)
        r.g_q[h] = norm_back(back * r.mults[4:5, 0:HD], unit, r.q_inv[h]).astype(BF)

    attend_back(0)
    back_v = halo_back(1, aside_v)
    for s in (sx2, sz2):
        s.take(3)
    for h in range(1, HEADS):
        attend_back(h)
    aside_k = halo_aside(0, r.d_keys, SCALE)
    for steps in (2, 1, 3):
        so.take(steps)

    normed, turned = r.normed[...], r.normed_t[...]
    for h in range(HEADS):
        r.g_x1[h // 2, :, 256 * (h % 2) : 256 * (h % 2) + 256] = t_mm(normed, r.g_q[h]).astype(BF)
    for steps in (2, 1, 3, 0):
        sx1.give(steps)
    back_k = halo_back(0, aside_k)
    sd.take(3)
    for s in wide:
        s.step2()
    for steps in (2, 1, 3):
        sx1.take(steps)
    own_k = halo_sum(0, r.d_keys, SCALE, back_k)
    own_v = halo_sum(1, r.d_values, 1.0, back_v)
    key_back = spin_back(own_k, cosine, sine)
    k_unit = r.k_unit[...]
    key_gain = jnp.sum(key_back * k_unit, axis=0, keepdims=True)
    grad_k = norm_back(key_back * r.mults[5:6, 0:HD], k_unit, key_inv).astype(BF)
    grad_v = own_v.astype(BF)
    r.g_z1[0, :, 0:256] = t_mm(turned, grad_k).astype(BF)
    r.g_z1[1, :, 0:256] = t_mm(turned, grad_v).astype(BF)
    r.g_z1[1, :, 256:384] = jnp.zeros((D, 128), BF)
    grad_natural = mm_t(r.g_q[0], r.w_x1[0, :, 0:256])
    for h in range(1, HEADS):
        grad_natural = grad_natural + mm_t(r.g_q[h], r.w_x1[h // 2, :, 256 * (h % 2) : 256 * (h % 2) + 256])
    grad_turned = mm_t(grad_k, r.w_z1[0, :, 0:256]) + mm_t(grad_v, r.w_z1[1, :, 0:256])
    grad_normed = grad_natural + split_dot(grad_turned, r.turn[...])
    in_unit = r.in_unit[...]
    r.gain_sums[0:1] = jnp.sum(grad_normed * in_unit, axis=0, keepdims=True)
    both = jnp.concatenate([r.q_gain[...], key_gain, jnp.zeros((6, HD), F32)], axis=0).astype(BF)
    r.gain_sums[4:6] = mm_t(both, r.pick[...])[0:2]
    r.g_z1[0, :, 256:384] = lax.dot_general(
        r.turn[...], r.gain_sums[...].astype(BF), (((0,), (1,)), ((), ())), preferred_element_type=F32
    ).astype(BF)
    for steps in (2, 1, 3, 0):
        sz1.give(steps)
    so.step2()
    for steps in (2, 1, 3):
        sz1.take(steps)
    for s in wide:
        s.take(0)
        s.step3()
    sx1.step2()
    r.igrad[...] = r.g_middle[...] + norm_back(grad_normed * r.mults[0:1], in_unit, input_inv)
    sz1.step2()
    so.take(0)
    so.step3()
    for s in wide:
        s.step4()
    sx1.take(0)
    sx1.step3()
    sz1.take(0)
    sz1.step3()
    so.step4()
    for s in wide:
        s.step5()
    sx1.step4()
    sz1.step4()
    so.step5()
    sx1.step5()
    for s in wide:
        s.step6()
    sz1.step5()
    so.step6()
    sx1.step6()
    sz1.step6()
    net.finish()


def layer(*args):
    vmem = pltpu.VMEM
    ins = ("h", "q", "k", "v", "o", "g", "u", "d", *GAINS, "lens", "og")
    outs = {
        "mixed": ((T, D), BF),
        "igrad": ((T, D), F32),
        "out_x1": ((2, 8, WX1), F32),
        "out_z1": ((2, 8, WZ1), F32),
        "out_o": ((2, 8, WO), F32),
        "out_x2": ((2, 8, WX2), F32),
        "out_z2": ((2, 8, WZ2), F32),
        "out_d": ((16, WD), F32),
    }
    scratch = {}
    for name, w in (("x1", WX1), ("z1", WZ1), ("x2", WX2), ("z2", WZ2)):
        scratch |= {
            "own_" + name: ((2, 16, w), F32),
            "es_" + name: ((16, w), BF),
            "ed_" + name: ((16, w), BF),
            "s1_" + name: ((4, 16, w), BF),
            "s2_" + name: ((4, 48, w), BF),
            "b3_" + name: ((160, w), BF),
            "w_" + name: ((2, D, w), BF),
            "b_" + name: ((4, 160, w), BF),
            "f_" + name: ((2, 80, w), BF),
            "n_" + name: ((2, 160, w), BF),
            "r2_" + name: ((3, 48, w), BF),
            "r1_" + name: ((3, 16, w), BF),
            "swap_" + name: ((8, w), F32),
            "got_" + name: ((8, w), F32),
        }
    for name, w in (("o", WO), ("d", WD)):
        scratch |= {
            "b_" + name: ((4, 16, 16, w), BF),
            "f_" + name: ((2, 8, 16, w), BF),
            "n_" + name: ((2, 16, 16, w), BF),
            "t2_" + name: ((16, 16, w), BF),
            "r2_" + name: ((3, 4, 16, w), BF),
            "t1_" + name: ((4, 16, w), BF),
            "r1_" + name: ((3, 16, w), BF),
        }
    scratch |= {
        "g_x1": ((2, D, WX1), BF),
        "g_z1": ((2, D, WZ1), BF),
        "total_z2": ((160, WZ2), F32),
        "total_z1": ((160, WZ1), F32),
        "own_o": ((2, 16, WO), F32),
        "es_o": ((16, WO), BF),
        "ed_o": ((16, WO), BF),
        "s1_o": ((16, WO), BF),
        "swap_o": ((8, WO), F32),
        "got_o": ((8, WO), F32),
        "w_o": ((2, 4, 16, 16, WO), BF),
        "w_d": ((16, 4, 2, 16, WD), BF),
        "tmp": ((160, 1024), F32),
        "gain_rows": ((16, 128), F32),
        "turn": ((D, D), BF),
        "pick": ((D, HD), BF),
        "cosine": ((SPAN, 128), F32),
        "sine": ((SPAN, 128), F32),
        "rows_in": ((2, T, D), BF),
        "rows_side": ((T, D), BF),
        "bias": ((T, SPAN), F32),
        "mults": ((8, D), F32),
        "gain_sums": ((128, D), F32),
        "in_unit": ((T, D), F32),
        "normed": ((T, D), BF),
        "normed_t": ((T, D), BF),
        "k_unit": ((T, HD), F32),
        "keys": ((SPAN, HD), BF),
        "values": ((SPAN, HD), BF),
        "queries": ((HEADS, T, HD), BF),
        "q_unit": ((HEADS, T, HD), F32),
        "q_inv": ((HEADS, T, 1), F32),
        "probs": ((HEADS, T, SPAN), F32),
        "attended": ((HEADS, T, HD), BF),
        "mix_unit": ((T, D), F32),
        "mid_unit": ((T, D), F32),
        "middle": ((T, D), F32),
        "mid": ((T, D), BF),
        "mid_t": ((T, D), BF),
        "units": ((4, T, 512), BF),
        "active": ((4, T, 512), F32),
        "slope_up": ((4, T, 512), F32),
        "acc": ((T, D), F32),
        "acc_t": ((T, D), F32),
        "g_ffn": ((T, D), BF),
        "g_att": ((HEADS, T, HD), BF),
        "g_q": ((HEADS, T, HD), BF),
        "d_keys": ((SPAN, HD), F32),
        "d_values": ((SPAN, HD), F32),
        "low": ((2, 2 * T, HD), BF),
        "side": ((2, T, HD), BF),
        "onward": ((2, T, HD), BF),
        "back": ((2, T, HD), BF),
        "q_gain": ((1, HD), F32),
    }
    inside = pl.BlockSpec(memory_space=vmem)
    names = (*ins, *outs, *scratch, "send_sems", "recv_sems")
    return pl.pallas_call(
        lambda *refs: layer_kernel(names, *refs),
        out_shape=[jax.ShapeDtypeStruct(*s) for s in outs.values()],
        in_specs=[inside] * len(ins),
        out_specs=[inside] * len(outs),
        scratch_shapes=[vmem(*s) for s in scratch.values()] + [pltpu.SemaphoreType.DMA((SEMS,))] * 2,
        compiler_params=pltpu.CompilerParams(
            collective_id=0, has_side_effects=True, vmem_limit_bytes=VMEM_CAP
        ),
        name="decoder_layer",
    )(*args)


def deliver_kernel(mixed, igrad, x1, z1, o, x2, z2, d, *outs):
    outs[0][...] = mixed[...]
    outs[1][...] = igrad[...]
    outs[2][:, 0:512] = x1[0, 0:5]
    outs[2][:, 512:1024] = x1[1, 0:5]
    outs[3][...] = z1[0, 0:5, 0:256]
    outs[4][...] = z1[1, 0:5, 0:256]
    outs[5][:, 0:384] = o[0]
    outs[5][:, 384:640] = o[1, :, 0:256]
    for i in range(2):
        outs[6 + i][:, 0:1024] = x2[i, 0:5]
        outs[6 + i][:, 1024:2048] = z2[i, 0:5]
    outs[8][...] = d[...]
    gains = z1[0, :, 256:384].T
    for at, row, n in ((9, 0, 5), (10, 4, 2), (11, 5, 2), (12, 1, 5), (13, 2, 5), (14, 3, 5)):
        outs[at][...] = gains[row : row + 1, 0:n].reshape(n)


def deliver(*parts):
    inside = pl.BlockSpec(memory_space=pltpu.VMEM)
    shapes = [(T, D), (5, 1024), (5, 256), (5, 256), (8, D), (5, 2048), (5, 2048), (16, D)]
    shapes += [(5,), (2,), (2,), (5,), (5,), (5,)]
    return pl.pallas_call(
        deliver_kernel,
        out_shape=[jax.ShapeDtypeStruct((T, D), BF)] + [jax.ShapeDtypeStruct(s, F32) for s in shapes],
        in_specs=[inside] * len(parts),
        out_specs=[inside] * 15,
        name="deliver",
    )(*parts)


def per_device(
    hidden_in,
    query_weight,
    key_weight,
    value_weight,
    output_weight,
    gate_weight,
    up_weight,
    down_weight,
    input_gain,
    query_gain,
    key_gain,
    mixer_gain,
    middle_gain,
    output_gain,
    seq_lengths,
    out_grad,
):
    gains = (input_gain, mixer_gain, middle_gain, output_gain, query_gain, key_gain)
    parts = layer(
        hidden_in,
        query_weight,
        key_weight,
        value_weight,
        output_weight,
        gate_weight,
        up_weight,
        down_weight,
        *[a.reshape(1, -1) for a in gains],
        seq_lengths.reshape(1, 64),
        out_grad,
    )
    return tuple(deliver(*parts))


def solution(mesh):
    return jax.shard_map(
        per_device,
        mesh=mesh,
        in_specs=(
            P("dp", None),
            P("dp", None),
            P("dp", None),
            P("dp", None),
            P("dp", None),
            P("dp", None),
            P("dp", None),
            P("dp", None),
            P("dp"),
            P("dp"),
            P("dp"),
            P("dp"),
            P("dp"),
            P("dp"),
            P(),
            P("dp", None),
        ),
        out_specs=(
            P("dp", None),
            P("dp", None),
            P("dp", None),
            P("dp", None),
            P("dp", None),
            P("dp", None),
            P("dp", None),
            P("dp", None),
            P("dp", None),
            P("dp"),
            P("dp"),
            P("dp"),
            P("dp"),
            P("dp"),
            P("dp"),
        ),
        check_vma=False,
    )
```

```python
import math

import jax
import jax.numpy as jnp
from jax import lax
from jax.experimental import pallas as pl
from jax.experimental.pallas import tpu as pltpu
from jax.sharding import PartitionSpec as P

MESH = pl.DeviceIdType.MESH
BF = jnp.bfloat16
F32 = jnp.float32
T = 256
D = 640
HD = 256
HEADS = 4
SPAN = 3 * T
WINDOW = 512
EPSILON = 1e-06
ROPE_BASE = 10000.0
NEG_FILL = -1e30
SCALE = 1.0 / math.sqrt(HD)
GELU_A = math.sqrt(2.0 / math.pi)
GELU_B = 0.044715
WX1, WZ1, WX2, WZ2, WD, WO = 512, 384, 1024, 1024, 640, 384
SEMS = 232
GAINS = ("n_in", "n_mix", "n_mid", "n_out", "n_q", "n_k")
VMEM_CAP = 62 << 20


def place(x, z, y, c):
    return ((x % 4) * 4 + (z % 4)) * 8 + (y % 4) * 2 + c


class Links:
    def __init__(self, send_sems, recv_sems):
        self.me = lax.axis_index("dp")
        self.at = {"x": self.me // 32, "z": (self.me // 8) % 4, "y": (self.me // 2) % 4}
        self.core = self.me % 2
        self.other = 1 - self.core
        self.sib = place(self.at["x"], self.at["z"], self.at["y"], self.other)
        self.xz = self.at["x"] * 4 + self.at["z"]
        self.send_sems, self.recv_sems, self.used, self.open = send_sems, recv_sems, 0, []

    def peer(self, axis, steps):
        moved = dict(self.at)
        moved[axis] = moved[axis] + steps
        return place(moved["x"], moved["z"], moved["y"], self.core)

    def along(self, steps):
        return (self.me + 128 + steps) % 128

    def slot(self, axis, steps):
        return (self.at[axis] + steps) % 4

    def greet(self):
        sem = pltpu.get_barrier_semaphore()
        partners = [self.sib] + [self.along(s) for s in (2, -2)]
        for axis in ("x", "z", "y"):
            partners += [self.peer(axis, o) for o in (1, 2, 3)]
        for p in partners:
            pl.semaphore_signal(sem, inc=1, device_id=(p,), device_id_type=MESH)
        self.greeted = len(partners)

    def meet(self):
        pl.semaphore_wait(pltpu.get_barrier_semaphore(), self.greeted)

    def send(self, src, dst, target):
        i = self.used
        self.used += 1
        copy = pltpu.make_async_remote_copy(
            src_ref=src,
            dst_ref=dst,
            send_sem=self.send_sems.at[i],
            recv_sem=self.recv_sems.at[i],
            device_id=(target,),
            device_id_type=MESH,
        )
        copy.start()
        self.open.append(copy.wait_send)
        return copy

    def local(self, src, dst):
        i = self.used
        self.used += 1
        copy = pltpu.make_async_copy(src, dst, self.send_sems.at[i])
        copy.start()
        return copy

    def finish(self):
        for wait in self.open:
            wait()
        self.open = []


class Rows:
    def __init__(self, net, axes, width, refs):
        self.net, self.axes, self.width = net, axes, width
        self.own, self.e_src, self.e_dst, self.s1, self.s2, self.b3, self.w, self.tmp = refs
        self.ends = []

    def view(self, slot, at, n):
        rows = pl.ds(pl.multiple_of(slot * 160 + at * 16, 16), n * 16)
        return self.w.at[self.net.core, rows]

    def step0(self):
        self.e_src[...] = self.own[self.net.other].astype(BF)

    def step0b(self):
        self.swap = self.net.send(self.e_src, self.e_dst, self.net.sib)

    def step1(self):
        net, wide = self.net, slice(0, self.width)
        self.swap.wait_recv()
        mine = self.own[net.core][0:5]
        theirs = self.e_dst[...].astype(F32)[0:5]
        first = net.core == 0
        self.tmp[0:5, wide] = jnp.where(first, mine, theirs)
        self.tmp[5:10, wide] = jnp.where(first, theirs, mine)
        slot = self.s1.at[net.at[self.axes[0]]]
        slot[...] = self.tmp[0:16, wide].astype(BF)
        self.p = [net.send(slot, slot, net.peer(self.axes[0], o)) for o in (1, 2, 3)]

    def step2(self):
        net, wide = self.net, slice(0, self.width)
        for copy in self.p:
            copy.wait_recv()
        for j in range(4):
            self.tmp[10 * j : 10 * j + 10, wide] = self.s1[j].astype(F32)[0:10]
        slot = self.s2.at[net.at[self.axes[1]]]
        slot[...] = self.tmp[0:48, wide].astype(BF)
        self.p = [net.send(slot, slot, net.peer(self.axes[1], o)) for o in (1, 2, 3)]

    def step3(self):
        net, wide = self.net, slice(0, self.width)
        for copy in self.p:
            copy.wait_recv()
        for j in range(4):
            self.tmp[40 * j : 40 * j + 40, wide] = self.s2[j].astype(F32)[0:40]
        self.b3[...] = self.tmp[0:160, wide].astype(BF)
        axis = self.axes[2]
        dst = self.view(net.at[axis], 0, 10)
        self.up = net.send(self.b3, dst, net.peer(axis, 1))
        self.down = net.send(self.b3, dst, net.peer(axis, 3))
        self.ends.append(net.send(self.b3, dst, net.sib).wait_recv)
        self.ends.append(net.local(self.b3, dst).wait)

    blocks = 10

    def step4(self):
        net, axis, n = self.net, self.axes[2], self.blocks
        half = n // 2
        self.up.wait_recv()
        part = self.view(net.slot(axis, 3), 0, half)
        self.far_up = net.send(part, part, net.peer(axis, 1))
        self.down.wait_recv()
        part = self.view(net.slot(axis, 1), half, half)
        self.far_down = net.send(part, part, net.peer(axis, 3))
        for steps in (3, 1):
            whole = self.view(net.slot(axis, steps), 0, n)
            self.ends.append(net.send(whole, whole, net.sib).wait_recv)

    def step5(self):
        net, axis, half = self.net, self.axes[2], self.blocks // 2
        for copy, at in ((self.far_up, 0), (self.far_down, half)):
            copy.wait_recv()
            part = self.view(net.slot(axis, 2), at, half)
            self.ends.append(net.send(part, part, net.sib).wait_recv)

    def step6(self):
        for wait in self.ends:
            wait()


class Tiles(Rows):
    blocks = 16

    def __init__(self, net, axes, w, by_core):
        self.net, self.axes, self.w, self.by_core = net, axes, w, by_core
        self.ends = []

    def view(self, slot, at, n):
        if self.by_core:
            return self.w.at[pl.ds(at, n), slot, self.net.core]
        return self.w.at[self.net.core, slot, pl.ds(at, n)]

    def first(self, src):
        net = self.net
        a, b, c = (net.at[axis] for axis in self.axes)
        dst = self.w.at[b * 4 + a, c, net.core] if self.by_core else self.w.at[net.core, c, b * 4 + a]
        self.p = [net.send(src, dst, net.peer(self.axes[0], o)) for o in (1, 2, 3)]
        self.kept = net.local(src, dst)

    def step2(self):
        net = self.net
        for copy in self.p:
            copy.wait_recv()
        self.kept.wait()
        part = self.view(net.at[self.axes[2]], net.at[self.axes[1]] * 4, 4)
        self.p = [net.send(part, part, net.peer(self.axes[1], o)) for o in (1, 2, 3)]

    def step3(self):
        net, axis = self.net, self.axes[2]
        for copy in self.p:
            copy.wait_recv()
        part = self.view(net.at[axis], 0, 16)
        self.up = net.send(part, part, net.peer(axis, 1))
        self.down = net.send(part, part, net.peer(axis, 3))
        self.ends.append(net.send(part, part, net.sib).wait_recv)


class RowSums:
    blocks = 10

    def __init__(self, net, axes, width, refs):
        self.net, self.axes, self.width = net, axes, width
        (self.g, self.b, self.f, self.n, self.t2, self.r2, self.t1, self.r1, self.total) = refs[:9]
        self.rest = refs[9:]
        self.swaps, self.onward, self.near = {}, {}, {}

    def view(self, steps, at, n, which):
        slot = self.net.slot(self.axes[2], steps)
        rows = pl.ds(pl.multiple_of(slot * 160 + at * 16, 16), n * 16)
        return self.g.at[which, rows]

    def rows(self, at, n):
        return pl.ds(at * 16, n * 16)

    def tile(self, steps, i):
        slot = self.net.slot(self.axes[2], steps)
        return (self.net.core, pl.ds(pl.multiple_of(slot * 160 + i * 16, 16), 16))

    def block(self, i):
        return pl.ds(pl.multiple_of(i * 16, 16), 16)

    def give(self, steps):
        src = self.view(steps, 0, self.blocks, self.net.other)
        self.swaps[steps] = self.net.send(src, self.b.at[steps], self.net.sib)

    def add(self, steps, held, at, count):
        def body(i, carry):
            where = self.tile(steps, i + at)
            self.g[where] = self.g[where] + held[self.block(i)]
            return carry

        lax.fori_loop(0, count, body, 0)

    def take(self, steps):
        net, axis, n, core = self.net, self.axes[2], self.blocks, self.net.core
        half = n // 2
        self.swaps[steps].wait_recv()
        if steps == 0:
            return
        self.add(steps, self.b.at[steps], 0, n)
        if steps == 2:
            self.onward[1] = net.send(self.view(2, 0, half, core), self.f.at[0], net.peer(axis, 1))
            self.onward[3] = net.send(self.view(2, half, half, core), self.f.at[1], net.peer(axis, 3))
        elif steps == 1:
            self.near["a"] = net.send(
                self.view(1, half, half, core), self.n.at[0, self.rows(half, half)], net.peer(axis, 1)
            )
        else:
            self.near["b"] = net.send(
                self.view(3, 0, half, core), self.n.at[1, self.rows(0, half)], net.peer(axis, 3)
            )

    def step2(self):
        net, axis, core = self.net, self.axes[2], self.net.core
        half = self.blocks // 2
        self.onward[1].wait_recv()
        self.add(1, self.f.at[0], 0, half)
        self.near["c"] = net.send(self.view(1, 0, half, core), self.n.at[0, self.rows(0, half)], net.peer(axis, 1))
        self.onward[3].wait_recv()
        self.add(3, self.f.at[1], half, half)
        self.near["d"] = net.send(
            self.view(3, half, half, core), self.n.at[1, self.rows(half, half)], net.peer(axis, 3)
        )

    def total3(self, i):
        at = self.block(i)
        own = self.g[self.tile(0, i)].astype(F32) + self.b[0, at].astype(F32)
        return own + self.n[0, at].astype(F32) + self.n[1, at].astype(F32)

    def step3(self):
        net, width, axis = self.net, self.width, self.axes[1]
        for part in "abcd":
            self.near[part].wait_recv()

        def body(i, carry):
            self.total[self.block(i), 0 : self.width] = self.total3(i)
            return carry

        lax.fori_loop(0, 10, body, 0)
        for j in range(4):
            part = self.total[40 * j : 40 * j + 40, 0:width]
            self.t2[j] = jnp.concatenate([part, jnp.zeros((8, width), F32)], axis=0).astype(BF)
        self.p = [net.send(self.t2.at[net.slot(axis, o)], self.r2.at[o - 1], net.peer(axis, o)) for o in (1, 2, 3)]

    def step4(self):
        net, width, axis = self.net, self.width, self.axes[0]
        for copy in self.p:
            copy.wait_recv()
        own = self.t2[net.at[self.axes[1]]].astype(F32)
        for o in range(3):
            own = own + self.r2[o].astype(F32)
        self.total[0:48, 0:width] = own
        for j in range(4):
            part = self.total[10 * j : 10 * j + 10, 0:width]
            self.t1[j] = jnp.concatenate([part, jnp.zeros((6, width), F32)], axis=0).astype(BF)
        self.p = [net.send(self.t1.at[net.slot(axis, o)], self.r1.at[o - 1], net.peer(axis, o)) for o in (1, 2, 3)]

    def step5(self):
        net = self.net
        swap, got, out = self.rest
        for copy in self.p:
            copy.wait_recv()
        own = self.t1[net.at[self.axes[0]]].astype(F32)
        for o in range(3):
            own = own + self.r1[o].astype(F32)
        self.total[0:16, 0 : self.width] = own
        low_rows = self.total[0:8, 0 : self.width]
        high_rows = self.total[5:13, 0 : self.width]
        first = net.core == 0
        swap[...] = jnp.where(first, high_rows, low_rows)
        out[net.core] = jnp.where(first, low_rows, high_rows)
        self.last = net.send(swap, got, net.sib)

    def step6(self):
        swap, got, out = self.rest
        self.last.wait_recv()
        out[self.net.other] = got[...]


class TileSums(RowSums):
    blocks = 16

    def __init__(self, net, axes, width, by_core, refs):
        self.by_core = by_core
        super().__init__(net, axes, width, refs)

    def view(self, steps, at, n, which):
        slot = self.net.slot(self.axes[2], steps)
        if self.by_core:
            return self.g.at[pl.ds(at, n), slot, which]
        return self.g.at[which, slot, pl.ds(at, n)]

    def rows(self, at, n):
        return pl.ds(at, n)

    def tile(self, steps, i):
        slot = self.net.slot(self.axes[2], steps)
        return (i, slot, self.net.core) if self.by_core else (self.net.core, slot, i)

    def block(self, i):
        return i

    def step3(self):
        net = self.net
        for part in "abcd":
            self.near[part].wait_recv()

        def body(i, carry):
            self.t2[i] = self.total3(i).astype(BF)
            return carry

        lax.fori_loop(0, 16, body, 0)
        self.p = [
            net.send(
                self.t2.at[pl.ds(net.slot(self.axes[1], o) * 4, 4)], self.r2.at[o - 1], net.peer(self.axes[1], o)
            )
            for o in (1, 2, 3)
        ]

    def step4(self):
        net = self.net
        for copy in self.p:
            copy.wait_recv()
        for j in range(4):
            value = self.t2[net.at[self.axes[1]] * 4 + j].astype(F32)
            for o in range(3):
                value = value + self.r2[o, j].astype(F32)
            self.t1[j] = value.astype(BF)
        axis = self.axes[0]
        self.p = [net.send(self.t1.at[net.slot(axis, o)], self.r1.at[o - 1], net.peer(axis, o)) for o in (1, 2, 3)]

    def step5(self):
        net = self.net
        for copy in self.p:
            copy.wait_recv()
        own = self.t1[net.at[self.axes[0]]].astype(F32)
        for o in range(3):
            own = own + self.r1[o].astype(F32)
        if self.by_core:
            self.rest[0][...] = own
            return
        swap, got, out = self.rest
        first = net.core == 0
        swap[...] = jnp.where(first, own[8:16], own[0:8])
        out[net.core] = jnp.where(first, own[0:8], own[8:16])
        self.last = net.send(swap, got, net.sib)

    def step6(self):
        if not self.by_core:
            super().step6()


def mm(left, right):
    return jnp.dot(left, right, preferred_element_type=F32)


def mm_t(left, right):
    return lax.dot_general(left, right, (((1,), (1,)), ((), ())), preferred_element_type=F32)


def t_mm(left, right):
    return lax.dot_general(left, right, (((0,), (0,)), ((), ())), preferred_element_type=F32)


def inv_of(values):
    return lax.rsqrt(jnp.mean(values * values, axis=-1, keepdims=True) + EPSILON)


def norm_back(upstream, unit_rows, inv_rms):
    return inv_rms * (upstream - unit_rows * jnp.mean(unit_rows * upstream, axis=-1, keepdims=True))


def spin(values, cosine, sine):
    a, b = values[:, :128], values[:, 128:]
    return jnp.concatenate([a * cosine - b * sine, b * cosine + a * sine], axis=1)


def spin_back(values, cosine, sine):
    a, b = values[:, :128], values[:, 128:]
    return jnp.concatenate([a * cosine + b * sine, b * cosine - a * sine], axis=1)


def count(shape, dim):
    return lax.broadcasted_iota(jnp.int32, shape, dim)


def hot(condition):
    return jnp.where(condition, 1.0, 0.0).astype(BF)


def split_dot(value, fixed):
    high = value.astype(BF)
    low = (value - high.astype(F32)).astype(BF)
    return mm_t(high, fixed) + mm_t(low, fixed)


class Refs:
    pass


def gather_setup(net, r):
    for ref in (r.own_x1, r.own_z1, r.own_x2, r.own_z2, r.own_o):
        ref[...] = jnp.zeros_like(ref)
    q = r.q[...].astype(F32)
    r.own_x1[0, 0:5] = q[:, 0:512]
    r.own_x1[1, 0:5] = q[:, 512:1024]
    r.gain_rows[...] = jnp.zeros_like(r.gain_rows)
    for i, gain in enumerate((r.n_in, r.n_mix, r.n_mid, r.n_out, r.n_q, r.n_k)):
        r.gain_rows[i : i + 1, 0 : gain.shape[1]] = gain[...].astype(F32)
    tile = t_mm(r.gain_rows[...].astype(BF), hot(count((16, 128), 0) == count((16, 128), 1)))
    r.own_z1[0, 0:5, 256:384] = tile[0:5]
    r.own_z1[0, 0:5, 0:256] = r.k[...].astype(F32)
    r.own_z1[1, 0:5, 0:256] = r.v[...].astype(F32)
    g, u = r.g[...].astype(F32), r.u[...].astype(F32)
    r.own_x2[0, 0:5] = g[:, 0:1024]
    r.own_x2[1, 0:5] = u[:, 0:1024]
    r.own_z2[0, 0:5] = g[:, 1024:2048]
    r.own_z2[1, 0:5] = u[:, 1024:2048]
    o = r.o[...].astype(F32)
    r.own_o[0, 0:8] = o[:, 0:384]
    r.own_o[1, 0:8, 0:256] = o[:, 384:640]

    def rows(name, axes, width):
        names = ("own_", "es_", "ed_", "s1_", "s2_", "b3_", "w_")
        return Rows(net, axes, width, [getattr(r, n + name) for n in names] + [r.tmp])

    x1 = rows("x1", ("y", "z", "x"), WX1)
    z1 = rows("z1", ("x", "y", "z"), WZ1)
    x2 = rows("x2", ("y", "z", "x"), WX2)
    z2 = rows("z2", ("x", "y", "z"), WZ2)
    for s in (x1, z1, x2, z2):
        s.step0()
    r.es_o[...] = r.own_o[net.other].astype(BF)
    return x1, z1, x2, z2, Tiles(net, ("y", "x", "z"), r.w_o, False), Tiles(net, ("z", "x", "y"), r.w_d, True)


def layer_kernel(names, *refs):
    r = Refs()
    for name, ref in zip(names, refs):
        setattr(r, name, ref)
    r.g_x2, r.g_z2, r.g_d, r.g_o = r.w_x2, r.w_z2, r.w_d, r.w_o
    for name in ("x1", "z1", "x2", "z2"):
        setattr(r, "t2_" + name, getattr(r, "s2_" + name))
        setattr(r, "t1_" + name, getattr(r, "s1_" + name))
    r.total_x2 = r.total_x1 = r.total_o = r.total_d = r.tmp
    r.g_middle = r.igrad
    net = Links(r.send_sems, r.recv_sems)
    net.greet()
    x1, z1, x2, z2, ow, dw = gather_setup(net, r)
    r.rows_in[0] = r.h[...]
    net.meet()
    x1.step0b()
    z1.step0b()
    swap_o = net.send(r.es_o, r.ed_o, net.sib)
    x2.step0b()
    z2.step0b()
    x1.step1()
    z1.step1()
    swap_o.wait_recv()
    mine, theirs = r.own_o[net.core][0:8], r.ed_o[...].astype(F32)[0:8]
    r.tmp[0:8, 0:WO] = jnp.where(net.core == 0, mine, theirs)
    r.tmp[8:16, 0:WO] = jnp.where(net.core == 0, theirs, mine)
    r.s1_o[...] = r.tmp[0:16, 0:WO].astype(BF)
    ow.first(r.s1_o)
    x2.step1()
    z2.step1()
    dw.first(r.d)

    k_dim, j_dim = count((D, D), 0), count((D, D), 1)
    tens = (j_dim * 52429) >> 19
    source = (tens & 3) * 160 + (tens >> 4) * 40 + ((tens >> 2) & 3) * 10 + (j_dim - 10 * tens)
    r.turn[...] = hot(k_dim == source)
    spot = count((64, 64), 0)
    lens = jnp.broadcast_to(r.lens[...].astype(F32), (64, 64))
    column = jnp.sum(jnp.where(spot == count((64, 64), 1), lens, 0.0), axis=1, keepdims=True)
    ends = jnp.sum(jnp.where(spot <= count((64, 64), 1), column, 0.0), axis=0, keepdims=True)
    offset = net.me * T
    token = (count((SPAN, 64), 0) + (offset - 2 * T)).astype(F32)
    start = jnp.max(jnp.where(ends <= token, ends, 0.0), axis=1, keepdims=True)
    position = token[:, 0:1] - start
    pair = count((1, 128), 1).astype(F32)
    angle = position * jnp.exp(pair * (-2.0 * math.log(ROPE_BASE) / HD))
    r.cosine[...] = jnp.cos(angle)
    r.sine[...] = jnp.sin(angle)
    ahead = count((T, SPAN), 1) - 2 * T
    distance = count((T, SPAN), 0) - ahead
    inside = (distance >= 0) & (distance < WINDOW) & ((ahead + offset).astype(F32) >= start[2 * T :])
    r.bias[...] = jnp.where(inside, 0.0, NEG_FILL)
    hidden = r.h[...].astype(F32)
    input_inv = inv_of(hidden)
    r.in_unit[...] = hidden * input_inv

    early, late = (x1, z1, ow), (x2, z2, dw)
    for s in early:
        s.step2()
    for s in late:
        s.step2()
    ahead_copy = net.send(r.rows_in.at[0], r.rows_in.at[1], net.along(2))
    for s in (*early, *late):
        s.step3()
    ahead_copy.wait_recv()
    side_copy = net.send(r.rows_in.at[net.core], r.rows_side, net.sib)
    for s in (*early, *late):
        s.step4()
    for s in early:
        s.step5()
    x1.step6()
    z1.step6()

    gain_rows = lax.dot_general(
        r.w_z1[0, :, 256:384], r.turn[...], (((0,), (1,)), ((), ())), preferred_element_type=F32
    )
    far, near = count((D, HD), 0), count((D, HD), 1)
    r.pick[...] = hot(far == 5 * (near >> 1) + (near & 1))
    head_rows = mm(gain_rows.astype(BF), r.pick[...])
    r.mults[0:4] = 1.0 + gain_rows[0:4]
    r.mults[4:6, 0:HD] = 1.0 + head_rows[4:6]
    normed = (r.in_unit[...] * r.mults[0:1]).astype(BF)
    r.normed[...] = normed
    turned = mm(normed, r.turn[...]).astype(BF)
    r.normed_t[...] = turned
    cosine, sine = r.cosine[2 * T :], r.sine[2 * T :]
    for h in range(HEADS):
        raw = mm(normed, r.w_x1[h // 2, :, 256 * (h % 2) : 256 * (h % 2) + 256])
        inv = inv_of(raw)
        r.q_inv[h] = inv
        r.q_unit[h] = raw * inv
        r.queries[h] = spin(raw * inv * r.mults[4:5, 0:HD], cosine, sine).astype(BF)
    side_copy.wait_recv()
    for i in range(3):
        some = slice(T * i, T * i + T)
        if i < 2:
            rows = (r.rows_in[1] if i == 0 else r.rows_side[...]).astype(F32)
            here = (rows * inv_of(rows) * r.mults[0:1]).astype(BF)
            there = mm(here, r.turn[...]).astype(BF)
        else:
            there = turned
        key_raw = mm(there, r.w_z1[0, :, 0:256])
        key_inv = inv_of(key_raw)
        key_unit = key_raw * key_inv
        r.keys[some] = spin(key_unit * r.mults[5:6, 0:HD], r.cosine[some], r.sine[some]).astype(BF)
        r.values[some] = mm(there, r.w_z1[1, :, 0:256]).astype(BF)
    r.k_unit[...] = key_unit
    for s in late:
        s.step5()

    def attend(h):
        scores = mm_t(r.queries[h], r.keys[...]) * SCALE + r.bias[...]
        row_max = jnp.max(scores, axis=1, keepdims=True)
        weights = jnp.exp(scores - row_max)
        probs = weights / jnp.sum(weights, axis=1, keepdims=True)
        r.probs[h] = probs
        r.attended[h] = mm(probs.astype(BF), r.values[...]).astype(BF)

    for h in range(HEADS):
        attend(h)

    ow.step6()
    left = jnp.zeros((T, 384), F32)
    right = jnp.zeros((T, 256), F32)
    for h in range(HEADS):
        some = slice(4 * h, 4 * h + 4)
        left = left + mm(r.attended[h], r.w_o[0, :, some].reshape(256, WO))
        right = right + mm(r.attended[h], r.w_o[1, :, some].reshape(256, WO)[:, 0:256])
    mixer_out = jnp.concatenate([left, right], axis=1)
    mixer_inv = inv_of(mixer_out)
    r.mix_unit[...] = mixer_out * mixer_inv
    middle = r.h[...].astype(F32) + r.mix_unit[...] * r.mults[1:2]
    middle_inv = inv_of(middle)
    r.mid_unit[...] = middle * middle_inv
    r.middle[...] = middle
    r.mid[...] = (r.mid_unit[...] * r.mults[2:3]).astype(BF)
    r.mid_t[...] = mm(r.mid[...], r.turn[...]).astype(BF)
    for s in late:
        s.step6()

    r.acc[...] = jnp.zeros_like(r.acc)
    for w, rows_in, first in ((r.w_x2, r.mid, 0), (r.w_z2, r.mid_t, 2)):

        def forward(j, carry, w=w, rows_in=rows_in, first=first):
            cols = slice(512 * j, 512 * j + 512)
            gate = mm(rows_in[...], w[0, :, cols])
            up = mm(rows_in[...], w[1, :, cols])
            square = gate * gate
            tanh = jnp.tanh(GELU_A * gate * (1.0 + GELU_B * square))
            active = 0.5 * gate * (1.0 + tanh)
            slope = 0.5 * (1.0 + tanh) + 0.5 * gate * (1.0 - tanh * tanh) * (
                GELU_A * (1.0 + 3.0 * GELU_B * square)
            )
            units = (active * up).astype(BF)
            part = first + j
            r.units[part] = units
            r.active[part] = active
            r.slope_up[part] = slope * up
            r.acc[...] += mm(units, r.w_d[4 * part : 4 * part + 4].reshape(512, D))
            return carry

        for j in range(2):
            forward(j, 0)
    ffn_out = r.acc[...]
    ffn_inv = inv_of(ffn_out)
    ffn_unit = ffn_out * ffn_inv
    r.mixed[...] = (r.middle[...] + ffn_unit * r.mults[3:4]).astype(BF)
    grad_out = r.og[...].astype(F32)
    r.gain_sums[...] = jnp.zeros_like(r.gain_sums)
    r.gain_sums[3:4] = jnp.sum(grad_out * ffn_unit, axis=0, keepdims=True)
    r.g_ffn[...] = norm_back(grad_out * r.mults[3:4], ffn_unit, ffn_inv).astype(BF)
    net.finish()

    def sums(kind, name, *args):
        tags = ("g_", "b_", "f_", "n_", "t2_", "r2_", "t1_", "r1_", "total_", "swap_", "got_", "out_")
        if name == "d":
            tags = tags[:9] + tags[11:]
        return kind(net, *args, [getattr(r, tag + name) for tag in tags])

    sx1 = sums(RowSums, "x1", ("y", "z", "x"), WX1)
    sz1 = sums(RowSums, "z1", ("x", "y", "z"), WZ1)
    sx2 = sums(RowSums, "x2", ("y", "z", "x"), WX2)
    sz2 = sums(RowSums, "z2", ("x", "y", "z"), WZ2)
    so = sums(TileSums, "o", ("y", "x", "z"), WO, False)
    sd = sums(TileSums, "d", ("z", "x", "y"), WD, True)
    wide = (sx2, sz2, sd)
    for w, g, rows_in, first, total in (
        (r.w_x2, r.g_x2, r.mid, 0, r.acc),
        (r.w_z2, r.g_z2, r.mid_t, 2, r.acc_t),
    ):
        total[...] = jnp.zeros_like(total)

        def backward(j, carry, w=w, g=g, rows_in=rows_in, first=first, total=total):
            cols = slice(512 * j, 512 * j + 512)
            part = first + j
            some = slice(4 * part, 4 * part + 4)
            g_ffn = r.g_ffn[...]
            grad_hidden = mm_t(g_ffn, r.w_d[some].reshape(512, D))
            r.g_d[some] = t_mm(r.units[part], g_ffn).astype(BF).reshape(4, 4, 2, 16, D)
            grad_gate = (grad_hidden * r.slope_up[part]).astype(BF)
            grad_up = (grad_hidden * r.active[part]).astype(BF)
            total[...] += mm_t(grad_gate, w[0, :, cols]) + mm_t(grad_up, w[1, :, cols])
            g[0, :, cols] = t_mm(rows_in[...], grad_gate).astype(BF)
            g[1, :, cols] = t_mm(rows_in[...], grad_up).astype(BF)
            return carry

        for j in range(2):
            backward(j, 0)
        if first == 0:
            for steps in (2, 1, 3, 0):
                sx2.give(steps)
    for steps in (2, 1, 3, 0):
        sz2.give(steps)
        sd.give(steps)

    grad_in = r.acc[...] + split_dot(r.acc_t[...], r.turn[...])
    mid_unit = r.mid_unit[...]
    r.gain_sums[2:3] = jnp.sum(grad_in * mid_unit, axis=0, keepdims=True)
    grad_middle = r.og[...].astype(F32) + norm_back(grad_in * r.mults[2:3], mid_unit, inv_of(r.middle[...]))
    r.g_middle[...] = grad_middle
    mix_unit = r.mix_unit[...]
    r.gain_sums[1:2] = jnp.sum(grad_middle * mix_unit, axis=0, keepdims=True)
    grad_mixer = norm_back(grad_middle * r.mults[1:2], mix_unit, mixer_inv).astype(BF)
    for s in wide:
        s.take(2)
    for h in range(HEADS):
        some = slice(4 * h, 4 * h + 4)
        r.g_att[h] = (
            mm_t(grad_mixer[:, 0:384], r.w_o[0, :, some].reshape(256, WO))
            + mm_t(grad_mixer[:, 384:640], r.w_o[1, :, some].reshape(256, WO)[:, 0:256])
        ).astype(BF)
        grad = t_mm(r.attended[h], grad_mixer).astype(BF)
        r.g_o[0, :, some] = grad[:, 0:384].reshape(4, 4, 16, 384)
        r.g_o[1, :, some, :, 0:256] = grad[:, 384:640].reshape(4, 4, 16, 256)
    for steps in (2, 1, 3, 0):
        so.give(steps)
    r.d_values[...] = t_mm(r.probs[0].astype(BF), r.g_att[0])
    for h in range(1, HEADS):
        r.d_values[...] += t_mm(r.probs[h].astype(BF), r.g_att[h])

    def halo_aside(i, whole, scale):
        r.low[i] = (whole[0 : 2 * T] * scale).astype(BF)
        return net.send(r.low.at[i, pl.ds(T, T)], r.side.at[i], net.sib)

    def halo_back(i, copy):
        copy.wait_recv()
        far = r.low[i, 0:T]
        r.onward[i] = jnp.where(net.core == 1, far + r.side[i], far)
        return net.send(r.onward.at[i], r.back.at[i], net.along(-2))

    def halo_sum(i, whole, scale, copy):
        copy.wait_recv()
        side = jnp.where(net.core == 0, r.side[i].astype(F32), 0.0)
        return whole[2 * T :] * scale + r.back[i].astype(F32) + side

    aside_v = halo_aside(1, r.d_values, 1.0)
    for s in wide:
        s.take(1)

    r.d_keys[...] = jnp.zeros_like(r.d_keys)
    r.q_gain[...] = jnp.zeros_like(r.q_gain)

    def attend_back(h):
        probs = r.probs[h]
        grad_probs = mm_t(r.g_att[h], r.values[...])
        delta = jnp.sum(probs * grad_probs, axis=1, keepdims=True)
        grad_scores = probs * (grad_probs - delta)
        r.probs[h] = grad_scores
        r.d_keys[...] += t_mm(grad_scores.astype(BF), r.queries[h])

    def query_back(h):
        grad_q = mm(r.probs[h].astype(BF), r.keys[...]) * SCALE
        back = spin_back(grad_q, cosine, sine)
        unit = r.q_unit[h]
        r.q_gain[...] += jnp.sum(back * unit, axis=0, keepdims=True)
        r.g_q[h] = norm_back(back * r.mults[4:5, 0:HD], unit, r.q_inv[h]).astype(BF)

    attend_back(0)
    back_v = halo_back(1, aside_v)
    for s in (sx2, sz2):
        s.take(3)
    for h in range(1, HEADS):
        attend_back(h)
    aside_k = halo_aside(0, r.d_keys, SCALE)

    normed, turned = r.normed[...], r.normed_t[...]
    query_back(0)
    back_k = halo_back(0, aside_k)
    for h in range(1, HEADS):
        query_back(h)
    for h in range(HEADS):
        r.g_x1[h // 2, :, 256 * (h % 2) : 256 * (h % 2) + 256] = t_mm(normed, r.g_q[h]).astype(BF)
    for steps in (2, 1, 3, 0):
        sx1.give(steps)
    sd.take(3)
    for steps in (2, 1, 3):
        so.take(steps)
    for s in wide:
        s.step2()
    for steps in (2, 1, 3):
        sx1.take(steps)
    own_v = halo_sum(1, r.d_values, 1.0, back_v)
    grad_v = own_v.astype(BF)
    r.g_z1[1, :, 0:256] = t_mm(turned, grad_v).astype(BF)
    r.g_z1[1, :, 256:384] = jnp.zeros((D, 128), BF)
    grad_natural = mm_t(r.g_q[0], r.w_x1[0, :, 0:256])
    for h in range(1, HEADS):
        grad_natural = grad_natural + mm_t(r.g_q[h], r.w_x1[h // 2, :, 256 * (h % 2) : 256 * (h % 2) + 256])
    r.acc[...] = grad_natural
    r.acc_t[...] = mm_t(grad_v, r.w_z1[1, :, 0:256])
    own_k = halo_sum(0, r.d_keys, SCALE, back_k)
    key_back = spin_back(own_k, cosine, sine)
    k_unit = r.k_unit[...]
    key_gain = jnp.sum(key_back * k_unit, axis=0, keepdims=True)
    grad_k = norm_back(key_back * r.mults[5:6, 0:HD], k_unit, key_inv).astype(BF)
    r.g_z1[0, :, 0:256] = t_mm(turned, grad_k).astype(BF)
    grad_turned = r.acc_t[...] + mm_t(grad_k, r.w_z1[0, :, 0:256])
    grad_normed = r.acc[...] + split_dot(grad_turned, r.turn[...])
    in_unit = r.in_unit[...]
    r.gain_sums[0:1] = jnp.sum(grad_normed * in_unit, axis=0, keepdims=True)
    both = jnp.concatenate([r.q_gain[...], key_gain, jnp.zeros((6, HD), F32)], axis=0).astype(BF)
    r.gain_sums[4:6] = mm_t(both, r.pick[...])[0:2]
    r.g_z1[0, :, 256:384] = lax.dot_general(
        r.turn[...], r.gain_sums[...].astype(BF), (((0,), (1,)), ((), ())), preferred_element_type=F32
    ).astype(BF)
    for steps in (2, 1, 3, 0):
        sz1.give(steps)
    so.step2()
    for steps in (2, 1, 3):
        sz1.take(steps)
    for s in wide:
        s.take(0)
        s.step3()
    sx1.step2()
    r.igrad[...] = r.g_middle[...] + norm_back(grad_normed * r.mults[0:1], in_unit, input_inv)
    sz1.step2()
    so.take(0)
    so.step3()
    for s in wide:
        s.step4()
    sx1.take(0)
    sx1.step3()
    sz1.take(0)
    sz1.step3()
    so.step4()
    for s in wide:
        s.step5()
    sx1.step4()
    sz1.step4()
    so.step5()
    sx1.step5()
    for s in wide:
        s.step6()
    sz1.step5()
    so.step6()
    sx1.step6()
    sz1.step6()
    net.finish()


def layer(*args):
    vmem = pltpu.VMEM
    ins = ("h", "q", "k", "v", "o", "g", "u", "d", *GAINS, "lens", "og")
    outs = {
        "mixed": ((T, D), BF),
        "igrad": ((T, D), F32),
        "out_x1": ((2, 8, WX1), F32),
        "out_z1": ((2, 8, WZ1), F32),
        "out_o": ((2, 8, WO), F32),
        "out_x2": ((2, 8, WX2), F32),
        "out_z2": ((2, 8, WZ2), F32),
        "out_d": ((16, WD), F32),
    }
    scratch = {}
    for name, w in (("x1", WX1), ("z1", WZ1), ("x2", WX2), ("z2", WZ2)):
        scratch |= {
            "own_" + name: ((2, 16, w), F32),
            "es_" + name: ((16, w), BF),
            "ed_" + name: ((16, w), BF),
            "s1_" + name: ((4, 16, w), BF),
            "s2_" + name: ((4, 48, w), BF),
            "b3_" + name: ((160, w), BF),
            "w_" + name: ((2, D, w), BF),
            "b_" + name: ((4, 160, w), BF),
            "f_" + name: ((2, 80, w), BF),
            "n_" + name: ((2, 160, w), BF),
            "r2_" + name: ((3, 48, w), BF),
            "r1_" + name: ((3, 16, w), BF),
            "swap_" + name: ((8, w), F32),
            "got_" + name: ((8, w), F32),
        }
    for name, w in (("o", WO), ("d", WD)):
        scratch |= {
            "b_" + name: ((4, 16, 16, w), BF),
            "f_" + name: ((2, 8, 16, w), BF),
            "n_" + name: ((2, 16, 16, w), BF),
            "t2_" + name: ((16, 16, w), BF),
            "r2_" + name: ((3, 4, 16, w), BF),
            "t1_" + name: ((4, 16, w), BF),
            "r1_" + name: ((3, 16, w), BF),
        }
    scratch |= {
        "g_x1": ((2, D, WX1), BF),
        "g_z1": ((2, D, WZ1), BF),
        "total_z2": ((160, WZ2), F32),
        "total_z1": ((160, WZ1), F32),
        "own_o": ((2, 16, WO), F32),
        "es_o": ((16, WO), BF),
        "ed_o": ((16, WO), BF),
        "s1_o": ((16, WO), BF),
        "swap_o": ((8, WO), F32),
        "got_o": ((8, WO), F32),
        "w_o": ((2, 4, 16, 16, WO), BF),
        "w_d": ((16, 4, 2, 16, WD), BF),
        "tmp": ((160, 1024), F32),
        "gain_rows": ((16, 128), F32),
        "turn": ((D, D), BF),
        "pick": ((D, HD), BF),
        "cosine": ((SPAN, 128), F32),
        "sine": ((SPAN, 128), F32),
        "rows_in": ((2, T, D), BF),
        "rows_side": ((T, D), BF),
        "bias": ((T, SPAN), F32),
        "mults": ((8, D), F32),
        "gain_sums": ((128, D), F32),
        "in_unit": ((T, D), F32),
        "normed": ((T, D), BF),
        "normed_t": ((T, D), BF),
        "k_unit": ((T, HD), F32),
        "keys": ((SPAN, HD), BF),
        "values": ((SPAN, HD), BF),
        "queries": ((HEADS, T, HD), BF),
        "q_unit": ((HEADS, T, HD), F32),
        "q_inv": ((HEADS, T, 1), F32),
        "probs": ((HEADS, T, SPAN), F32),
        "attended": ((HEADS, T, HD), BF),
        "mix_unit": ((T, D), F32),
        "mid_unit": ((T, D), F32),
        "middle": ((T, D), F32),
        "mid": ((T, D), BF),
        "mid_t": ((T, D), BF),
        "units": ((4, T, 512), BF),
        "active": ((4, T, 512), F32),
        "slope_up": ((4, T, 512), F32),
        "acc": ((T, D), F32),
        "acc_t": ((T, D), F32),
        "g_ffn": ((T, D), BF),
        "g_att": ((HEADS, T, HD), BF),
        "g_q": ((HEADS, T, HD), BF),
        "d_keys": ((SPAN, HD), F32),
        "d_values": ((SPAN, HD), F32),
        "low": ((2, 2 * T, HD), BF),
        "side": ((2, T, HD), BF),
        "onward": ((2, T, HD), BF),
        "back": ((2, T, HD), BF),
        "q_gain": ((1, HD), F32),
    }
    inside = pl.BlockSpec(memory_space=vmem)
    names = (*ins, *outs, *scratch, "send_sems", "recv_sems")
    return pl.pallas_call(
        lambda *refs: layer_kernel(names, *refs),
        out_shape=[jax.ShapeDtypeStruct(*s) for s in outs.values()],
        in_specs=[inside] * len(ins),
        out_specs=[inside] * len(outs),
        scratch_shapes=[vmem(*s) for s in scratch.values()] + [pltpu.SemaphoreType.DMA((SEMS,))] * 2,
        compiler_params=pltpu.CompilerParams(
            collective_id=0, has_side_effects=True, vmem_limit_bytes=VMEM_CAP
        ),
        name="decoder_layer",
    )(*args)


def deliver_kernel(mixed, igrad, x1, z1, o, x2, z2, d, *outs):
    *outs, sems = outs
    large = [pltpu.make_async_copy(a, b, sems.at[i]) for i, (a, b) in enumerate(((mixed, outs[0]), (igrad, outs[1])))]
    for copy in large:
        copy.start()
    outs[2][:, 0:512] = x1[0, 0:5]
    outs[2][:, 512:1024] = x1[1, 0:5]
    outs[3][...] = z1[0, 0:5, 0:256]
    outs[4][...] = z1[1, 0:5, 0:256]
    outs[5][:, 0:384] = o[0]
    outs[5][:, 384:640] = o[1, :, 0:256]
    for i in range(2):
        outs[6 + i][:, 0:1024] = x2[i, 0:5]
        outs[6 + i][:, 1024:2048] = z2[i, 0:5]
    outs[8][...] = d[...]
    gains = z1[0, :, 256:384].T
    for at, row, n in ((9, 0, 5), (10, 4, 2), (11, 5, 2), (12, 1, 5), (13, 2, 5), (14, 3, 5)):
        outs[at][...] = gains[row : row + 1, 0:n].reshape(n)
    for copy in large:
        copy.wait()


def deliver(*parts):
    inside = pl.BlockSpec(memory_space=pltpu.VMEM)
    anywhere = pl.BlockSpec(memory_space=pl.ANY)
    shapes = [(T, D), (5, 1024), (5, 256), (5, 256), (8, D), (5, 2048), (5, 2048), (16, D)]
    shapes += [(5,), (2,), (2,), (5,), (5,), (5,)]
    return pl.pallas_call(
        deliver_kernel,
        out_shape=[jax.ShapeDtypeStruct((T, D), BF)] + [jax.ShapeDtypeStruct(s, F32) for s in shapes],
        in_specs=[anywhere] * 2 + [inside] * (len(parts) - 2),
        out_specs=[anywhere] * 2 + [inside] * 13,
        scratch_shapes=[pltpu.SemaphoreType.DMA((2,))],
        name="deliver",
    )(*parts)


def per_device(
    hidden_in,
    query_weight,
    key_weight,
    value_weight,
    output_weight,
    gate_weight,
    up_weight,
    down_weight,
    input_gain,
    query_gain,
    key_gain,
    mixer_gain,
    middle_gain,
    output_gain,
    seq_lengths,
    out_grad,
):
    gains = (input_gain, mixer_gain, middle_gain, output_gain, query_gain, key_gain)
    parts = layer(
        hidden_in,
        query_weight,
        key_weight,
        value_weight,
        output_weight,
        gate_weight,
        up_weight,
        down_weight,
        *[a.reshape(1, -1) for a in gains],
        seq_lengths.reshape(1, 64),
        out_grad,
    )
    return tuple(deliver(*parts))


def solution(mesh):
    return jax.shard_map(
        per_device,
        mesh=mesh,
        in_specs=(
            P("dp", None),
            P("dp", None),
            P("dp", None),
            P("dp", None),
            P("dp", None),
            P("dp", None),
            P("dp", None),
            P("dp", None),
            P("dp"),
            P("dp"),
            P("dp"),
            P("dp"),
            P("dp"),
            P("dp"),
            P(),
            P("dp", None),
        ),
        out_specs=(
            P("dp", None),
            P("dp", None),
            P("dp", None),
            P("dp", None),
            P("dp", None),
            P("dp", None),
            P("dp", None),
            P("dp", None),
            P("dp", None),
            P("dp"),
            P("dp"),
            P("dp"),
            P("dp"),
            P("dp"),
            P("dp"),
        ),
        check_vma=False,
    )
```

```python
import math

import jax
import jax.numpy as jnp
from jax import lax
from jax.experimental import pallas as pl
from jax.experimental.pallas import tpu as pltpu
from jax.sharding import PartitionSpec as P

MESH = pl.DeviceIdType.MESH
BF = jnp.bfloat16
F32 = jnp.float32
T = 256
D = 640
HD = 256
HEADS = 4
SPAN = 3 * T
WINDOW = 512
EPSILON = 1e-06
ROPE_BASE = 10000.0
NEG_FILL = -1e30
SCALE = 1.0 / math.sqrt(HD)
GELU_A = math.sqrt(2.0 / math.pi)
GELU_B = 0.044715
WX1, WZ1, WX2, WZ2, WD, WO = 512, 384, 1024, 1024, 640, 384
SEMS = 232
GAINS = ("n_in", "n_mix", "n_mid", "n_out", "n_q", "n_k")
VMEM_CAP = 62 << 20


def place(x, z, y, c):
    return ((x % 4) * 4 + (z % 4)) * 8 + (y % 4) * 2 + c


class Links:
    def __init__(self, send_sems, recv_sems):
        self.me = lax.axis_index("dp")
        self.at = {"x": self.me // 32, "z": (self.me // 8) % 4, "y": (self.me // 2) % 4}
        self.core = self.me % 2
        self.other = 1 - self.core
        self.sib = place(self.at["x"], self.at["z"], self.at["y"], self.other)
        self.xz = self.at["x"] * 4 + self.at["z"]
        self.send_sems, self.recv_sems, self.used, self.open = send_sems, recv_sems, 0, []

    def peer(self, axis, steps):
        moved = dict(self.at)
        moved[axis] = moved[axis] + steps
        return place(moved["x"], moved["z"], moved["y"], self.core)

    def along(self, steps):
        return (self.me + 128 + steps) % 128

    def slot(self, axis, steps):
        return (self.at[axis] + steps) % 4

    def greet(self):
        sem = pltpu.get_barrier_semaphore()
        partners = [self.sib] + [self.along(s) for s in (2, -2)]
        for axis in ("x", "z", "y"):
            partners += [self.peer(axis, o) for o in (1, 2, 3)]
        for p in partners:
            pl.semaphore_signal(sem, inc=1, device_id=(p,), device_id_type=MESH)
        self.greeted = len(partners)

    def meet(self):
        pl.semaphore_wait(pltpu.get_barrier_semaphore(), self.greeted)

    def send(self, src, dst, target):
        i = self.used
        self.used += 1
        copy = pltpu.make_async_remote_copy(
            src_ref=src,
            dst_ref=dst,
            send_sem=self.send_sems.at[i],
            recv_sem=self.recv_sems.at[i],
            device_id=(target,),
            device_id_type=MESH,
        )
        copy.start()
        self.open.append(copy.wait_send)
        return copy

    def local(self, src, dst):
        i = self.used
        self.used += 1
        copy = pltpu.make_async_copy(src, dst, self.send_sems.at[i])
        copy.start()
        return copy

    def finish(self):
        for wait in self.open:
            wait()
        self.open = []


class Rows:
    def __init__(self, net, axes, width, refs):
        self.net, self.axes, self.width = net, axes, width
        self.own, self.e_src, self.e_dst, self.s1, self.s2, self.b3, self.w, self.tmp = refs
        self.ends = []

    def view(self, slot, at, n):
        rows = pl.ds(pl.multiple_of(slot * 160 + at * 16, 16), n * 16)
        return self.w.at[self.net.core, rows]

    def step0(self):
        self.e_src[...] = self.own[self.net.other].astype(BF)

    def step0b(self):
        self.swap = self.net.send(self.e_src, self.e_dst, self.net.sib)

    def step1(self):
        net, wide = self.net, slice(0, self.width)
        self.swap.wait_recv()
        mine = self.own[net.core][0:5]
        theirs = self.e_dst[...].astype(F32)[0:5]
        first = net.core == 0
        self.tmp[0:5, wide] = jnp.where(first, mine, theirs)
        self.tmp[5:10, wide] = jnp.where(first, theirs, mine)
        slot = self.s1.at[net.at[self.axes[0]]]
        slot[...] = self.tmp[0:16, wide].astype(BF)
        self.p = [net.send(slot, slot, net.peer(self.axes[0], o)) for o in (1, 2, 3)]

    def step2(self):
        net, wide = self.net, slice(0, self.width)
        for copy in self.p:
            copy.wait_recv()
        for j in range(4):
            self.tmp[10 * j : 10 * j + 10, wide] = self.s1[j].astype(F32)[0:10]
        slot = self.s2.at[net.at[self.axes[1]]]
        slot[...] = self.tmp[0:48, wide].astype(BF)
        self.p = [net.send(slot, slot, net.peer(self.axes[1], o)) for o in (1, 2, 3)]

    def step3(self):
        net, wide = self.net, slice(0, self.width)
        for copy in self.p:
            copy.wait_recv()
        for j in range(4):
            self.tmp[40 * j : 40 * j + 40, wide] = self.s2[j].astype(F32)[0:40]
        self.b3[...] = self.tmp[0:160, wide].astype(BF)
        axis = self.axes[2]
        dst = self.view(net.at[axis], 0, 10)
        self.up = net.send(self.b3, dst, net.peer(axis, 1))
        self.down = net.send(self.b3, dst, net.peer(axis, 3))
        self.ends.append(net.send(self.b3, dst, net.sib).wait_recv)
        self.ends.append(net.local(self.b3, dst).wait)

    blocks = 10

    def step4(self):
        net, axis, n = self.net, self.axes[2], self.blocks
        half = n // 2
        self.up.wait_recv()
        part = self.view(net.slot(axis, 3), 0, half)
        self.far_up = net.send(part, part, net.peer(axis, 1))
        self.down.wait_recv()
        part = self.view(net.slot(axis, 1), half, half)
        self.far_down = net.send(part, part, net.peer(axis, 3))
        for steps in (3, 1):
            whole = self.view(net.slot(axis, steps), 0, n)
            self.ends.append(net.send(whole, whole, net.sib).wait_recv)

    def step5(self):
        net, axis, half = self.net, self.axes[2], self.blocks // 2
        for copy, at in ((self.far_up, 0), (self.far_down, half)):
            copy.wait_recv()
            part = self.view(net.slot(axis, 2), at, half)
            self.ends.append(net.send(part, part, net.sib).wait_recv)

    def step6(self):
        for wait in self.ends:
            wait()


class Tiles(Rows):
    blocks = 16

    def __init__(self, net, axes, w, by_core):
        self.net, self.axes, self.w, self.by_core = net, axes, w, by_core
        self.ends = []

    def view(self, slot, at, n):
        if self.by_core:
            return self.w.at[pl.ds(at, n), slot, self.net.core]
        return self.w.at[self.net.core, slot, pl.ds(at, n)]

    def first(self, src):
        net = self.net
        a, b, c = (net.at[axis] for axis in self.axes)
        dst = self.w.at[b * 4 + a, c, net.core] if self.by_core else self.w.at[net.core, c, b * 4 + a]
        self.p = [net.send(src, dst, net.peer(self.axes[0], o)) for o in (1, 2, 3)]
        self.kept = net.local(src, dst)

    def step2(self):
        net = self.net
        for copy in self.p:
            copy.wait_recv()
        self.kept.wait()
        part = self.view(net.at[self.axes[2]], net.at[self.axes[1]] * 4, 4)
        self.p = [net.send(part, part, net.peer(self.axes[1], o)) for o in (1, 2, 3)]

    def step3(self):
        net, axis = self.net, self.axes[2]
        for copy in self.p:
            copy.wait_recv()
        part = self.view(net.at[axis], 0, 16)
        self.up = net.send(part, part, net.peer(axis, 1))
        self.down = net.send(part, part, net.peer(axis, 3))
        self.ends.append(net.send(part, part, net.sib).wait_recv)


class RowSums:
    blocks = 10

    def __init__(self, net, axes, width, refs):
        self.net, self.axes, self.width = net, axes, width
        (self.g, self.b, self.f, self.n, self.t2, self.r2, self.t1, self.r1, self.total) = refs[:9]
        self.rest = refs[9:]
        self.swaps, self.onward, self.near = {}, {}, {}

    def view(self, steps, at, n, which):
        slot = self.net.slot(self.axes[2], steps)
        rows = pl.ds(pl.multiple_of(slot * 160 + at * 16, 16), n * 16)
        return self.g.at[which, rows]

    def rows(self, at, n):
        return pl.ds(at * 16, n * 16)

    def tile(self, steps, i):
        slot = self.net.slot(self.axes[2], steps)
        return (self.net.core, pl.ds(pl.multiple_of(slot * 160 + i * 16, 16), 16))

    def block(self, i):
        return pl.ds(pl.multiple_of(i * 16, 16), 16)

    def give(self, steps):
        src = self.view(steps, 0, self.blocks, self.net.other)
        self.swaps[steps] = self.net.send(src, self.b.at[steps], self.net.sib)

    def add(self, steps, held, at, count):
        def body(i, carry):
            where = self.tile(steps, i + at)
            self.g[where] = self.g[where] + held[self.block(i)]
            return carry

        lax.fori_loop(0, count, body, 0)

    def take(self, steps):
        net, axis, n, core = self.net, self.axes[2], self.blocks, self.net.core
        half = n // 2
        self.swaps[steps].wait_recv()
        if steps == 0:
            return
        self.add(steps, self.b.at[steps], 0, n)
        if steps == 2:
            self.onward[1] = net.send(self.view(2, 0, half, core), self.f.at[0], net.peer(axis, 1))
            self.onward[3] = net.send(self.view(2, half, half, core), self.f.at[1], net.peer(axis, 3))
        elif steps == 1:
            self.near["a"] = net.send(
                self.view(1, half, half, core), self.n.at[0, self.rows(half, half)], net.peer(axis, 1)
            )
        else:
            self.near["b"] = net.send(
                self.view(3, 0, half, core), self.n.at[1, self.rows(0, half)], net.peer(axis, 3)
            )

    def step2(self):
        net, axis, core = self.net, self.axes[2], self.net.core
        half = self.blocks // 2
        self.onward[1].wait_recv()
        self.add(1, self.f.at[0], 0, half)
        self.near["c"] = net.send(self.view(1, 0, half, core), self.n.at[0, self.rows(0, half)], net.peer(axis, 1))
        self.onward[3].wait_recv()
        self.add(3, self.f.at[1], half, half)
        self.near["d"] = net.send(
            self.view(3, half, half, core), self.n.at[1, self.rows(half, half)], net.peer(axis, 3)
        )

    def total3(self, i):
        at = self.block(i)
        own = self.g[self.tile(0, i)].astype(F32) + self.b[0, at].astype(F32)
        return own + self.n[0, at].astype(F32) + self.n[1, at].astype(F32)

    def step3(self):
        net, width, axis = self.net, self.width, self.axes[1]
        for part in "abcd":
            self.near[part].wait_recv()

        def body(i, carry):
            self.total[self.block(i), 0 : self.width] = self.total3(i)
            return carry

        lax.fori_loop(0, 10, body, 0)
        for j in range(4):
            part = self.total[40 * j : 40 * j + 40, 0:width]
            self.t2[j] = jnp.concatenate([part, jnp.zeros((8, width), F32)], axis=0).astype(BF)
        self.p = [net.send(self.t2.at[net.slot(axis, o)], self.r2.at[o - 1], net.peer(axis, o)) for o in (1, 2, 3)]

    def step4(self):
        net, width, axis = self.net, self.width, self.axes[0]
        for copy in self.p:
            copy.wait_recv()
        own = self.t2[net.at[self.axes[1]]].astype(F32)
        for o in range(3):
            own = own + self.r2[o].astype(F32)
        self.total[0:48, 0:width] = own
        for j in range(4):
            part = self.total[10 * j : 10 * j + 10, 0:width]
            self.t1[j] = jnp.concatenate([part, jnp.zeros((6, width), F32)], axis=0).astype(BF)
        self.p = [net.send(self.t1.at[net.slot(axis, o)], self.r1.at[o - 1], net.peer(axis, o)) for o in (1, 2, 3)]

    def step5(self):
        net = self.net
        swap, got, out = self.rest
        for copy in self.p:
            copy.wait_recv()
        own = self.t1[net.at[self.axes[0]]].astype(F32)
        for o in range(3):
            own = own + self.r1[o].astype(F32)
        self.total[0:16, 0 : self.width] = own
        low_rows = self.total[0:8, 0 : self.width]
        high_rows = self.total[5:13, 0 : self.width]
        first = net.core == 0
        swap[...] = jnp.where(first, high_rows, low_rows)
        out[net.core] = jnp.where(first, low_rows, high_rows)
        self.last = net.send(swap, got, net.sib)

    def step6(self):
        swap, got, out = self.rest
        self.last.wait_recv()
        out[self.net.other] = got[...]


class TileSums(RowSums):
    blocks = 16

    def __init__(self, net, axes, width, by_core, refs):
        self.by_core = by_core
        super().__init__(net, axes, width, refs)

    def view(self, steps, at, n, which):
        slot = self.net.slot(self.axes[2], steps)
        if self.by_core:
            return self.g.at[pl.ds(at, n), slot, which]
        return self.g.at[which, slot, pl.ds(at, n)]

    def rows(self, at, n):
        return pl.ds(at, n)

    def tile(self, steps, i):
        slot = self.net.slot(self.axes[2], steps)
        return (i, slot, self.net.core) if self.by_core else (self.net.core, slot, i)

    def block(self, i):
        return i

    def step3(self):
        net = self.net
        for part in "abcd":
            self.near[part].wait_recv()

        def body(i, carry):
            self.t2[i] = self.total3(i).astype(BF)
            return carry

        lax.fori_loop(0, 16, body, 0)
        self.p = [
            net.send(
                self.t2.at[pl.ds(net.slot(self.axes[1], o) * 4, 4)], self.r2.at[o - 1], net.peer(self.axes[1], o)
            )
            for o in (1, 2, 3)
        ]

    def step4(self):
        net = self.net
        for copy in self.p:
            copy.wait_recv()
        for j in range(4):
            value = self.t2[net.at[self.axes[1]] * 4 + j].astype(F32)
            for o in range(3):
                value = value + self.r2[o, j].astype(F32)
            self.t1[j] = value.astype(BF)
        axis = self.axes[0]
        self.p = [net.send(self.t1.at[net.slot(axis, o)], self.r1.at[o - 1], net.peer(axis, o)) for o in (1, 2, 3)]

    def step5(self):
        net = self.net
        for copy in self.p:
            copy.wait_recv()
        own = self.t1[net.at[self.axes[0]]].astype(F32)
        for o in range(3):
            own = own + self.r1[o].astype(F32)
        if self.by_core:
            self.rest[0][...] = own
            return
        swap, got, out = self.rest
        first = net.core == 0
        swap[...] = jnp.where(first, own[8:16], own[0:8])
        out[net.core] = jnp.where(first, own[0:8], own[8:16])
        self.last = net.send(swap, got, net.sib)

    def step6(self):
        if not self.by_core:
            super().step6()


def mm(left, right):
    return jnp.dot(left, right, preferred_element_type=F32)


def mm_t(left, right):
    return lax.dot_general(left, right, (((1,), (1,)), ((), ())), preferred_element_type=F32)


def t_mm(left, right):
    return lax.dot_general(left, right, (((0,), (0,)), ((), ())), preferred_element_type=F32)


def inv_of(values):
    return lax.rsqrt(jnp.mean(values * values, axis=-1, keepdims=True) + EPSILON)


def norm_back(upstream, unit_rows, inv_rms):
    return inv_rms * (upstream - unit_rows * jnp.mean(unit_rows * upstream, axis=-1, keepdims=True))


def spin(values, cosine, sine):
    a, b = values[:, :128], values[:, 128:]
    return jnp.concatenate([a * cosine - b * sine, b * cosine + a * sine], axis=1)


def spin_back(values, cosine, sine):
    a, b = values[:, :128], values[:, 128:]
    return jnp.concatenate([a * cosine + b * sine, b * cosine - a * sine], axis=1)


def count(shape, dim):
    return lax.broadcasted_iota(jnp.int32, shape, dim)


def hot(condition):
    return jnp.where(condition, 1.0, 0.0).astype(BF)


def split_dot(value, fixed):
    high = value.astype(BF)
    low = (value - high.astype(F32)).astype(BF)
    return mm_t(high, fixed) + mm_t(low, fixed)


class Refs:
    pass


def gather_setup(net, r):
    for ref in (r.own_x1, r.own_z1, r.own_x2, r.own_z2, r.own_o):
        ref[...] = jnp.zeros_like(ref)
    q = r.q[...].astype(F32)
    r.own_x1[0, 0:5] = q[:, 0:512]
    r.own_x1[1, 0:5] = q[:, 512:1024]
    r.gain_rows[...] = jnp.zeros_like(r.gain_rows)
    for i, gain in enumerate((r.n_in, r.n_mix, r.n_mid, r.n_out, r.n_q, r.n_k)):
        r.gain_rows[i : i + 1, 0 : gain.shape[1]] = gain[...].astype(F32)
    tile = t_mm(r.gain_rows[...].astype(BF), hot(count((16, 128), 0) == count((16, 128), 1)))
    r.own_z1[0, 0:5, 256:384] = tile[0:5]
    r.own_z1[0, 0:5, 0:256] = r.k[...].astype(F32)
    r.own_z1[1, 0:5, 0:256] = r.v[...].astype(F32)
    g, u = r.g[...].astype(F32), r.u[...].astype(F32)
    r.own_x2[0, 0:5] = g[:, 0:1024]
    r.own_x2[1, 0:5] = u[:, 0:1024]
    r.own_z2[0, 0:5] = g[:, 1024:2048]
    r.own_z2[1, 0:5] = u[:, 1024:2048]
    o = r.o[...].astype(F32)
    r.own_o[0, 0:8] = o[:, 0:384]
    r.own_o[1, 0:8, 0:256] = o[:, 384:640]

    def rows(name, axes, width):
        names = ("own_", "es_", "ed_", "s1_", "s2_", "b3_", "w_")
        return Rows(net, axes, width, [getattr(r, n + name) for n in names] + [r.tmp])

    x1 = rows("x1", ("y", "z", "x"), WX1)
    z1 = rows("z1", ("x", "y", "z"), WZ1)
    x2 = rows("x2", ("y", "z", "x"), WX2)
    z2 = rows("z2", ("x", "y", "z"), WZ2)
    for s in (x1, z1, x2, z2):
        s.step0()
    r.es_o[...] = r.own_o[net.other].astype(BF)
    return x1, z1, x2, z2, Tiles(net, ("y", "x", "z"), r.w_o, False), Tiles(net, ("z", "x", "y"), r.w_d, True)


def layer_kernel(names, *refs):
    r = Refs()
    for name, ref in zip(names, refs):
        setattr(r, name, ref)
    r.g_x2, r.g_z2, r.g_d, r.g_o = r.w_x2, r.w_z2, r.w_d, r.w_o
    for name in ("x1", "z1", "x2", "z2"):
        setattr(r, "t2_" + name, getattr(r, "s2_" + name))
        setattr(r, "t1_" + name, getattr(r, "s1_" + name))
    r.total_x2 = r.total_x1 = r.total_o = r.total_d = r.tmp
    r.g_middle = r.igrad
    net = Links(r.send_sems, r.recv_sems)
    net.greet()
    x1, z1, x2, z2, ow, dw = gather_setup(net, r)
    r.rows_in[0] = r.h[...]
    net.meet()
    x1.step0b()
    z1.step0b()
    swap_o = net.send(r.es_o, r.ed_o, net.sib)
    x2.step0b()
    z2.step0b()
    x1.step1()
    z1.step1()
    swap_o.wait_recv()
    mine, theirs = r.own_o[net.core][0:8], r.ed_o[...].astype(F32)[0:8]
    r.tmp[0:8, 0:WO] = jnp.where(net.core == 0, mine, theirs)
    r.tmp[8:16, 0:WO] = jnp.where(net.core == 0, theirs, mine)
    r.s1_o[...] = r.tmp[0:16, 0:WO].astype(BF)
    ow.first(r.s1_o)
    x2.step1()
    z2.step1()
    dw.first(r.d)

    k_dim, j_dim = count((D, D), 0), count((D, D), 1)
    tens = (j_dim * 52429) >> 19
    source = (tens & 3) * 160 + (tens >> 4) * 40 + ((tens >> 2) & 3) * 10 + (j_dim - 10 * tens)
    r.turn[...] = hot(k_dim == source)
    spot = count((64, 64), 0)
    lens = jnp.broadcast_to(r.lens[...].astype(F32), (64, 64))
    column = jnp.sum(jnp.where(spot == count((64, 64), 1), lens, 0.0), axis=1, keepdims=True)
    ends = jnp.sum(jnp.where(spot <= count((64, 64), 1), column, 0.0), axis=0, keepdims=True)
    offset = net.me * T
    token = (count((SPAN, 64), 0) + (offset - 2 * T)).astype(F32)
    start = jnp.max(jnp.where(ends <= token, ends, 0.0), axis=1, keepdims=True)
    position = token[:, 0:1] - start
    pair = count((1, 128), 1).astype(F32)
    angle = position * jnp.exp(pair * (-2.0 * math.log(ROPE_BASE) / HD))
    r.cosine[...] = jnp.cos(angle)
    r.sine[...] = jnp.sin(angle)
    ahead = count((T, SPAN), 1) - 2 * T
    distance = count((T, SPAN), 0) - ahead
    inside = (distance >= 0) & (distance < WINDOW) & ((ahead + offset).astype(F32) >= start[2 * T :])
    r.bias[...] = jnp.where(inside, 0.0, NEG_FILL)
    hidden = r.h[...].astype(F32)
    input_inv = inv_of(hidden)
    r.in_unit[...] = hidden * input_inv

    early, late = (x1, z1, ow), (x2, z2, dw)
    for s in early:
        s.step2()
    for s in late:
        s.step2()
    ahead_copy = net.send(r.rows_in.at[0], r.rows_in.at[1], net.along(2))
    for s in (*early, *late):
        s.step3()
    ahead_copy.wait_recv()
    side_copy = net.send(r.rows_in.at[net.core], r.rows_side, net.sib)
    for s in (*early, *late):
        s.step4()
    for s in early:
        s.step5()
    x1.step6()
    z1.step6()

    gain_rows = lax.dot_general(
        r.w_z1[0, :, 256:384], r.turn[...], (((0,), (1,)), ((), ())), preferred_element_type=F32
    )
    far, near = count((D, HD), 0), count((D, HD), 1)
    r.pick[...] = hot(far == 5 * (near >> 1) + (near & 1))
    head_rows = mm(gain_rows.astype(BF), r.pick[...])
    r.mults[0:4] = 1.0 + gain_rows[0:4]
    r.mults[4:6, 0:HD] = 1.0 + head_rows[4:6]
    normed = (r.in_unit[...] * r.mults[0:1]).astype(BF)
    r.normed[...] = normed
    turned = mm(normed, r.turn[...]).astype(BF)
    r.normed_t[...] = turned
    cosine, sine = r.cosine[2 * T :], r.sine[2 * T :]
    for h in range(HEADS):
        raw = mm(normed, r.w_x1[h // 2, :, 256 * (h % 2) : 256 * (h % 2) + 256])
        inv = inv_of(raw)
        r.q_inv[h] = inv
        r.q_unit[h] = raw * inv
        r.queries[h] = spin(raw * inv * r.mults[4:5, 0:HD], cosine, sine).astype(BF)
    side_copy.wait_recv()
    for i in range(3):
        some = slice(T * i, T * i + T)
        if i < 2:
            rows = (r.rows_in[1] if i == 0 else r.rows_side[...]).astype(F32)
            here = (rows * inv_of(rows) * r.mults[0:1]).astype(BF)
            there = mm(here, r.turn[...]).astype(BF)
        else:
            there = turned
        key_raw = mm(there, r.w_z1[0, :, 0:256])
        key_inv = inv_of(key_raw)
        key_unit = key_raw * key_inv
        r.keys[some] = spin(key_unit * r.mults[5:6, 0:HD], r.cosine[some], r.sine[some]).astype(BF)
        r.values[some] = mm(there, r.w_z1[1, :, 0:256]).astype(BF)
    r.k_unit[...] = key_unit
    for s in late:
        s.step5()

    def attend(h):
        scores = mm_t(r.queries[h], r.keys[...]) * SCALE + r.bias[...]
        row_max = jnp.max(scores, axis=1, keepdims=True)
        weights = jnp.exp(scores - row_max)
        probs = weights / jnp.sum(weights, axis=1, keepdims=True)
        r.probs[h] = probs
        r.attended[h] = mm(probs.astype(BF), r.values[...]).astype(BF)

    for h in range(HEADS):
        attend(h)

    ow.step6()
    left = jnp.zeros((T, 384), F32)
    right = jnp.zeros((T, 256), F32)
    for h in range(HEADS):
        some = slice(4 * h, 4 * h + 4)
        left = left + mm(r.attended[h], r.w_o[0, :, some].reshape(256, WO))
        right = right + mm(r.attended[h], r.w_o[1, :, some].reshape(256, WO)[:, 0:256])
    mixer_out = jnp.concatenate([left, right], axis=1)
    mixer_inv = inv_of(mixer_out)
    r.mix_unit[...] = mixer_out * mixer_inv
    middle = r.h[...].astype(F32) + r.mix_unit[...] * r.mults[1:2]
    middle_inv = inv_of(middle)
    r.mid_unit[...] = middle * middle_inv
    r.middle[...] = middle
    r.mid[...] = (r.mid_unit[...] * r.mults[2:3]).astype(BF)
    r.mid_t[...] = mm(r.mid[...], r.turn[...]).astype(BF)
    for s in late:
        s.step6()

    r.acc[...] = jnp.zeros_like(r.acc)
    for w, rows_in, first in ((r.w_x2, r.mid, 0), (r.w_z2, r.mid_t, 2)):

        def forward(j, carry, w=w, rows_in=rows_in, first=first):
            cols = slice(512 * j, 512 * j + 512)
            gate = mm(rows_in[...], w[0, :, cols])
            up = mm(rows_in[...], w[1, :, cols])
            square = gate * gate
            tanh = jnp.tanh(GELU_A * gate * (1.0 + GELU_B * square))
            active = 0.5 * gate * (1.0 + tanh)
            slope = 0.5 * (1.0 + tanh) + 0.5 * gate * (1.0 - tanh * tanh) * (
                GELU_A * (1.0 + 3.0 * GELU_B * square)
            )
            units = (active * up).astype(BF)
            part = first + j
            r.units[part] = units
            r.active[part] = active
            r.slope_up[part] = slope * up
            r.acc[...] += mm(units, r.w_d[4 * part : 4 * part + 4].reshape(512, D))
            return carry

        for j in range(2):
            forward(j, 0)
    ffn_out = r.acc[...]
    ffn_inv = inv_of(ffn_out)
    ffn_unit = ffn_out * ffn_inv
    r.mixed[...] = (r.middle[...] + ffn_unit * r.mults[3:4]).astype(BF)
    grad_out = r.og[...].astype(F32)
    r.gain_sums[...] = jnp.zeros_like(r.gain_sums)
    r.gain_sums[3:4] = jnp.sum(grad_out * ffn_unit, axis=0, keepdims=True)
    r.g_ffn[...] = norm_back(grad_out * r.mults[3:4], ffn_unit, ffn_inv).astype(BF)
    net.finish()

    def sums(kind, name, *args):
        tags = ("g_", "b_", "f_", "n_", "t2_", "r2_", "t1_", "r1_", "total_", "swap_", "got_", "out_")
        if name == "d":
            tags = tags[:9] + tags[11:]
        return kind(net, *args, [getattr(r, tag + name) for tag in tags])

    sx1 = sums(RowSums, "x1", ("y", "z", "x"), WX1)
    sz1 = sums(RowSums, "z1", ("x", "y", "z"), WZ1)
    sx2 = sums(RowSums, "x2", ("y", "z", "x"), WX2)
    sz2 = sums(RowSums, "z2", ("x", "y", "z"), WZ2)
    so = sums(TileSums, "o", ("y", "x", "z"), WO, False)
    sd = sums(TileSums, "d", ("z", "x", "y"), WD, True)
    wide = (sx2, sz2, sd)
    for w, g, rows_in, first, total in (
        (r.w_x2, r.g_x2, r.mid, 0, r.acc),
        (r.w_z2, r.g_z2, r.mid_t, 2, r.acc_t),
    ):
        total[...] = jnp.zeros_like(total)

        def backward(j, carry, w=w, g=g, rows_in=rows_in, first=first, total=total):
            cols = slice(512 * j, 512 * j + 512)
            part = first + j
            some = slice(4 * part, 4 * part + 4)
            g_ffn = r.g_ffn[...]
            grad_hidden = mm_t(g_ffn, r.w_d[some].reshape(512, D))
            r.g_d[some] = t_mm(r.units[part], g_ffn).astype(BF).reshape(4, 4, 2, 16, D)
            grad_gate = (grad_hidden * r.slope_up[part]).astype(BF)
            grad_up = (grad_hidden * r.active[part]).astype(BF)
            total[...] += mm_t(grad_gate, w[0, :, cols]) + mm_t(grad_up, w[1, :, cols])
            g[0, :, cols] = t_mm(rows_in[...], grad_gate).astype(BF)
            g[1, :, cols] = t_mm(rows_in[...], grad_up).astype(BF)
            return carry

        for j in range(2):
            backward(j, 0)
        if first == 0:
            for steps in (2, 1, 3, 0):
                sx2.give(steps)
    for steps in (2, 1, 3, 0):
        sz2.give(steps)
        sd.give(steps)

    grad_in = r.acc[...] + split_dot(r.acc_t[...], r.turn[...])
    mid_unit = r.mid_unit[...]
    r.gain_sums[2:3] = jnp.sum(grad_in * mid_unit, axis=0, keepdims=True)
    grad_middle = r.og[...].astype(F32) + norm_back(grad_in * r.mults[2:3], mid_unit, inv_of(r.middle[...]))
    r.g_middle[...] = grad_middle
    mix_unit = r.mix_unit[...]
    r.gain_sums[1:2] = jnp.sum(grad_middle * mix_unit, axis=0, keepdims=True)
    grad_mixer = norm_back(grad_middle * r.mults[1:2], mix_unit, mixer_inv).astype(BF)
    for s in wide:
        s.take(2)
    for h in range(HEADS):
        some = slice(4 * h, 4 * h + 4)
        r.g_att[h] = (
            mm_t(grad_mixer[:, 0:384], r.w_o[0, :, some].reshape(256, WO))
            + mm_t(grad_mixer[:, 384:640], r.w_o[1, :, some].reshape(256, WO)[:, 0:256])
        ).astype(BF)
        grad = t_mm(r.attended[h], grad_mixer).astype(BF)
        r.g_o[0, :, some] = grad[:, 0:384].reshape(4, 4, 16, 384)
        r.g_o[1, :, some, :, 0:256] = grad[:, 384:640].reshape(4, 4, 16, 256)
    for steps in (2, 1, 3, 0):
        so.give(steps)
    r.d_values[...] = t_mm(r.probs[0].astype(BF), r.g_att[0])
    for h in range(1, HEADS):
        r.d_values[...] += t_mm(r.probs[h].astype(BF), r.g_att[h])

    def halo_aside(i, whole, scale):
        r.low[i] = (whole[0 : 2 * T] * scale).astype(BF)
        return net.send(r.low.at[i, pl.ds(T, T)], r.side.at[i], net.sib)

    def halo_back(i, copy):
        copy.wait_recv()
        far = r.low[i, 0:T]
        r.onward[i] = jnp.where(net.core == 1, far + r.side[i], far)
        return net.send(r.onward.at[i], r.back.at[i], net.along(-2))

    def halo_sum(i, whole, scale, copy):
        copy.wait_recv()
        side = jnp.where(net.core == 0, r.side[i].astype(F32), 0.0)
        return whole[2 * T :] * scale + r.back[i].astype(F32) + side

    aside_v = halo_aside(1, r.d_values, 1.0)
    for s in wide:
        s.take(1)

    r.d_keys[...] = jnp.zeros_like(r.d_keys)
    r.q_gain[...] = jnp.zeros_like(r.q_gain)

    def attend_back(h):
        probs = r.probs[h]
        grad_probs = mm_t(r.g_att[h], r.values[...])
        delta = jnp.sum(probs * grad_probs, axis=1, keepdims=True)
        grad_scores = probs * (grad_probs - delta)
        r.probs[h] = grad_scores
        r.d_keys[...] += t_mm(grad_scores.astype(BF), r.queries[h])

    def query_back(h):
        grad_q = mm(r.probs[h].astype(BF), r.keys[...]) * SCALE
        back = spin_back(grad_q, cosine, sine)
        unit = r.q_unit[h]
        r.q_gain[...] += jnp.sum(back * unit, axis=0, keepdims=True)
        r.g_q[h] = norm_back(back * r.mults[4:5, 0:HD], unit, r.q_inv[h]).astype(BF)

    attend_back(0)
    back_v = halo_back(1, aside_v)
    for s in (sx2, sz2):
        s.take(3)
    for h in range(1, HEADS):
        attend_back(h)
    aside_k = halo_aside(0, r.d_keys, SCALE)

    normed, turned = r.normed[...], r.normed_t[...]
    query_back(0)
    back_k = halo_back(0, aside_k)
    for h in range(1, HEADS):
        query_back(h)
    for h in range(HEADS):
        r.g_x1[h // 2, :, 256 * (h % 2) : 256 * (h % 2) + 256] = t_mm(normed, r.g_q[h]).astype(BF)
    for steps in (2, 1, 3, 0):
        sx1.give(steps)
    sd.take(3)
    for steps in (2, 1, 3):
        so.take(steps)
    for s in wide:
        s.step2()
    for steps in (2, 1, 3):
        sx1.take(steps)
    own_v = halo_sum(1, r.d_values, 1.0, back_v)
    grad_v = own_v.astype(BF)
    r.g_z1[1, :, 0:256] = t_mm(turned, grad_v).astype(BF)
    r.g_z1[1, :, 256:384] = jnp.zeros((D, 128), BF)
    grad_natural = mm_t(r.g_q[0], r.w_x1[0, :, 0:256])
    for h in range(1, HEADS):
        grad_natural = grad_natural + mm_t(r.g_q[h], r.w_x1[h // 2, :, 256 * (h % 2) : 256 * (h % 2) + 256])
    r.acc[...] = grad_natural
    r.acc_t[...] = mm_t(grad_v, r.w_z1[1, :, 0:256])
    own_k = halo_sum(0, r.d_keys, SCALE, back_k)
    key_back = spin_back(own_k, cosine, sine)
    k_unit = r.k_unit[...]
    key_gain = jnp.sum(key_back * k_unit, axis=0, keepdims=True)
    grad_k = norm_back(key_back * r.mults[5:6, 0:HD], k_unit, key_inv).astype(BF)
    r.g_z1[0, :, 0:256] = t_mm(turned, grad_k).astype(BF)
    grad_turned = r.acc_t[...] + mm_t(grad_k, r.w_z1[0, :, 0:256])
    grad_normed = r.acc[...] + split_dot(grad_turned, r.turn[...])
    in_unit = r.in_unit[...]
    r.gain_sums[0:1] = jnp.sum(grad_normed * in_unit, axis=0, keepdims=True)
    both = jnp.concatenate([r.q_gain[...], key_gain, jnp.zeros((6, HD), F32)], axis=0).astype(BF)
    r.gain_sums[4:6] = mm_t(both, r.pick[...])[0:2]
    r.g_z1[0, :, 256:384] = lax.dot_general(
        r.turn[...], r.gain_sums[...].astype(BF), (((0,), (1,)), ((), ())), preferred_element_type=F32
    ).astype(BF)
    for steps in (2, 1, 3, 0):
        sz1.give(steps)
    so.step2()
    for steps in (2, 1, 3):
        sz1.take(steps)
    for s in wide:
        s.take(0)
        s.step3()
    sx1.step2()
    r.igrad[...] = r.g_middle[...] + norm_back(grad_normed * r.mults[0:1], in_unit, input_inv)
    sz1.step2()
    so.take(0)
    so.step3()
    for s in wide:
        s.step4()
    sx1.take(0)
    sx1.step3()
    sz1.take(0)
    sz1.step3()
    so.step4()
    for s in wide:
        s.step5()
    sx1.step4()
    sz1.step4()
    so.step5()
    sx1.step5()
    for s in wide:
        s.step6()
    sz1.step5()
    so.step6()
    sx1.step6()
    sz1.step6()
    net.finish()


def layer(*args):
    vmem = pltpu.VMEM
    ins = ("h", "q", "k", "v", "o", "g", "u", "d", *GAINS, "lens", "og")
    outs = {
        "mixed": ((T, D), BF),
        "igrad": ((T, D), F32),
        "out_x1": ((2, 8, WX1), F32),
        "out_z1": ((2, 8, WZ1), F32),
        "out_o": ((2, 8, WO), F32),
        "out_x2": ((2, 8, WX2), F32),
        "out_z2": ((2, 8, WZ2), F32),
        "out_d": ((16, WD), F32),
    }
    scratch = {}
    for name, w in (("x1", WX1), ("z1", WZ1), ("x2", WX2), ("z2", WZ2)):
        scratch |= {
            "own_" + name: ((2, 16, w), F32),
            "es_" + name: ((16, w), BF),
            "ed_" + name: ((16, w), BF),
            "s1_" + name: ((4, 16, w), BF),
            "s2_" + name: ((4, 48, w), BF),
            "b3_" + name: ((160, w), BF),
            "w_" + name: ((2, D, w), BF),
            "b_" + name: ((4, 160, w), BF),
            "f_" + name: ((2, 80, w), BF),
            "n_" + name: ((2, 160, w), BF),
            "r2_" + name: ((3, 48, w), BF),
            "r1_" + name: ((3, 16, w), BF),
            "swap_" + name: ((8, w), F32),
            "got_" + name: ((8, w), F32),
        }
    for name, w in (("o", WO), ("d", WD)):
        scratch |= {
            "b_" + name: ((4, 16, 16, w), BF),
            "f_" + name: ((2, 8, 16, w), BF),
            "n_" + name: ((2, 16, 16, w), BF),
            "t2_" + name: ((16, 16, w), BF),
            "r2_" + name: ((3, 4, 16, w), BF),
            "t1_" + name: ((4, 16, w), BF),
            "r1_" + name: ((3, 16, w), BF),
        }
    scratch |= {
        "g_x1": ((2, D, WX1), BF),
        "g_z1": ((2, D, WZ1), BF),
        "total_z2": ((160, WZ2), F32),
        "total_z1": ((160, WZ1), F32),
        "own_o": ((2, 16, WO), F32),
        "es_o": ((16, WO), BF),
        "ed_o": ((16, WO), BF),
        "s1_o": ((16, WO), BF),
        "swap_o": ((8, WO), F32),
        "got_o": ((8, WO), F32),
        "w_o": ((2, 4, 16, 16, WO), BF),
        "w_d": ((16, 4, 2, 16, WD), BF),
        "tmp": ((160, 1024), F32),
        "gain_rows": ((16, 128), F32),
        "turn": ((D, D), BF),
        "pick": ((D, HD), BF),
        "cosine": ((SPAN, 128), F32),
        "sine": ((SPAN, 128), F32),
        "rows_in": ((2, T, D), BF),
        "rows_side": ((T, D), BF),
        "bias": ((T, SPAN), F32),
        "mults": ((8, D), F32),
        "gain_sums": ((128, D), F32),
        "in_unit": ((T, D), F32),
        "normed": ((T, D), BF),
        "normed_t": ((T, D), BF),
        "k_unit": ((T, HD), F32),
        "keys": ((SPAN, HD), BF),
        "values": ((SPAN, HD), BF),
        "queries": ((HEADS, T, HD), BF),
        "q_unit": ((HEADS, T, HD), F32),
        "q_inv": ((HEADS, T, 1), F32),
        "probs": ((HEADS, T, SPAN), F32),
        "attended": ((HEADS, T, HD), BF),
        "mix_unit": ((T, D), F32),
        "mid_unit": ((T, D), F32),
        "middle": ((T, D), F32),
        "mid": ((T, D), BF),
        "mid_t": ((T, D), BF),
        "units": ((4, T, 512), BF),
        "active": ((4, T, 512), F32),
        "slope_up": ((4, T, 512), F32),
        "acc": ((T, D), F32),
        "acc_t": ((T, D), F32),
        "g_ffn": ((T, D), BF),
        "g_att": ((HEADS, T, HD), BF),
        "g_q": ((HEADS, T, HD), BF),
        "d_keys": ((SPAN, HD), F32),
        "d_values": ((SPAN, HD), F32),
        "low": ((2, 2 * T, HD), BF),
        "side": ((2, T, HD), BF),
        "onward": ((2, T, HD), BF),
        "back": ((2, T, HD), BF),
        "q_gain": ((1, HD), F32),
    }
    inside = pl.BlockSpec(memory_space=vmem)
    names = (*ins, *outs, *scratch, "send_sems", "recv_sems")
    return pl.pallas_call(
        lambda *refs: layer_kernel(names, *refs),
        out_shape=[jax.ShapeDtypeStruct(*s) for s in outs.values()],
        in_specs=[inside] * len(ins),
        out_specs=[inside] * len(outs),
        scratch_shapes=[vmem(*s) for s in scratch.values()] + [pltpu.SemaphoreType.DMA((SEMS,))] * 2,
        compiler_params=pltpu.CompilerParams(
            collective_id=0, has_side_effects=True, vmem_limit_bytes=VMEM_CAP
        ),
        name="decoder_layer",
    )(*args)


def deliver_kernel(mixed, igrad, x1, z1, o, x2, z2, d, *outs):
    outs[0][...] = mixed[...]
    outs[1][...] = igrad[...]
    outs[2][:, 0:512] = x1[0, 0:5]
    outs[2][:, 512:1024] = x1[1, 0:5]
    outs[3][...] = z1[0, 0:5, 0:256]
    outs[4][...] = z1[1, 0:5, 0:256]
    outs[5][:, 0:384] = o[0]
    outs[5][:, 384:640] = o[1, :, 0:256]
    for i in range(2):
        outs[6 + i][:, 0:1024] = x2[i, 0:5]
        outs[6 + i][:, 1024:2048] = z2[i, 0:5]
    outs[8][...] = d[...]
    gains = z1[0, :, 256:384].T
    for at, row, n in ((9, 0, 5), (10, 4, 2), (11, 5, 2), (12, 1, 5), (13, 2, 5), (14, 3, 5)):
        outs[at][...] = gains[row : row + 1, 0:n].reshape(n)


def deliver(*parts):
    inside = pl.BlockSpec(memory_space=pltpu.VMEM)
    shapes = [(T, D), (5, 1024), (5, 256), (5, 256), (8, D), (5, 2048), (5, 2048), (16, D)]
    shapes += [(5,), (2,), (2,), (5,), (5,), (5,)]
    return pl.pallas_call(
        deliver_kernel,
        out_shape=[jax.ShapeDtypeStruct((T, D), BF)] + [jax.ShapeDtypeStruct(s, F32) for s in shapes],
        in_specs=[inside] * len(parts),
        out_specs=[inside] * 15,
        name="deliver",
    )(*parts)


def per_device(
    hidden_in,
    query_weight,
    key_weight,
    value_weight,
    output_weight,
    gate_weight,
    up_weight,
    down_weight,
    input_gain,
    query_gain,
    key_gain,
    mixer_gain,
    middle_gain,
    output_gain,
    seq_lengths,
    out_grad,
):
    gains = (input_gain, mixer_gain, middle_gain, output_gain, query_gain, key_gain)
    parts = layer(
        hidden_in,
        query_weight,
        key_weight,
        value_weight,
        output_weight,
        gate_weight,
        up_weight,
        down_weight,
        *[a.reshape(1, -1) for a in gains],
        seq_lengths.reshape(1, 64),
        out_grad,
    )
    return tuple(deliver(*parts))


def solution(mesh):
    return jax.shard_map(
        per_device,
        mesh=mesh,
        in_specs=(
            P("dp", None),
            P("dp", None),
            P("dp", None),
            P("dp", None),
            P("dp", None),
            P("dp", None),
            P("dp", None),
            P("dp", None),
            P("dp"),
            P("dp"),
            P("dp"),
            P("dp"),
            P("dp"),
            P("dp"),
            P(),
            P("dp", None),
        ),
        out_specs=(
            P("dp", None),
            P("dp", None),
            P("dp", None),
            P("dp", None),
            P("dp", None),
            P("dp", None),
            P("dp", None),
            P("dp", None),
            P("dp", None),
            P("dp"),
            P("dp"),
            P("dp"),
            P("dp"),
            P("dp"),
            P("dp"),
        ),
        check_vma=False,
    )
```
